128 devices in a mesh: ex: 4 (over x), tp: 4 (over z), ps: 8 (over y, core).
Axes of the slice: x: 4, y: 4, z: 4, core: 2. Of those that a mesh axis runs over, the one named last changes fastest.
Arguments:
- tokens: bfloat16 [4096, 8192], P(('ex', 'ps'), 'tp'), may hold values from -6 to 6
- output_gradient: bfloat16 [4096, 29568], P(('ex', 'ps'), 'tp'), may hold values from -6 to 6
- adapter_down_factor: bfloat16 [8192, 128], P('tp'), may hold values from -0.0625 to 0.0625
- adapter_up_factor: bfloat16 [29568, 128], P('tp'), may hold values from -0.03125 to 0.03125
- first_moment_down: float32 [4, 2048, 128], P('tp', ('ex', 'ps')), may hold values from -0.012 to 0.012
- second_moment_down: float32 [4, 2048, 128], P('tp', ('ex', 'ps')), may hold values from 2e-07 to 2e-06
- first_moment_up: float32 [4, 7392, 128], P('tp', ('ex', 'ps')), may hold values from -0.012 to 0.012
- second_moment_up: float32 [4, 7392, 128], P('tp', ('ex', 'ps')), may hold values from 2e-07 to 2e-06
- down_row_seeds: int32 [4, 2048], P('tp', ('ex', 'ps')), may hold values from 0 to 15
- up_row_seeds: int32 [4, 7392], P('tp', ('ex', 'ps')), may hold values from 0 to 15
- segments: int32 [4096], replicated, may hold values from 0 to 3, never falling along the last dimension, each value on 1 to 2048 neighbouring positions
- bank: bfloat16 [16, 128, 8192], P(None, None, ('ex', 'tp', 'ps')), may hold values from -6 to 6
Outputs:
- sketch: float32 [4, 8192], P(None, ('ex', 'tp', 'ps'))
The draws below stay inside these ranges and needn't reach their ends.
Inputs may be any that keep to these rules, and one draw needn't show every extreme that they name: `segments`: never falls along the rows; every example has 1 to 2048 rows and one has exactly 2048.
All inputs are finite; a program needn't handle non-finite values.
Results may differ from the reference program's by a relative error of at most 0.0033.
Values may be sent and summed in bfloat16 or wider, within the bound.
No kernel may reach another device: no remote copies, remote signals or barrier semaphores. Data moves between devices by JAX's collectives and lax.ppermute only.
A program may use at most 64 MiB of HBM per device.

```python
import math
import jax
import jax.numpy as jnp
import numpy as np
from jax import lax

MODEL_WIDTH = 8192
HIDDEN_WIDTH = 29568
ADAPTER_RANK = 128
K = 8192
BANK = 16
EXAMPLES = 4
TOKENS = 4096
MOST = 2048
N_TP = 4


def place_ends(drawn, own_key, smallest, high):
    spot = [jax.random.randint(jax.random.fold_in(own_key, axis), (), 0, length) for axis, length in enumerate(drawn.shape)]
    widest = drawn.shape.index(max(drawn.shape))
    beside = spot[:widest] + [(spot[widest] + 1) % drawn.shape[widest]] + spot[widest + 1:]
    return drawn.at[tuple(spot)].set(smallest).at[tuple(beside)].set(high)


def steps_of(key, dims, pieces, smallest, top_value):
    factor_of = 1.0
    for axis_at, shards_of in pieces:
        heights = jax.random.uniform(jax.random.fold_in(jax.random.fold_in(key, 6), axis_at), (shards_of,), jnp.float32, smallest / len(pieces), top_value / len(pieces))
        factor_of = factor_of * jnp.repeat(jnp.exp(heights), dims[axis_at] // shards_of).reshape((-1,) + (1,) * (len(dims) - 1 - axis_at))
    return factor_of


def profile(count, total, most, lean):
    weights = [(1 << 20) // math.isqrt(standing ** lean) + 1 for standing in range(2, count + 1)]
    surplus, given = total - most - (count - 1), [1] * (count - 1)
    while surplus > 0:
        movable = [i for i in range(count - 1) if given[i] < most]
        pool, left = sum([weights[i] for i in movable]), surplus
        for i in movable:
            extra = min(most - given[i], max(1, left * weights[i] // pool), surplus)
            given[i] = given[i] + extra
            surplus = surplus - extra
    return np.array([most] + given)


def uneven_parts(stream_key, amount, total, bound, skew):
    if amount == 2:
        one = jax.random.randint(stream_key, (), max(1, total - bound), min(bound, total - 1) + 1)
        return jnp.stack([one, total - one])
    sizes = jnp.asarray(profile(amount, total, bound, skew), jnp.int32)
    couples = (amount - 1) // 2
    giver, receiver = sizes[1:1 + 2 * couples:2], sizes[2:2 + 2 * couples:2]
    margin = jnp.minimum(giver - 1, bound - receiver)
    passed = jax.random.randint(jax.random.fold_in(stream_key, 1), (couples,), 0, 1 << 20) % (margin + 1)
    sizes = sizes.at[1:1 + 2 * couples:2].set(giver - passed).at[2:2 + 2 * couples:2].set(receiver + passed)
    return sizes[jax.random.permutation(jax.random.fold_in(stream_key, 2), amount)]


def gaussian(own_key, dims, scale, reach, pieces=(), held_as=jnp.bfloat16):
    values = scale * jax.random.normal(own_key, dims, jnp.float32)
    if pieces:
        values = values * steps_of(own_key, dims, pieces, -0.22, 0.18)
    return jnp.clip(values, -reach, reach).astype(held_as)


def setup_inputs(seed: int = 0) -> dict:
    keys = jax.random.split(jax.random.key(seed), 13)
    return {
        "tokens": gaussian(keys[0], (TOKENS, MODEL_WIDTH), 1.0, 6.0, ((0, 32), (1, 4))),
        "output_gradient": gaussian(keys[1], (TOKENS, HIDDEN_WIDTH), 1.0, 6.0, ((0, 32), (1, 4))),
        "adapter_down_factor": gaussian(keys[2], (MODEL_WIDTH, ADAPTER_RANK), MODEL_WIDTH ** -0.5, 0.0625, ((0, 4),)),
        "adapter_up_factor": gaussian(keys[3], (HIDDEN_WIDTH, ADAPTER_RANK), HIDDEN_WIDTH ** -0.5, 0.03125, ((0, 4),)),
        "first_moment_down": gaussian(keys[4], (N_TP, MODEL_WIDTH // N_TP, ADAPTER_RANK), 0.002, 0.012, ((0, 4), (1, 32)), jnp.float32),
        "second_moment_down": jnp.clip(jnp.exp(math.log(1.9999999949504854e-06) - 2.3025851 * jax.random.uniform(keys[5], (N_TP, MODEL_WIDTH // N_TP, ADAPTER_RANK), jnp.float32) ** steps_of(keys[5], (N_TP, MODEL_WIDTH // N_TP, ADAPTER_RANK), ((0, 4), (1, 32)), -0.2, 0.2)), 2.0000000233721948e-07, 1.9999999949504854e-06),
        "first_moment_up": gaussian(keys[6], (N_TP, HIDDEN_WIDTH // N_TP, ADAPTER_RANK), 0.002, 0.012, ((0, 4), (1, 32)), jnp.float32),
        "second_moment_up": jnp.clip(jnp.exp(math.log(1.9999999949504854e-06) - 2.3025851 * jax.random.uniform(keys[7], (N_TP, HIDDEN_WIDTH // N_TP, ADAPTER_RANK), jnp.float32) ** steps_of(keys[7], (N_TP, HIDDEN_WIDTH // N_TP, ADAPTER_RANK), ((0, 4), (1, 32)), -0.2, 0.2)), 2.0000000233721948e-07, 1.9999999949504854e-06),
        "down_row_seeds": place_ends(jax.random.randint(keys[8], (N_TP, MODEL_WIDTH // N_TP), 0, BANK), jax.random.fold_in(keys[8], 1), 0, BANK - 1).astype(jnp.int32),
        "up_row_seeds": place_ends(jax.random.randint(keys[9], (N_TP, HIDDEN_WIDTH // N_TP), 0, BANK), jax.random.fold_in(keys[9], 1), 0, BANK - 1).astype(jnp.int32),
        "segments": jnp.searchsorted(jnp.cumsum(uneven_parts(keys[10], EXAMPLES, TOKENS, MOST, 2)), jnp.arange(TOKENS), side="right").astype(jnp.int32),
        "bank": gaussian(keys[11], (BANK, ADAPTER_RANK, K), 1.0, 6.0, ((2, 128),)),
    }


def adam_feature(grad, first, second):
    moved = 0.9 * first[None, :, :] + 0.1 * grad
    scaled = 0.999 * second[None, :, :] + 0.001 * grad * grad
    return moved / (jnp.sqrt(scaled) + 1e-08)

def reference(tokens, output_gradient, adapter_down_factor, adapter_up_factor, first_moment_down, second_moment_down, first_moment_up, second_moment_up, down_row_seeds, up_row_seeds, segments, bank):
    hidden_inner_product = jnp.dot(tokens, adapter_down_factor, preferred_element_type=jnp.float32).astype(jnp.bfloat16)
    input_inner_product = jnp.dot(output_gradient, adapter_up_factor, preferred_element_type=jnp.float32).astype(jnp.bfloat16)
    labels = jnp.arange(EXAMPLES, dtype=jnp.int32)
    counts = lax.optimization_barrier(jnp.sum((segments[None, :] == labels[:, None]).astype(jnp.int32), axis=1)).astype(jnp.int32)
    starts = (jnp.cumsum(counts) - counts).astype(jnp.int32)

    def one_example(index):
        first_row = starts[index]
        length = counts[index]
        base = jnp.minimum(first_row, TOKENS - MOST).astype(jnp.int32)
        position = base + jnp.arange(MOST, dtype=jnp.int32)
        keep = ((position >= first_row) & (position < first_row + length)).astype(tokens.dtype)[:, None]
        rows_x = lax.dynamic_slice_in_dim(tokens, base, MOST, 0)
        rows_g = lax.dynamic_slice_in_dim(output_gradient, base, MOST, 0)
        rows_u = lax.dynamic_slice_in_dim(input_inner_product, base, MOST, 0) * keep
        rows_h = lax.dynamic_slice_in_dim(hidden_inner_product, base, MOST, 0) * keep
        part_a = jnp.dot(rows_x.T, rows_u, preferred_element_type=jnp.float32)
        part_b = jnp.dot(rows_g.T, rows_h, preferred_element_type=jnp.float32)
        scale = length.astype(jnp.float32)
        return (part_a / scale, part_b / scale)
    grad_a, grad_b = lax.map(one_example, labels)
    feature_a = adam_feature(grad_a, first_moment_down.reshape(MODEL_WIDTH, ADAPTER_RANK), second_moment_down.reshape(MODEL_WIDTH, ADAPTER_RANK))
    feature_b = adam_feature(grad_b, first_moment_up.reshape(HIDDEN_WIDTH, ADAPTER_RANK), second_moment_up.reshape(HIDDEN_WIDTH, ADAPTER_RANK))
    blocks = jnp.arange(BANK, dtype=jnp.int32)
    select_a = (down_row_seeds.reshape(MODEL_WIDTH)[:, None] == blocks[None, :]).astype(jnp.float32)
    select_b = (up_row_seeds.reshape(HIDDEN_WIDTH)[:, None] == blocks[None, :]).astype(jnp.float32)
    summed = jnp.einsum('nj,enr->ejr', select_a, feature_a, precision=lax.Precision.HIGHEST)
    summed = summed + jnp.einsum('nj,enr->ejr', select_b, feature_b, precision=lax.Precision.HIGHEST)
    inverse = 1.0 / math.sqrt((MODEL_WIDTH + HIDDEN_WIDTH) * ADAPTER_RANK)
    sketch = jnp.einsum('ejr,jrk->ek', summed, bank.astype(jnp.float32), precision=lax.Precision.HIGHEST)
    return sketch * inverse
```

```python
import functools
import math

import jax
import jax.numpy as jnp
from jax import lax
from jax.experimental import pallas as pl
from jax.experimental.pallas import tpu as pltpu
from jax.sharding import Mesh, PartitionSpec as P

MODEL_WIDTH = 8192
HIDDEN_WIDTH = 29568
RANK = 128
BANK = 16
EXAMPLES = 4
UP_ROWS = 231
DOWN_ROWS = 64
WINDOW = 256
ROWS = WINDOW + DOWN_ROWS
LOCAL_UP = 7392
PAIR = 2 * RANK
WIDE = EXAMPLES * RANK
BF = jnp.bfloat16
F32 = jnp.float32
VMEM = pl.BlockSpec(memory_space=pltpu.VMEM)
SMEM = pl.BlockSpec(memory_space=pltpu.SMEM)
PLANE = ("ex", "py", "co")


def window_start(owner):
    return jnp.minimum((owner * UP_ROWS) // 16 * 16, LOCAL_UP - WINDOW)


def along(position, shift):
    x, y, c = position
    return (x, (y + shift) % 4, 0) if c == 0 else ((x + shift) % 4, y, 1)


def across(position, shift):
    x, y, c = position
    return ((x + shift) % 4, y, 0) if c == 0 else (x, (y + shift) % 4, 1)


def flat(position):
    return position[0] * 8 + position[1] * 2 + position[2]


def pairs(move):
    everyone = [(x, y, c) for x in range(4) for y in range(4) for c in range(2)]
    return [(flat(p), flat(move(p))) for p in everyone]


def send_same(value, shift):
    return lax.ppermute(value, PLANE, pairs(lambda p: along(p, shift)))


def send_other(value, shift):
    return lax.ppermute(value, PLANE, pairs(lambda p: along((p[0], p[1], 1 - p[2]), shift)))


def send_across(value, shift):
    return lax.ppermute(value, PLANE, pairs(lambda p: across(p, shift)))


def pack_kernel(owner_ref, start_ref, grad_ref, tokens_ref, *rest):
    outs, turned = rest[:8], rest[8]
    turned[...] = tokens_ref[...].T
    for slot in range(8):
        for i in range(4):
            start = pl.multiple_of(start_ref[slot * 4 + i], 16)
            column = pl.multiple_of(owner_ref[slot * 4 + i] * DOWN_ROWS, DOWN_ROWS)
            outs[slot][i, :WINDOW, :] = grad_ref[pl.ds(start, WINDOW), :]
            outs[slot][i, WINDOW:, :] = turned[pl.ds(column, DOWN_ROWS), :]


def partial_kernel(order_ref, *rest):
    same, other, inner, mask_ref = rest[0:4], rest[4:8], rest[8:12], rest[12]
    own_ref, sends = rest[13], rest[14:17]
    right_h, right_u = rest[17], rest[18]
    for k in range(4):
        for e in range(EXAMPLES):
            picked = mask_ref[k, :, e * RANK:(e + 1) * RANK]
            right_h[k, :, e * RANK:(e + 1) * RANK] = inner[k][:, :RANK] * picked
            right_u[k, :, e * RANK:(e + 1) * RANK] = inner[k][:, RANK:] * picked
    for j in range(4):
        i = order_ref[j]
        up = jnp.zeros((WINDOW, WIDE), F32)
        down = jnp.zeros((DOWN_ROWS, WIDE), F32)
        for k in range(4):
            left = jnp.concatenate([same[k][i], other[k][i]], axis=1)
            up += jnp.dot(left[:WINDOW], right_h[k], preferred_element_type=F32)
            down += jnp.dot(left[WINDOW:], right_u[k], preferred_element_type=F32)
        out = own_ref if j == 0 else sends[j - 1]
        out[:WINDOW, :] = up.astype(out.dtype)
        out[WINDOW:, :] = down.astype(out.dtype)


def feature_kernel(own_ref, a_ref, b_ref, c_ref, length_ref, first_ref, second_ref, select_ref, out_ref):
    first = 0.9 * first_ref[...]
    second = 0.999 * second_ref[...]
    select = select_ref[...]
    for e in range(EXAMPLES):
        at = pl.ds(e * RANK, RANK)
        total = own_ref[:, at] + a_ref[:, at].astype(F32) + b_ref[:, at].astype(F32) + c_ref[:, at].astype(F32)
        grad = total / length_ref[e]
        feature = (first + 0.1 * grad) / (jnp.sqrt(second + 0.001 * grad * grad) + 1e-08)
        high = feature.astype(BF)
        low = (feature - high.astype(F32)).astype(BF)
        out_ref[:, at] = jnp.dot(select, high, preferred_element_type=F32) + jnp.dot(
            select, low, preferred_element_type=F32
        )


def spread_sum(value, axes, count):
    copies = jnp.broadcast_to(value[None], (count,) + value.shape)
    return jnp.sum(lax.all_to_all(copies, axes, split_axis=0, concat_axis=0, tiled=True), axis=0)


def on_device(
    tokens,
    output_gradient,
    adapter_down_factor,
    adapter_up_factor,
    first_moment_down,
    second_moment_down,
    first_moment_up,
    second_moment_up,
    down_row_seeds,
    up_row_seeds,
    segments,
    bank,
):
    x, y, c = lax.axis_index("ex"), lax.axis_index("py"), lax.axis_index("co")
    me = x * 8 + y * 2 + c

    portion = jnp.concatenate(
        [
            jnp.dot(tokens, adapter_down_factor, preferred_element_type=F32),
            jnp.dot(output_gradient, adapter_up_factor, preferred_element_type=F32),
        ],
        axis=1,
    )
    whole = portion
    for shift in (1, 2, 3):
        whole = whole + lax.ppermute(portion, ("t1", "t0"), [(i, (i + shift) % 4) for i in range(4)])
    whole = whole.astype(BF)
    sibling = lax.ppermute(whole, "co", [(0, 1), (1, 0)])
    chip_inner = jnp.concatenate([whole, sibling], axis=0)
    inner = [chip_inner] + [send_same(chip_inner, k) for k in (1, 2, 3)]

    steps = jnp.arange(4, dtype=jnp.int32)
    owners_y = 8 * steps[None, :] + 2 * ((y + steps) % 4)[:, None]
    owners_x = 8 * ((x + steps) % 4)[:, None] + 2 * steps[None, :] + 1
    same_owners = jnp.where(c == 0, owners_y, owners_x)
    other_owners = jnp.where(c == 0, owners_x, owners_y)
    owners = jnp.concatenate([same_owners, other_owners], axis=0).reshape(32)
    packed = pl.pallas_call(
        pack_kernel,
        out_shape=[jax.ShapeDtypeStruct((4, ROWS, 128), BF)] * 8,
        in_specs=[SMEM, SMEM, VMEM, VMEM],
        out_specs=[VMEM] * 8,
        scratch_shapes=[pltpu.VMEM((2048, 128), BF)],
        compiler_params=pltpu.CompilerParams(vmem_limit_bytes=32 << 20),
        cost_estimate=pl.CostEstimate(flops=0, bytes_accessed=5 << 20, transcendentals=0),
    )(owners, window_start(owners), output_gradient.T, tokens)
    same = [packed[0]] + [send_same(packed[k], k) for k in (1, 2, 3)]
    other = [send_other(packed[4 + k], k) for k in range(4)]

    chip_x = jnp.where(c == 0, x, (x - steps) % 4)
    chip_y = jnp.where(c == 0, (y - steps) % 4, y)
    chips = segments.reshape(16, 2, 128)[chip_x * 4 + chip_y]
    labels = jnp.concatenate([jnp.where(c == 0, chips[:, 0], chips[:, 1]), jnp.where(c == 0, chips[:, 1], chips[:, 0])], axis=1)
    mask = (labels[:, :, None] == (jnp.arange(WIDE, dtype=jnp.int32) // RANK)).astype(BF)

    order = (jnp.where(c == 0, x, y) + steps) % 4
    sums = pl.pallas_call(
        partial_kernel,
        out_shape=[jax.ShapeDtypeStruct((ROWS, WIDE), F32)] + [jax.ShapeDtypeStruct((ROWS, WIDE), BF)] * 3,
        in_specs=[SMEM] + [VMEM] * 13,
        out_specs=[VMEM] * 4,
        scratch_shapes=[pltpu.VMEM((4, PAIR, WIDE), BF), pltpu.VMEM((4, PAIR, WIDE), BF)],
        compiler_params=pltpu.CompilerParams(vmem_limit_bytes=32 << 20),
        cost_estimate=pl.CostEstimate(flops=2 * 4 * ROWS * 1024 * WIDE, bytes_accessed=6 << 20, transcendentals=0),
    )(order, *same, *other, *inner, mask)
    arrived = [send_across(sums[k], k) for k in (1, 2, 3)]

    lengths = jnp.sum(
        (segments[None, :] == jnp.arange(EXAMPLES, dtype=jnp.int32)[:, None]).astype(jnp.int32), axis=1
    ).astype(F32)
    offset = me * UP_ROWS - window_start(me)

    def placed(up, down, fill):
        space = jnp.full((WINDOW,) + up.shape[1:], fill, up.dtype)
        return jnp.concatenate([lax.dynamic_update_slice_in_dim(space, up, offset, 0), down], axis=0)

    first = placed(first_moment_up[0], first_moment_down[0], 0)
    second = placed(second_moment_up[0], second_moment_down[0], 0)
    seeds = placed(up_row_seeds[0], down_row_seeds[0], -1)
    select = (jnp.arange(BANK, dtype=jnp.int32)[:, None] == seeds[None, :]).astype(BF)
    blocks = pl.pallas_call(
        feature_kernel,
        out_shape=jax.ShapeDtypeStruct((BANK, WIDE), F32),
        in_specs=[VMEM] * 4 + [SMEM] + [VMEM] * 3,
        out_specs=VMEM,
        compiler_params=pltpu.CompilerParams(vmem_limit_bytes=32 << 20),
        cost_estimate=pl.CostEstimate(flops=0, bytes_accessed=3 << 20, transcendentals=0),
    )(sums[0], *arrived, lengths, first, second, select)

    half = BANK // 2
    kept = lax.dynamic_slice_in_dim(blocks, c * half, half, 0)
    given = lax.dynamic_slice_in_dim(blocks, (1 - c) * half, half, 0)
    total = kept + lax.ppermute(given, "co", [(0, 1), (1, 0)])
    total = spread_sum(total, ("ex", "t1"), 8)
    total = spread_sum(total, ("t0", "py"), 8)
    theirs = lax.ppermute(total, "co", [(0, 1), (1, 0)])
    summed = jnp.concatenate([jnp.where(c == 0, total, theirs), jnp.where(c == 0, theirs, total)], axis=0)
    inverse = 1.0 / math.sqrt((MODEL_WIDTH + HIDDEN_WIDTH) * RANK)
    sketch = jnp.einsum(
        "jer,jrk->ek", summed.reshape(BANK, EXAMPLES, RANK), bank.astype(F32), precision=lax.Precision.HIGHEST
    )
    return sketch * inverse


def solution(mesh):
    rows = ("ex", "py", "co")
    tp = ("t1", "t0")
    split = Mesh(mesh.devices.reshape(4, 2, 2, 4, 2), ("ex", "t1", "t0", "py", "co"))
    return jax.shard_map(
        on_device,
        mesh=split,
        in_specs=(
            P(rows, tp),
            P(rows, tp),
            P(tp, None),
            P(tp, None),
            P(tp, rows, None),
            P(tp, rows, None),
            P(tp, rows, None),
            P(tp, rows, None),
            P(tp, rows),
            P(tp, rows),
            P(),
            P(None, None, ("ex", "t1", "t0", "py", "co")),
        ),
        out_specs=P(None, ("ex", "t1", "t0", "py", "co")),
        check_vma=False,
    )
```

```python
import functools
import math

import jax
import jax.numpy as jnp
from jax import lax
from jax.experimental import pallas as pl
from jax.experimental.pallas import tpu as pltpu
from jax.sharding import Mesh, PartitionSpec as P

MODEL_WIDTH = 8192
HIDDEN_WIDTH = 29568
RANK = 128
BANK = 16
EXAMPLES = 4
UP_ROWS = 231
DOWN_ROWS = 64
WINDOW = 256
ROWS = WINDOW + DOWN_ROWS
LOCAL_UP = 7392
PAIR = 2 * RANK
WIDE = EXAMPLES * RANK
BF = jnp.bfloat16
F32 = jnp.float32
VMEM = pl.BlockSpec(memory_space=pltpu.VMEM)
ANY = pl.BlockSpec(memory_space=pl.ANY)
SMEM = pl.BlockSpec(memory_space=pltpu.SMEM)
PLANE = ("ex", "py", "co")


def window_start(owner):
    return jnp.minimum((owner * UP_ROWS) // 16 * 16, LOCAL_UP - WINDOW)


def along(position, shift):
    x, y, c = position
    return (x, (y + shift) % 4, 0) if c == 0 else ((x + shift) % 4, y, 1)


def across(position, shift):
    x, y, c = position
    return ((x + shift) % 4, y, 0) if c == 0 else (x, (y + shift) % 4, 1)


def flat(position):
    return position[0] * 8 + position[1] * 2 + position[2]


def pairs(move):
    everyone = [(x, y, c) for x in range(4) for y in range(4) for c in range(2)]
    return [(flat(p), flat(move(p))) for p in everyone]


def send_same(value, shift):
    return lax.ppermute(value, PLANE, pairs(lambda p: along(p, shift)))


def send_other(value, shift):
    return lax.ppermute(value, PLANE, pairs(lambda p: along((p[0], p[1], 1 - p[2]), shift)))


def send_across(value, shift):
    return lax.ppermute(value, PLANE, pairs(lambda p: across(p, shift)))


def pack_kernel(where_ref, grad_hbm, tokens_ref, down_ref, up_ref, *rest):
    outs, portion_ref = rest[:8], rest[8]
    grad, turned, load, sent = rest[9:]
    load_grad = pltpu.make_async_copy(grad_hbm, grad, load)
    load_grad.start()
    x, y, c = where_ref[0], where_ref[1], where_ref[2]
    turned[...] = tokens_ref[...].T
    copies = []
    for slot in range(8):
        target = c if slot < 4 else 1 - c
        k = slot % 4
        for i in range(4):
            to_x = lax.rem(x + jnp.where(target == 0, i, k), 4)
            to_y = lax.rem(y + jnp.where(target == 0, k, i), 4)
            owner = to_x * 8 + to_y * 2 + target
            start = pl.multiple_of(window_start(owner), 16)
            column = pl.multiple_of(owner * DOWN_ROWS, DOWN_ROWS)
            copies.append(
                pltpu.make_async_copy(
                    grad.at[pl.ds(start, WINDOW)], outs[slot].at[pl.ds(i * WINDOW, WINDOW)], sent
                )
            )
            copies.append(
                pltpu.make_async_copy(
                    turned.at[pl.ds(column, DOWN_ROWS)], outs[slot].at[pl.ds(4 * WINDOW + i * DOWN_ROWS, DOWN_ROWS)], sent
                )
            )
    portion_ref[:, :RANK] = jnp.dot(tokens_ref[...], down_ref[...], preferred_element_type=F32)
    load_grad.wait()
    for copy in copies:
        copy.start()
    product = jnp.zeros((128, RANK), F32)
    for begin in range(0, LOCAL_UP, 1024):
        end = min(begin + 1024, LOCAL_UP)
        product += lax.dot_general(
            grad[begin:end, :], up_ref[begin:end, :], (((0,), (0,)), ((), ())), preferred_element_type=F32
        )
    portion_ref[:, RANK:] = product
    for copy in copies:
        copy.wait()


def partial_kernel(where_ref, bounds_ref, *rest):
    columns, inner = rest[0:8], rest[8:12]
    own_ref, sends = rest[12], rest[13:16]
    left, right_h, right_u, arrive = rest[16:]
    copies = [
        pltpu.make_async_copy(columns[s], left.at[:, pl.ds((2 * (s % 4) + s // 4) * 128, 128)], arrive) for s in range(8)
    ]
    for copy in copies:
        copy.start()
    x, y, c = where_ref[0], where_ref[1], where_ref[2]
    row = lax.broadcasted_iota(jnp.int32, (128, RANK), 0)
    for k in range(4):
        chip = jnp.where(c == 0, x * 4 + lax.rem(y - k + 4, 4), lax.rem(x - k + 4, 4) * 4 + y)
        for part in range(2):
            token = row + (chip * PAIR + jnp.where(part == 0, c, 1 - c) * 128)
            rows = pl.ds(k * PAIR + part * 128, 128)
            h = inner[k][part * 128:(part + 1) * 128, :RANK]
            u = inner[k][part * 128:(part + 1) * 128, RANK:]
            for e in range(EXAMPLES):
                inside = (token >= bounds_ref[e]) & (token < bounds_ref[e + 1])
                picked = jnp.where(inside, 1.0, 0.0).astype(BF)
                right_h[rows, e * RANK:(e + 1) * RANK] = h * picked
                right_u[rows, e * RANK:(e + 1) * RANK] = u * picked
    for copy in copies:
        copy.wait()
    for j in range(4):
        up = jnp.dot(left[j * WINDOW:(j + 1) * WINDOW, :], right_h[...], preferred_element_type=F32)
        out = own_ref if j == 0 else sends[j - 1]
        out[:WINDOW, :] = up.astype(out.dtype)
    down = jnp.dot(left[4 * WINDOW:, :], right_u[...], preferred_element_type=F32)
    for j in range(4):
        out = own_ref if j == 0 else sends[j - 1]
        out[WINDOW:, :] = down[j * DOWN_ROWS:(j + 1) * DOWN_ROWS].astype(out.dtype)


def feature_kernel(
    own_ref, a_ref, b_ref, c_ref, bounds_ref, offset_ref, select_ref,
    first_up, first_down, second_up, second_down, out_ref, first_ref, second_ref,
):
    for up, down, space in ((first_up, first_down, first_ref), (second_up, second_down, second_ref)):
        space[:WINDOW, :] = jnp.zeros((WINDOW, RANK), F32)
        space[:UP_ROWS, :] = up[...]
        space[:WINDOW, :] = pltpu.roll(space[:WINDOW, :], offset_ref[0], 0)
        space[WINDOW:, :] = down[...]
    first = 0.9 * first_ref[...]
    second = 0.999 * second_ref[...]
    select = select_ref[...]
    for e in range(EXAMPLES):
        at = pl.ds(e * RANK, RANK)
        length = (bounds_ref[e + 1] - bounds_ref[e]).astype(F32)
        total = own_ref[:, at] + a_ref[:, at].astype(F32) + b_ref[:, at].astype(F32) + c_ref[:, at].astype(F32)
        grad = total / length
        feature = (first + 0.1 * grad) / (jnp.sqrt(second + 0.001 * grad * grad) + 1e-08)
        high = feature.astype(BF)
        low = (feature - high.astype(F32)).astype(BF)
        out_ref[:, at] = jnp.dot(select, high, preferred_element_type=F32) + jnp.dot(
            select, low, preferred_element_type=F32
        )


def spread_sum(value, axes, count):
    copies = jnp.broadcast_to(value[None], (count,) + value.shape)
    return jnp.sum(lax.all_to_all(copies, axes, split_axis=0, concat_axis=0, tiled=True), axis=0)


def on_device(
    tokens,
    output_gradient,
    adapter_down_factor,
    adapter_up_factor,
    first_moment_down,
    second_moment_down,
    first_moment_up,
    second_moment_up,
    down_row_seeds,
    up_row_seeds,
    segments,
    bank,
):
    x, y, c = lax.axis_index("ex"), lax.axis_index("py"), lax.axis_index("co")
    me = x * 8 + y * 2 + c
    where = jnp.stack([x, y, c]).astype(jnp.int32)
    bounds = jnp.sum(
        (segments[None, :] < jnp.arange(EXAMPLES + 1, dtype=jnp.int32)[:, None]).astype(jnp.int32), axis=1
    )

    packed = pl.pallas_call(
        pack_kernel,
        out_shape=[jax.ShapeDtypeStruct((4 * ROWS, 128), BF)] * 8 + [jax.ShapeDtypeStruct((128, PAIR), F32)],
        in_specs=[SMEM, ANY, VMEM, VMEM, VMEM],
        out_specs=[ANY] * 8 + [VMEM],
        scratch_shapes=[
            pltpu.VMEM((LOCAL_UP, 128), BF),
            pltpu.VMEM((2048, 128), BF),
            pltpu.SemaphoreType.DMA,
            pltpu.SemaphoreType.DMA,
        ],
        compiler_params=pltpu.CompilerParams(vmem_limit_bytes=24 << 20),
        cost_estimate=pl.CostEstimate(flops=2 * 128 * 9440 * 128, bytes_accessed=8 << 20, transcendentals=0),
    )(where, output_gradient.T, tokens, adapter_down_factor, adapter_up_factor)
    portion = packed[8]
    whole = portion
    for shift in (1, 2, 3):
        whole = whole + lax.ppermute(portion, ("t1", "t0"), [(i, (i + shift) % 4) for i in range(4)])
    whole = whole.astype(BF)
    sibling = lax.ppermute(whole, "co", [(0, 1), (1, 0)])
    chip_inner = jnp.concatenate([whole, sibling], axis=0)
    inner = [chip_inner] + [send_same(chip_inner, k) for k in (1, 2, 3)]
    same = [packed[0]] + [send_same(packed[k], k) for k in (1, 2, 3)]
    other = [send_other(packed[4 + k], k) for k in range(4)]

    sums = pl.pallas_call(
        partial_kernel,
        out_shape=[jax.ShapeDtypeStruct((ROWS, WIDE), F32)] + [jax.ShapeDtypeStruct((ROWS, WIDE), BF)] * 3,
        in_specs=[SMEM, SMEM] + [ANY] * 8 + [VMEM] * 4,
        out_specs=[VMEM] * 4,
        scratch_shapes=[
            pltpu.VMEM((4 * ROWS, 1024), BF),
            pltpu.VMEM((1024, WIDE), BF),
            pltpu.VMEM((1024, WIDE), BF),
            pltpu.SemaphoreType.DMA,
        ],
        compiler_params=pltpu.CompilerParams(vmem_limit_bytes=24 << 20),
        cost_estimate=pl.CostEstimate(flops=2 * 4 * ROWS * 1024 * WIDE, bytes_accessed=6 << 20, transcendentals=0),
    )(where, bounds, *same, *other, *inner)
    arrived = [send_across(sums[k], k) for k in (1, 2, 3)]

    kept = (first_moment_up, second_moment_up, up_row_seeds, down_row_seeds)
    own, kept = lax.optimization_barrier((sums[0], kept))
    first_moment_up, second_moment_up, up_row_seeds, down_row_seeds = kept
    offset = me * UP_ROWS - window_start(me)
    seeds = jnp.concatenate(
        [
            lax.dynamic_update_slice_in_dim(jnp.full((WINDOW,), -1, jnp.int32), up_row_seeds[0], offset, 0),
            down_row_seeds[0],
        ]
    )
    select = (jnp.arange(BANK, dtype=jnp.int32)[:, None] == seeds[None, :]).astype(BF)
    blocks = pl.pallas_call(
        feature_kernel,
        out_shape=jax.ShapeDtypeStruct((BANK, WIDE), F32),
        in_specs=[VMEM] * 4 + [SMEM] * 2 + [VMEM] * 5,
        out_specs=VMEM,
        scratch_shapes=[pltpu.VMEM((ROWS, RANK), F32), pltpu.VMEM((ROWS, RANK), F32)],
        compiler_params=pltpu.CompilerParams(vmem_limit_bytes=24 << 20),
        cost_estimate=pl.CostEstimate(flops=0, bytes_accessed=3 << 20, transcendentals=0),
    )(
        own, *arrived, bounds, offset.astype(jnp.int32)[None], select,
        first_moment_up[0], first_moment_down[0], second_moment_up[0], second_moment_down[0],
    )

    half = BANK // 2
    kept = lax.dynamic_slice_in_dim(blocks, c * half, half, 0)
    given = lax.dynamic_slice_in_dim(blocks, (1 - c) * half, half, 0)
    total = kept + lax.ppermute(given, "co", [(0, 1), (1, 0)])
    total = spread_sum(total, ("ex", "t1"), 8)
    total = spread_sum(total, ("t0", "py"), 8)
    theirs = lax.ppermute(total, "co", [(0, 1), (1, 0)])
    summed = jnp.concatenate([jnp.where(c == 0, total, theirs), jnp.where(c == 0, theirs, total)], axis=0)
    inverse = 1.0 / math.sqrt((MODEL_WIDTH + HIDDEN_WIDTH) * RANK)
    sketch = jnp.einsum(
        "jer,jrk->ek", summed.reshape(BANK, EXAMPLES, RANK), bank.astype(F32), precision=lax.Precision.HIGHEST
    )
    return sketch * inverse


def solution(mesh):
    rows = ("ex", "py", "co")
    tp = ("t1", "t0")
    split = Mesh(mesh.devices.reshape(4, 2, 2, 4, 2), ("ex", "t1", "t0", "py", "co"))
    return jax.shard_map(
        on_device,
        mesh=split,
        in_specs=(
            P(rows, tp),
            P(rows, tp),
            P(tp, None),
            P(tp, None),
            P(tp, rows, None),
            P(tp, rows, None),
            P(tp, rows, None),
            P(tp, rows, None),
            P(tp, rows),
            P(tp, rows),
            P(),
            P(None, None, ("ex", "t1", "t0", "py", "co")),
        ),
        out_specs=P(None, ("ex", "t1", "t0", "py", "co")),
        check_vma=False,
    )
```

```python
import functools
import math

import jax
import jax.numpy as jnp
from jax import lax
from jax.experimental import pallas as pl
from jax.experimental.pallas import tpu as pltpu
from jax.sharding import Mesh, PartitionSpec as P

MODEL_WIDTH = 8192
HIDDEN_WIDTH = 29568
RANK = 128
BANK = 16
EXAMPLES = 4
UP_ROWS = 231
DOWN_ROWS = 64
WINDOW = 256
ROWS = WINDOW + DOWN_ROWS
LOCAL_UP = 7392
PAIR = 2 * RANK
WIDE = EXAMPLES * RANK
BF = jnp.bfloat16
F32 = jnp.float32
VMEM = pl.BlockSpec(memory_space=pltpu.VMEM)
ANY = pl.BlockSpec(memory_space=pl.ANY)
SMEM = pl.BlockSpec(memory_space=pltpu.SMEM)
PLANE = ("ex", "py", "co")


def window_start(owner):
    return jnp.minimum((owner * UP_ROWS) // 16 * 16, LOCAL_UP - WINDOW)


def along(position, shift):
    x, y, c = position
    return (x, (y + shift) % 4, 0) if c == 0 else ((x + shift) % 4, y, 1)


def across(position, shift):
    x, y, c = position
    return ((x + shift) % 4, y, 0) if c == 0 else (x, (y + shift) % 4, 1)


def flat(position):
    return position[0] * 8 + position[1] * 2 + position[2]


def pairs(move):
    everyone = [(x, y, c) for x in range(4) for y in range(4) for c in range(2)]
    return [(flat(p), flat(move(p))) for p in everyone]


def send_same(value, shift):
    return lax.ppermute(value, PLANE, pairs(lambda p: along(p, shift)))


def send_other(value, shift):
    return lax.ppermute(value, PLANE, pairs(lambda p: along((p[0], p[1], 1 - p[2]), shift)))


def send_across(value, shift):
    return lax.ppermute(value, PLANE, pairs(lambda p: across(p, shift)))


def pack_kernel(where_ref, grad_hbm, tokens_hbm, down_hbm, up_hbm, *rest):
    outs, portion_ref = rest[:8], rest[8]
    grad, tokens, down, up, turned, loads, sent = rest[9:]
    arrivals = [
        pltpu.make_async_copy(source, target, loads.at[i])
        for i, (source, target) in enumerate(((tokens_hbm, tokens), (grad_hbm, grad), (down_hbm, down), (up_hbm, up)))
    ]
    for arrival in arrivals:
        arrival.start()
    x, y, c = where_ref[0], where_ref[1], where_ref[2]
    turned_copies, grad_copies = [], []
    for slot in range(8):
        target = c if slot < 4 else 1 - c
        k = slot % 4
        for i in range(4):
            to_x = lax.rem(x + jnp.where(target == 0, i, k), 4)
            to_y = lax.rem(y + jnp.where(target == 0, k, i), 4)
            owner = to_x * 8 + to_y * 2 + target
            start = pl.multiple_of(window_start(owner), 16)
            column = pl.multiple_of(owner * DOWN_ROWS, DOWN_ROWS)
            grad_copies.append(
                pltpu.make_async_copy(
                    grad.at[pl.ds(start, WINDOW)], outs[slot].at[pl.ds(i * WINDOW, WINDOW)], sent
                )
            )
            turned_copies.append(
                pltpu.make_async_copy(
                    turned.at[pl.ds(column, DOWN_ROWS)], outs[slot].at[pl.ds(4 * WINDOW + i * DOWN_ROWS, DOWN_ROWS)], sent
                )
            )
    arrivals[0].wait()
    turned[...] = tokens[...].T
    for copy in turned_copies:
        copy.start()
    arrivals[1].wait()
    for copy in grad_copies:
        copy.start()
    arrivals[2].wait()
    portion_ref[:, :RANK] = jnp.dot(tokens[...], down[...], preferred_element_type=F32)
    arrivals[3].wait()
    product = jnp.zeros((128, RANK), F32)
    for begin in range(0, LOCAL_UP, 1024):
        end = min(begin + 1024, LOCAL_UP)
        product += lax.dot_general(
            grad[begin:end, :], up[begin:end, :], (((0,), (0,)), ((), ())), preferred_element_type=F32
        )
    portion_ref[:, RANK:] = product
    for copy in turned_copies + grad_copies:
        copy.wait()


def partial_kernel(where_ref, bounds_ref, *rest):
    columns, inner, outs = rest[0:8], rest[8:12], rest[12:16]
    left, side, right_h, right_u, own, sends, inner_sem, columns_sem, sent = rest[16:]
    inner_copies = [pltpu.make_async_copy(inner[k], side.at[k], inner_sem) for k in range(4)]
    column_copies = [pltpu.make_async_copy(columns[s], left.at[2 * (s % 4) + s // 4], columns_sem) for s in range(8)]
    for copy in inner_copies + column_copies:
        copy.start()
    x, y, c = where_ref[0], where_ref[1], where_ref[2]
    row = lax.broadcasted_iota(jnp.int32, (128, RANK), 0)
    for copy in inner_copies:
        copy.wait()
    for k in range(4):
        chip = jnp.where(c == 0, x * 4 + lax.rem(y - k + 4, 4), lax.rem(x - k + 4, 4) * 4 + y)
        for part in range(2):
            token = row + (chip * PAIR + jnp.where(part == 0, c, 1 - c) * 128)
            rows = pl.ds(k * PAIR + part * 128, 128)
            h = side[k, part * 128:(part + 1) * 128, :RANK]
            u = side[k, part * 128:(part + 1) * 128, RANK:]
            for e in range(EXAMPLES):
                inside = (token >= bounds_ref[e]) & (token < bounds_ref[e + 1])
                picked = jnp.where(inside, 1.0, 0.0).astype(BF)
                right_h[rows, e * RANK:(e + 1) * RANK] = h * picked
                right_u[rows, e * RANK:(e + 1) * RANK] = u * picked
    for copy in column_copies:
        copy.wait()

    def joined(begin, count):
        return jnp.concatenate([left[s, begin:begin + count, :] for s in range(8)], axis=1)

    down = jnp.dot(joined(4 * WINDOW, 4 * DOWN_ROWS), right_u[...], preferred_element_type=F32)
    out_copies = []
    for j in (1, 2, 3, 0):
        up = jnp.dot(joined(j * WINDOW, WINDOW), right_h[...], preferred_element_type=F32)
        out = own if j == 0 else sends.at[j - 1]
        out[:WINDOW, :] = up.astype(out.dtype)
        out[WINDOW:, :] = down[j * DOWN_ROWS:(j + 1) * DOWN_ROWS].astype(out.dtype)
        out_copies.append(pltpu.make_async_copy(out, outs[j], sent))
        out_copies[-1].start()
    for copy in out_copies:
        copy.wait()


def feature_kernel(
    own_ref, a_ref, b_ref, c_ref, bounds_ref, offset_ref, select_ref,
    first_up, first_down, second_up, second_down, out_ref, first_ref, second_ref,
):
    for up, down, space in ((first_up, first_down, first_ref), (second_up, second_down, second_ref)):
        space[:WINDOW, :] = jnp.zeros((WINDOW, RANK), F32)
        space[:UP_ROWS, :] = up[...]
        space[:WINDOW, :] = pltpu.roll(space[:WINDOW, :], offset_ref[0], 0)
        space[WINDOW:, :] = down[...]
    first = 0.9 * first_ref[...]
    second = 0.999 * second_ref[...]
    select = select_ref[...]
    for e in range(EXAMPLES):
        at = pl.ds(e * RANK, RANK)
        length = (bounds_ref[e + 1] - bounds_ref[e]).astype(F32)
        total = own_ref[:, at] + a_ref[:, at].astype(F32) + b_ref[:, at].astype(F32) + c_ref[:, at].astype(F32)
        grad = total / length
        feature = (first + 0.1 * grad) / (jnp.sqrt(second + 0.001 * grad * grad) + 1e-08)
        high = feature.astype(BF)
        low = (feature - high.astype(F32)).astype(BF)
        out_ref[:, at] = jnp.dot(select, high, preferred_element_type=F32) + jnp.dot(
            select, low, preferred_element_type=F32
        )


EVERY = ("ex", "t1", "t0", "py", "co")


def groups(along_x):
    found = []
    for fixed in range(4):
        for c in range(2):
            for zs in ((0, 1), (2, 3)) if along_x else ((0, 3), (1, 2)):
                found.append(
                    [
                        (((x * 4 + z) * 4) + y) * 2 + c
                        for w in range(4)
                        for z in zs
                        for x, y in [(w, fixed) if along_x else (fixed, w)]
                    ]
                )
    return found


def spread_sum(value, along_x):
    copies = jnp.broadcast_to(value[None], (8,) + value.shape)
    arrived = lax.all_to_all(
        copies, EVERY, split_axis=0, concat_axis=0, tiled=True, axis_index_groups=groups(along_x)
    )
    return jnp.sum(arrived, axis=0)


def on_device(
    tokens,
    output_gradient,
    adapter_down_factor,
    adapter_up_factor,
    first_moment_down,
    second_moment_down,
    first_moment_up,
    second_moment_up,
    down_row_seeds,
    up_row_seeds,
    segments,
    bank,
):
    x, y, c = lax.axis_index("ex"), lax.axis_index("py"), lax.axis_index("co")
    me = x * 8 + y * 2 + c
    where = jnp.stack([x, y, c]).astype(jnp.int32)
    bounds = jnp.sum(
        (segments[None, :] < jnp.arange(EXAMPLES + 1, dtype=jnp.int32)[:, None]).astype(jnp.int32), axis=1
    )

    packed = pl.pallas_call(
        pack_kernel,
        out_shape=[jax.ShapeDtypeStruct((4 * ROWS, 128), BF)] * 8 + [jax.ShapeDtypeStruct((128, PAIR), F32)],
        in_specs=[SMEM, ANY, ANY, ANY, ANY],
        out_specs=[ANY] * 8 + [VMEM],
        scratch_shapes=[
            pltpu.VMEM((LOCAL_UP, 128), BF),
            pltpu.VMEM((128, 2048), BF),
            pltpu.VMEM((2048, 128), BF),
            pltpu.VMEM((LOCAL_UP, 128), BF),
            pltpu.VMEM((2048, 128), BF),
            pltpu.SemaphoreType.DMA((4,)),
            pltpu.SemaphoreType.DMA,
        ],
        compiler_params=pltpu.CompilerParams(vmem_limit_bytes=60 << 20),
        cost_estimate=pl.CostEstimate(flops=2 * 128 * 9440 * 128, bytes_accessed=8 << 20, transcendentals=0),
    )(where, output_gradient.T, tokens, adapter_down_factor, adapter_up_factor)
    portion = packed[8]
    whole = portion
    for shift in (1, 2, 3):
        whole = whole + lax.ppermute(portion, ("t1", "t0"), [(i, (i + shift) % 4) for i in range(4)])
    whole = whole.astype(BF)
    sibling = lax.ppermute(whole, "co", [(0, 1), (1, 0)])
    chip_inner = jnp.concatenate([whole, sibling], axis=0)
    same = [packed[0]] + [send_same(packed[k], k) for k in (1, 2, 3)]
    other = [send_other(packed[4 + k], k) for k in range(4)]
    chip_inner, same[1] = lax.optimization_barrier((chip_inner, same[1]))
    inner = [chip_inner] + [send_same(chip_inner, k) for k in (1, 2, 3)]

    sums = pl.pallas_call(
        partial_kernel,
        out_shape=[jax.ShapeDtypeStruct((ROWS, WIDE), F32)] + [jax.ShapeDtypeStruct((ROWS, WIDE), BF)] * 3,
        in_specs=[SMEM, SMEM] + [ANY] * 12,
        out_specs=[ANY] * 4,
        scratch_shapes=[
            pltpu.VMEM((8, 4 * ROWS, 128), BF),
            pltpu.VMEM((4, PAIR, PAIR), BF),
            pltpu.VMEM((1024, WIDE), BF),
            pltpu.VMEM((1024, WIDE), BF),
            pltpu.VMEM((ROWS, WIDE), F32),
            pltpu.VMEM((3, ROWS, WIDE), BF),
            pltpu.SemaphoreType.DMA,
            pltpu.SemaphoreType.DMA,
            pltpu.SemaphoreType.DMA,
        ],
        compiler_params=pltpu.CompilerParams(vmem_limit_bytes=60 << 20),
        cost_estimate=pl.CostEstimate(flops=2 * 4 * ROWS * 1024 * WIDE, bytes_accessed=6 << 20, transcendentals=0),
    )(where, bounds, *same, *other, *inner)
    arrived = [send_across(sums[k], k) for k in (1, 2, 3)]

    kept = (first_moment_up, second_moment_up, up_row_seeds, down_row_seeds)
    own, kept = lax.optimization_barrier((sums[0], kept))
    first_moment_up, second_moment_up, up_row_seeds, down_row_seeds = kept
    offset = me * UP_ROWS - window_start(me)
    seeds = jnp.concatenate(
        [
            lax.dynamic_update_slice_in_dim(jnp.full((WINDOW,), -1, jnp.int32), up_row_seeds[0], offset, 0),
            down_row_seeds[0],
        ]
    )
    select = (jnp.arange(BANK, dtype=jnp.int32)[:, None] == seeds[None, :]).astype(BF)
    blocks = pl.pallas_call(
        feature_kernel,
        out_shape=jax.ShapeDtypeStruct((BANK, WIDE), F32),
        in_specs=[VMEM] * 4 + [SMEM] * 2 + [VMEM] * 5,
        out_specs=VMEM,
        scratch_shapes=[pltpu.VMEM((ROWS, RANK), F32), pltpu.VMEM((ROWS, RANK), F32)],
        compiler_params=pltpu.CompilerParams(vmem_limit_bytes=24 << 20),
        cost_estimate=pl.CostEstimate(flops=0, bytes_accessed=3 << 20, transcendentals=0),
    )(
        own, *arrived, bounds, offset.astype(jnp.int32)[None], select,
        first_moment_up[0], first_moment_down[0], second_moment_up[0], second_moment_down[0],
    )

    half = BANK // 2
    kept = lax.dynamic_slice_in_dim(blocks, c * half, half, 0)
    given = lax.dynamic_slice_in_dim(blocks, (1 - c) * half, half, 0)
    total = kept + lax.ppermute(given, "co", [(0, 1), (1, 0)])
    total = spread_sum(total, True)
    total = spread_sum(total, False)
    theirs = lax.ppermute(total, "co", [(0, 1), (1, 0)])
    summed = jnp.concatenate([jnp.where(c == 0, total, theirs), jnp.where(c == 0, theirs, total)], axis=0)
    inverse = 1.0 / math.sqrt((MODEL_WIDTH + HIDDEN_WIDTH) * RANK)
    sketch = jnp.einsum(
        "jer,jrk->ek", summed.reshape(BANK, EXAMPLES, RANK), bank.astype(F32), precision=lax.Precision.HIGHEST
    )
    return sketch * inverse


def solution(mesh):
    rows = ("ex", "py", "co")
    tp = ("t1", "t0")
    split = Mesh(mesh.devices.reshape(4, 2, 2, 4, 2), ("ex", "t1", "t0", "py", "co"))
    return jax.shard_map(
        on_device,
        mesh=split,
        in_specs=(
            P(rows, tp),
            P(rows, tp),
            P(tp, None),
            P(tp, None),
            P(tp, rows, None),
            P(tp, rows, None),
            P(tp, rows, None),
            P(tp, rows, None),
            P(tp, rows),
            P(tp, rows),
            P(),
            P(None, None, ("ex", "t1", "t0", "py", "co")),
        ),
        out_specs=P(None, ("ex", "t1", "t0", "py", "co")),
        check_vma=False,
    )
```

```python
import functools
import math

import jax
import jax.numpy as jnp
from jax import lax
from jax.experimental import pallas as pl
from jax.experimental.pallas import tpu as pltpu
from jax.sharding import Mesh, PartitionSpec as P

MODEL_WIDTH = 8192
HIDDEN_WIDTH = 29568
RANK = 128
BANK = 16
EXAMPLES = 4
UP_ROWS = 231
DOWN_ROWS = 64
WINDOW = 256
ROWS = WINDOW + DOWN_ROWS
LOCAL_UP = 7392
PAIR = 2 * RANK
WIDE = EXAMPLES * RANK
BF = jnp.bfloat16
F32 = jnp.float32
VMEM = pl.BlockSpec(memory_space=pltpu.VMEM)
ANY = pl.BlockSpec(memory_space=pl.ANY)
SMEM = pl.BlockSpec(memory_space=pltpu.SMEM)
PLANE = ("ex", "py", "co")


def window_start(owner):
    return jnp.minimum((owner * UP_ROWS) // 16 * 16, LOCAL_UP - WINDOW)


def along(position, shift):
    x, y, c = position
    return (x, (y + shift) % 4, 0) if c == 0 else ((x + shift) % 4, y, 1)


def across(position, shift):
    x, y, c = position
    return ((x + shift) % 4, y, 0) if c == 0 else (x, (y + shift) % 4, 1)


def flat(position):
    return position[0] * 8 + position[1] * 2 + position[2]


def pairs(move):
    everyone = [(x, y, c) for x in range(4) for y in range(4) for c in range(2)]
    return [(flat(p), flat(move(p))) for p in everyone]


def send_same(value, shift):
    return lax.ppermute(value, PLANE, pairs(lambda p: along(p, shift)))


def send_across(value, shift):
    return lax.ppermute(value, PLANE, pairs(lambda p: across(p, shift)))


def position():
    return lax.axis_index("ex"), lax.axis_index("py"), lax.axis_index("co")


def pack_kernel(grad_hbm, tokens_hbm, down_hbm, up_hbm, give_ref, own_ref, *rest):
    sends, portion_ref = rest[:3], rest[3]
    grad, tokens, down, up, turned, loads, sent = rest[4:]
    arrivals = [
        pltpu.make_async_copy(source, target, loads.at[i])
        for i, (source, target) in enumerate(((tokens_hbm, tokens), (grad_hbm, grad), (down_hbm, down), (up_hbm, up)))
    ]
    for arrival in arrivals:
        arrival.start()
    x, y, c = position()
    outs = [give_ref.at[k] for k in range(4)] + [own_ref] + [send.at[0] for send in sends]
    turned_copies, grad_copies = [], []
    for slot in range(8):
        target = 1 - c if slot < 4 else c
        k = slot % 4
        for i in range(4):
            to_x = lax.rem(x + jnp.where(target == 0, i, k), 4)
            to_y = lax.rem(y + jnp.where(target == 0, k, i), 4)
            owner = to_x * 8 + to_y * 2 + target
            start = pl.multiple_of(window_start(owner), 16)
            column = pl.multiple_of(owner * DOWN_ROWS, DOWN_ROWS)
            grad_copies.append(
                pltpu.make_async_copy(
                    grad.at[pl.ds(start, WINDOW)], outs[slot].at[pl.ds(i * WINDOW, WINDOW)], sent
                )
            )
            turned_copies.append(
                pltpu.make_async_copy(
                    turned.at[pl.ds(column, DOWN_ROWS)], outs[slot].at[pl.ds(4 * WINDOW + i * DOWN_ROWS, DOWN_ROWS)], sent
                )
            )
    arrivals[0].wait()
    turned[...] = tokens[...].T
    for copy in turned_copies:
        copy.start()
    arrivals[1].wait()
    for copy in grad_copies:
        copy.start()
    arrivals[2].wait()
    portion_ref[:, :RANK] = jnp.dot(tokens[...], down[...], preferred_element_type=F32)
    arrivals[3].wait()
    product = jnp.zeros((128, RANK), F32)
    for begin in range(0, LOCAL_UP, 1024):
        end = min(begin + 1024, LOCAL_UP)
        product += lax.dot_general(
            grad[begin:end, :], up[begin:end, :], (((0,), (0,)), ((), ())), preferred_element_type=F32
        )
    portion_ref[:, RANK:] = product
    for copy in turned_copies + grad_copies:
        copy.wait()


def fill_kernel(taken_ref, a_in, b_in, c_in, a_ref, b_ref, c_ref, sent):
    copies = [
        pltpu.make_async_copy(taken_ref.at[k + 1], send.at[1], sent) for k, send in enumerate((a_ref, b_ref, c_ref))
    ]
    for copy in copies:
        copy.start()
    for copy in copies:
        copy.wait()


def partial_kernel(chunks, bounds_ref, own_ref, taken_ref, *rest):
    count = len(chunks)
    arrived, inner, outs = rest[0:3], rest[3:7], rest[7:7 + count]
    left, side, right_h, right_u, done, inner_sem, columns_sem, sent = rest[7 + count:]
    inner_copies = [pltpu.make_async_copy(inner[k], side.at[k], inner_sem) for k in range(4)]
    column_copies = []
    for s in range(8):
        k, part = s // 2, s % 2
        source = arrived[k - 1].at[part] if k else (taken_ref.at[0] if part else own_ref)
        for n, j in enumerate(chunks):
            for begin, at, size in ((j * WINDOW, n * WINDOW, WINDOW), (4 * WINDOW + j * DOWN_ROWS, count * WINDOW + n * DOWN_ROWS, DOWN_ROWS)):
                column_copies.append(
                    pltpu.make_async_copy(source.at[pl.ds(begin, size)], left.at[s, pl.ds(at, size)], columns_sem)
                )
    for copy in inner_copies + column_copies:
        copy.start()
    x, y, c = position()
    row = lax.broadcasted_iota(jnp.int32, (128, RANK), 0)
    for copy in inner_copies:
        copy.wait()
    for k in range(4):
        chip = jnp.where(c == 0, x * 4 + lax.rem(y - k + 4, 4), lax.rem(x - k + 4, 4) * 4 + y)
        for part in range(2):
            token = row + (chip * PAIR + jnp.where(part == 0, c, 1 - c) * 128)
            rows = pl.ds(k * PAIR + part * 128, 128)
            h = side[k, part * 128:(part + 1) * 128, :RANK]
            u = side[k, part * 128:(part + 1) * 128, RANK:]
            for e in range(EXAMPLES):
                inside = (token >= bounds_ref[e]) & (token < bounds_ref[e + 1])
                picked = jnp.where(inside, 1.0, 0.0).astype(BF)
                right_h[rows, e * RANK:(e + 1) * RANK] = h * picked
                right_u[rows, e * RANK:(e + 1) * RANK] = u * picked
    for copy in column_copies:
        copy.wait()

    def joined(begin, size):
        return jnp.concatenate([left[s, begin:begin + size, :] for s in range(8)], axis=1)

    down = jnp.dot(joined(count * WINDOW, count * DOWN_ROWS), right_u[...], preferred_element_type=F32)
    out_copies = []
    for n in range(count):
        up = jnp.dot(joined(n * WINDOW, WINDOW), right_h[...], preferred_element_type=F32)
        done[n, :WINDOW, :] = up.astype(BF)
        done[n, WINDOW:, :] = down[n * DOWN_ROWS:(n + 1) * DOWN_ROWS].astype(BF)
        out_copies.append(pltpu.make_async_copy(done.at[n], outs[n], sent))
        out_copies[-1].start()
    for copy in out_copies:
        copy.wait()


def partial_call(chunks, *operands):
    count = len(chunks)
    return pl.pallas_call(
        functools.partial(partial_kernel, chunks),
        out_shape=[jax.ShapeDtypeStruct((ROWS, WIDE), BF)] * count,
        in_specs=[SMEM] + [ANY] * 9,
        out_specs=[ANY] * count,
        scratch_shapes=[
            pltpu.VMEM((8, count * ROWS, 128), BF),
            pltpu.VMEM((4, PAIR, PAIR), BF),
            pltpu.VMEM((1024, WIDE), BF),
            pltpu.VMEM((1024, WIDE), BF),
            pltpu.VMEM((count, ROWS, WIDE), BF),
            pltpu.SemaphoreType.DMA,
            pltpu.SemaphoreType.DMA,
            pltpu.SemaphoreType.DMA,
        ],
        compiler_params=pltpu.CompilerParams(vmem_limit_bytes=60 << 20),
        cost_estimate=pl.CostEstimate(flops=2 * count * ROWS * 1024 * WIDE, bytes_accessed=4 << 20, transcendentals=0),
    )(*operands)


def feature_kernel(
    own_ref, a_ref, b_ref, c_ref, bounds_ref, offset_ref, select_ref,
    first_up, first_down, second_up, second_down, out_ref, first_ref, second_ref,
):
    for up, down, space in ((first_up, first_down, first_ref), (second_up, second_down, second_ref)):
        space[:WINDOW, :] = jnp.zeros((WINDOW, RANK), F32)
        space[:UP_ROWS, :] = up[...]
        space[:WINDOW, :] = pltpu.roll(space[:WINDOW, :], offset_ref[0], 0)
        space[WINDOW:, :] = down[...]
    first = 0.9 * first_ref[...]
    second = 0.999 * second_ref[...]
    select = select_ref[...]
    for e in range(EXAMPLES):
        at = pl.ds(e * RANK, RANK)
        length = (bounds_ref[e + 1] - bounds_ref[e]).astype(F32)
        total = (own_ref[:, at].astype(F32) + a_ref[:, at].astype(F32)) + (b_ref[:, at].astype(F32) + c_ref[:, at].astype(F32))
        grad = total / length
        feature = (first + 0.1 * grad) / (jnp.sqrt(second + 0.001 * grad * grad) + 1e-08)
        high = feature.astype(BF)
        low = (feature - high.astype(F32)).astype(BF)
        out_ref[:, at] = jnp.dot(select, high, preferred_element_type=F32) + jnp.dot(
            select, low, preferred_element_type=F32
        )


EVERY = ("ex", "t1", "t0", "py", "co")


def groups(along_x):
    found = []
    for fixed in range(4):
        for c in range(2):
            for zs in ((0, 1), (2, 3)) if along_x else ((0, 3), (1, 2)):
                found.append(
                    [
                        (((x * 4 + z) * 4) + y) * 2 + c
                        for w in range(4)
                        for z in zs
                        for x, y in [(w, fixed) if along_x else (fixed, w)]
                    ]
                )
    return found


def spread_sum(value, along_x):
    copies = jnp.broadcast_to(value[None], (8,) + value.shape)
    arrived = lax.all_to_all(
        copies, EVERY, split_axis=0, concat_axis=0, tiled=True, axis_index_groups=groups(along_x)
    )
    return jnp.sum(arrived, axis=0)


def on_device(
    tokens,
    output_gradient,
    adapter_down_factor,
    adapter_up_factor,
    first_moment_down,
    second_moment_down,
    first_moment_up,
    second_moment_up,
    down_row_seeds,
    up_row_seeds,
    segments,
    bank,
):
    x, y, c = position()
    me = x * 8 + y * 2 + c
    bounds = jnp.sum(
        (segments[None, :] < jnp.arange(EXAMPLES + 1, dtype=jnp.int32)[:, None]).astype(jnp.int32), axis=1
    )

    packed = pl.pallas_call(
        pack_kernel,
        out_shape=[
            jax.ShapeDtypeStruct((4, 4 * ROWS, 128), BF),
            jax.ShapeDtypeStruct((4 * ROWS, 128), BF),
        ]
        + [jax.ShapeDtypeStruct((2, 4 * ROWS, 128), BF)] * 3
        + [jax.ShapeDtypeStruct((128, PAIR), F32)],
        in_specs=[ANY, ANY, ANY, ANY],
        out_specs=[ANY] * 5 + [VMEM],
        scratch_shapes=[
            pltpu.VMEM((LOCAL_UP, 128), BF),
            pltpu.VMEM((128, 2048), BF),
            pltpu.VMEM((2048, 128), BF),
            pltpu.VMEM((LOCAL_UP, 128), BF),
            pltpu.VMEM((2048, 128), BF),
            pltpu.SemaphoreType.DMA((4,)),
            pltpu.SemaphoreType.DMA,
        ],
        compiler_params=pltpu.CompilerParams(vmem_limit_bytes=60 << 20),
        cost_estimate=pl.CostEstimate(flops=2 * 128 * 9440 * 128, bytes_accessed=8 << 20, transcendentals=0),
    )(output_gradient.T, tokens, adapter_down_factor, adapter_up_factor)
    give, own_columns, portion = packed[0], packed[1], packed[5]
    taken = lax.ppermute(give, "co", [(0, 1), (1, 0)])
    whole = portion
    for shift in (1, 2, 3):
        whole = whole + lax.ppermute(portion, ("t1", "t0"), [(i, (i + shift) % 4) for i in range(4)])
    whole = whole.astype(BF)
    sibling = lax.ppermute(whole, "co", [(0, 1), (1, 0)])
    chip_inner = jnp.concatenate([whole, sibling], axis=0)
    filled = pl.pallas_call(
        fill_kernel,
        out_shape=[jax.ShapeDtypeStruct((2, 4 * ROWS, 128), BF)] * 3,
        in_specs=[ANY] * 4,
        out_specs=[ANY] * 3,
        scratch_shapes=[pltpu.SemaphoreType.DMA],
        input_output_aliases={1: 0, 2: 1, 3: 2},
        compiler_params=pltpu.CompilerParams(vmem_limit_bytes=60 << 20),
        cost_estimate=pl.CostEstimate(flops=0, bytes_accessed=2 << 20, transcendentals=0),
    )(taken, *packed[2:5])
    arrived = [send_same(filled[k - 1], k) for k in (1, 2, 3)]
    inner = [chip_inner] + [send_same(chip_inner, k) for k in (1, 2, 3)]

    operands = (bounds, own_columns, taken, *arrived, *inner)
    far, near = partial_call((2, 1), *operands)
    last, own = partial_call((3, 0), *operands)
    arrived = [send_across(near, 1), send_across(far, 2), send_across(last, 3)]

    kept = (first_moment_up, second_moment_up, up_row_seeds, down_row_seeds)
    own, kept = lax.optimization_barrier((own, kept))
    first_moment_up, second_moment_up, up_row_seeds, down_row_seeds = kept
    offset = me * UP_ROWS - window_start(me)
    seeds = jnp.concatenate(
        [
            lax.dynamic_update_slice_in_dim(jnp.full((WINDOW,), -1, jnp.int32), up_row_seeds[0], offset, 0),
            down_row_seeds[0],
        ]
    )
    select = (jnp.arange(BANK, dtype=jnp.int32)[:, None] == seeds[None, :]).astype(BF)
    blocks = pl.pallas_call(
        feature_kernel,
        out_shape=jax.ShapeDtypeStruct((BANK, WIDE), F32),
        in_specs=[VMEM] * 4 + [SMEM] * 2 + [VMEM] * 5,
        out_specs=VMEM,
        scratch_shapes=[pltpu.VMEM((ROWS, RANK), F32), pltpu.VMEM((ROWS, RANK), F32)],
        compiler_params=pltpu.CompilerParams(vmem_limit_bytes=24 << 20),
        cost_estimate=pl.CostEstimate(flops=0, bytes_accessed=3 << 20, transcendentals=0),
    )(
        own, *arrived, bounds, offset.astype(jnp.int32)[None], select,
        first_moment_up[0], first_moment_down[0], second_moment_up[0], second_moment_down[0],
    )

    half = BANK // 2
    kept = lax.dynamic_slice_in_dim(blocks, c * half, half, 0)
    given = lax.dynamic_slice_in_dim(blocks, (1 - c) * half, half, 0)
    total = kept + lax.ppermute(given, "co", [(0, 1), (1, 0)])
    total = spread_sum(total, True)
    total = spread_sum(total, False)
    theirs = lax.ppermute(total, "co", [(0, 1), (1, 0)])
    summed = jnp.concatenate([jnp.where(c == 0, total, theirs), jnp.where(c == 0, theirs, total)], axis=0)
    inverse = 1.0 / math.sqrt((MODEL_WIDTH + HIDDEN_WIDTH) * RANK)
    sketch = jnp.einsum(
        "jer,jrk->ek", summed.reshape(BANK, EXAMPLES, RANK), bank.astype(F32), precision=lax.Precision.HIGHEST
    )
    return sketch * inverse


def solution(mesh):
    rows = ("ex", "py", "co")
    tp = ("t1", "t0")
    split = Mesh(mesh.devices.reshape(4, 2, 2, 4, 2), ("ex", "t1", "t0", "py", "co"))
    return jax.shard_map(
        on_device,
        mesh=split,
        in_specs=(
            P(rows, tp),
            P(rows, tp),
            P(tp, None),
            P(tp, None),
            P(tp, rows, None),
            P(tp, rows, None),
            P(tp, rows, None),
            P(tp, rows, None),
            P(tp, rows),
            P(tp, rows),
            P(),
            P(None, None, ("ex", "t1", "t0", "py", "co")),
        ),
        out_specs=P(None, ("ex", "t1", "t0", "py", "co")),
        check_vma=False,
    )
```

```python
import math

import jax
import jax.numpy as jnp
from jax import lax
from jax.experimental import pallas as pl
from jax.experimental.pallas import tpu as pltpu
from jax.sharding import Mesh, PartitionSpec as P

MODEL_WIDTH = 8192
HIDDEN_WIDTH = 29568
RANK = 128
BANK = 16
EXAMPLES = 4
UP_ROWS = 231
DOWN_ROWS = 64
WINDOW = 256
ROWS = WINDOW + DOWN_ROWS
LOCAL_UP = 7392
PAIR = 2 * RANK
WIDE = EXAMPLES * RANK
BF = jnp.bfloat16
F32 = jnp.float32
VMEM = pl.BlockSpec(memory_space=pltpu.VMEM)
ANY = pl.BlockSpec(memory_space=pl.ANY)
SMEM = pl.BlockSpec(memory_space=pltpu.SMEM)
PLANE = ("ex", "py", "co")


def window_start(owner):
    return jnp.minimum((owner * UP_ROWS) // 16 * 16, LOCAL_UP - WINDOW)


def along(position, shift):
    x, y, c = position
    return (x, (y + shift) % 4, 0) if c == 0 else ((x + shift) % 4, y, 1)


def across(position, shift):
    x, y, c = position
    return ((x + shift) % 4, y, 0) if c == 0 else (x, (y + shift) % 4, 1)


def flat(position):
    return position[0] * 8 + position[1] * 2 + position[2]


def pairs(move):
    everyone = [(x, y, c) for x in range(4) for y in range(4) for c in range(2)]
    return [(flat(p), flat(move(p))) for p in everyone]


def send_same(value, shift):
    return lax.ppermute(value, PLANE, pairs(lambda p: along(p, shift)))


def send_across(value, shift):
    return lax.ppermute(value, PLANE, pairs(lambda p: across(p, shift)))


def position():
    return lax.axis_index("ex"), lax.axis_index("py"), lax.axis_index("co")


def pack_kernel(grad_hbm, tokens_hbm, down_hbm, up_hbm, give_ref, *rest):
    sends, portion_ref = rest[:4], rest[4]
    grad, tokens, down, up, turned, loads, sent = rest[5:]
    arrivals = [
        pltpu.make_async_copy(source, target, loads.at[i])
        for i, (source, target) in enumerate(((tokens_hbm, tokens), (grad_hbm, grad), (down_hbm, down), (up_hbm, up)))
    ]
    for arrival in arrivals:
        arrival.start()
    x, y, c = position()
    outs = [give_ref.at[k] for k in range(4)] + [send.at[0] for send in sends]
    turned_copies, grad_copies = [], []
    for slot in range(8):
        target = 1 - c if slot < 4 else c
        k = slot % 4
        for i in range(4):
            to_x = lax.rem(x + jnp.where(target == 0, i, k), 4)
            to_y = lax.rem(y + jnp.where(target == 0, k, i), 4)
            owner = to_x * 8 + to_y * 2 + target
            start = pl.multiple_of(window_start(owner), 16)
            column = pl.multiple_of(owner * DOWN_ROWS, DOWN_ROWS)
            grad_copies.append(
                pltpu.make_async_copy(
                    grad.at[pl.ds(start, WINDOW)], outs[slot].at[pl.ds(i * WINDOW, WINDOW)], sent
                )
            )
            turned_copies.append(
                pltpu.make_async_copy(
                    turned.at[pl.ds(column, DOWN_ROWS)], outs[slot].at[pl.ds(4 * WINDOW + i * DOWN_ROWS, DOWN_ROWS)], sent
                )
            )
    arrivals[0].wait()
    turned[...] = tokens[...].T
    for copy in turned_copies:
        copy.start()
    arrivals[1].wait()
    for copy in grad_copies:
        copy.start()
    arrivals[2].wait()
    portion_ref[:, :RANK] = jnp.dot(tokens[...], down[...], preferred_element_type=F32)
    arrivals[3].wait()
    product = jnp.zeros((128, RANK), F32)
    for begin in range(0, LOCAL_UP, 1024):
        end = min(begin + 1024, LOCAL_UP)
        product += lax.dot_general(
            grad[begin:end, :], up[begin:end, :], (((0,), (0,)), ((), ())), preferred_element_type=F32
        )
    portion_ref[:, RANK:] = product
    for copy in turned_copies + grad_copies:
        copy.wait()


def fill_kernel(taken_ref, *rest):
    sends, sent = rest[4:8], rest[8]
    copies = [pltpu.make_async_copy(taken_ref.at[k], sends[k].at[1], sent) for k in range(4)]
    for copy in copies:
        copy.start()
    for copy in copies:
        copy.wait()


def partial_kernel(bounds_ref, *rest):
    columns, inner, outs = rest[0:4], rest[4:8], rest[8:12]
    left, low, side, right_h, right_u, done, inner_sem, low_sem, left_sem, sent = rest[12:]
    order = (1, 2, 3, 0)
    inner_copies = [pltpu.make_async_copy(inner[k], side.at[k], inner_sem) for k in range(4)]
    left_copies = {
        j: [
            pltpu.make_async_copy(
                columns[s // 2].at[s % 2, pl.ds(j * WINDOW, WINDOW)], left.at[s, pl.ds(j * WINDOW, WINDOW)], left_sem.at[j]
            )
            for s in range(8)
        ]
        for j in order
    }
    low_copies = [
        pltpu.make_async_copy(columns[s // 2].at[s % 2, pl.ds(4 * WINDOW, 4 * DOWN_ROWS)], low.at[s], low_sem)
        for s in range(8)
    ]
    for copy in inner_copies + low_copies:
        copy.start()
    for j in order:
        for copy in left_copies[j]:
            copy.start()
    x, y, c = position()
    row = lax.broadcasted_iota(jnp.int32, (128, RANK), 0)
    for copy in inner_copies:
        copy.wait()
    for k in range(4):
        chip = jnp.where(c == 0, x * 4 + lax.rem(y - k + 4, 4), lax.rem(x - k + 4, 4) * 4 + y)
        for part in range(2):
            token = row + (chip * PAIR + jnp.where(part == 0, c, 1 - c) * 128)
            rows = pl.ds(k * PAIR + part * 128, 128)
            h = side[k, part * 128:(part + 1) * 128, :RANK]
            u = side[k, part * 128:(part + 1) * 128, RANK:]
            for e in range(EXAMPLES):
                inside = (token >= bounds_ref[e]) & (token < bounds_ref[e + 1])
                picked = jnp.where(inside, 1.0, 0.0).astype(BF)
                right_h[rows, e * RANK:(e + 1) * RANK] = h * picked
                right_u[rows, e * RANK:(e + 1) * RANK] = u * picked
    for copy in low_copies:
        copy.wait()
    joined = jnp.concatenate([low[s] for s in range(8)], axis=1)
    down = jnp.dot(joined, right_u[...], preferred_element_type=F32)
    out_copies = []
    for j in order:
        for copy in left_copies[j]:
            copy.wait()
        joined = jnp.concatenate([left[s, j * WINDOW:(j + 1) * WINDOW, :] for s in range(8)], axis=1)
        up = jnp.dot(joined, right_h[...], preferred_element_type=F32)
        done[j, :WINDOW, :] = up.astype(BF)
        done[j, WINDOW:, :] = down[j * DOWN_ROWS:(j + 1) * DOWN_ROWS].astype(BF)
        out_copies.append(pltpu.make_async_copy(done.at[j], outs[j], sent))
        out_copies[-1].start()
    for copy in out_copies:
        copy.wait()


def feature_kernel(
    own_ref, a_ref, b_ref, c_ref, bounds_ref, offset_ref, select_ref,
    first_up, first_down, second_up, second_down, out_ref, first_ref, second_ref,
):
    for up, down, space in ((first_up, first_down, first_ref), (second_up, second_down, second_ref)):
        space[:WINDOW, :] = jnp.zeros((WINDOW, RANK), F32)
        space[:UP_ROWS, :] = up[...]
        space[:WINDOW, :] = pltpu.roll(space[:WINDOW, :], offset_ref[0], 0)
        space[WINDOW:, :] = down[...]
    first = 0.9 * first_ref[...]
    second = 0.999 * second_ref[...]
    select = select_ref[...]
    for e in range(EXAMPLES):
        at = pl.ds(e * RANK, RANK)
        length = (bounds_ref[e + 1] - bounds_ref[e]).astype(F32)
        total = (own_ref[:, at].astype(F32) + a_ref[:, at].astype(F32)) + (b_ref[:, at].astype(F32) + c_ref[:, at].astype(F32))
        grad = total / length
        feature = (first + 0.1 * grad) / (jnp.sqrt(second + 0.001 * grad * grad) + 1e-08)
        high = feature.astype(BF)
        low = (feature - high.astype(F32)).astype(BF)
        out_ref[:, at] = jnp.dot(select, high, preferred_element_type=F32) + jnp.dot(
            select, low, preferred_element_type=F32
        )


EVERY = ("ex", "t1", "t0", "py", "co")


def groups(along_x):
    found = []
    for fixed in range(4):
        for c in range(2):
            for zs in ((0, 1), (2, 3)) if along_x else ((0, 3), (1, 2)):
                found.append(
                    [
                        (((x * 4 + z) * 4) + y) * 2 + c
                        for w in range(4)
                        for z in zs
                        for x, y in [(w, fixed) if along_x else (fixed, w)]
                    ]
                )
    return found


def spread_sum(value, along_x):
    copies = jnp.broadcast_to(value[None], (8,) + value.shape)
    arrived = lax.all_to_all(
        copies, EVERY, split_axis=0, concat_axis=0, tiled=True, axis_index_groups=groups(along_x)
    )
    return jnp.sum(arrived, axis=0)


def on_device(
    tokens,
    output_gradient,
    adapter_down_factor,
    adapter_up_factor,
    first_moment_down,
    second_moment_down,
    first_moment_up,
    second_moment_up,
    down_row_seeds,
    up_row_seeds,
    segments,
    bank,
):
    x, y, c = position()
    me = x * 8 + y * 2 + c
    bounds = jnp.sum(
        (segments[None, :] < jnp.arange(EXAMPLES + 1, dtype=jnp.int32)[:, None]).astype(jnp.int32), axis=1
    )

    packed = pl.pallas_call(
        pack_kernel,
        out_shape=[jax.ShapeDtypeStruct((4, 4 * ROWS, 128), BF)]
        + [jax.ShapeDtypeStruct((2, 4 * ROWS, 128), BF)] * 4
        + [jax.ShapeDtypeStruct((128, PAIR), F32)],
        in_specs=[ANY, ANY, ANY, ANY],
        out_specs=[ANY] * 5 + [VMEM],
        scratch_shapes=[
            pltpu.VMEM((LOCAL_UP, 128), BF),
            pltpu.VMEM((128, 2048), BF),
            pltpu.VMEM((2048, 128), BF),
            pltpu.VMEM((LOCAL_UP, 128), BF),
            pltpu.VMEM((2048, 128), BF),
            pltpu.SemaphoreType.DMA((4,)),
            pltpu.SemaphoreType.DMA,
        ],
        compiler_params=pltpu.CompilerParams(vmem_limit_bytes=60 << 20),
        cost_estimate=pl.CostEstimate(flops=2 * 128 * 9440 * 128, bytes_accessed=8 << 20, transcendentals=0),
    )(output_gradient.T, tokens, adapter_down_factor, adapter_up_factor)
    give, portion = packed[0], packed[5]
    taken = lax.ppermute(give, "co", [(0, 1), (1, 0)])
    peers = [lax.ppermute(portion, ("t1", "t0"), [(i, (i + shift) % 4) for i in range(4)]) for shift in (1, 2, 3)]
    taken, peers[0] = lax.optimization_barrier((taken, peers[0]))
    whole = ((portion + peers[0]) + (peers[1] + peers[2])).astype(BF)
    sibling = lax.ppermute(whole, "co", [(0, 1), (1, 0)])
    chip_inner = jnp.concatenate([whole, sibling], axis=0)
    filled = pl.pallas_call(
        fill_kernel,
        out_shape=[jax.ShapeDtypeStruct((2, 4 * ROWS, 128), BF)] * 4,
        in_specs=[VMEM] + [ANY] * 4,
        out_specs=[ANY] * 4,
        scratch_shapes=[pltpu.SemaphoreType.DMA],
        input_output_aliases={1: 0, 2: 1, 3: 2, 4: 3},
        compiler_params=pltpu.CompilerParams(vmem_limit_bytes=60 << 20),
        cost_estimate=pl.CostEstimate(flops=0, bytes_accessed=2 << 20, transcendentals=0),
    )(taken, *packed[1:5])
    columns = [filled[0]] + [send_same(filled[k], k) for k in (1, 2, 3)]
    late_inner, columns[1] = lax.optimization_barrier((chip_inner, columns[1]))
    inner = [chip_inner, send_same(chip_inner, 1), send_same(late_inner, 2), send_same(chip_inner, 3)]

    own, *sums = pl.pallas_call(
        partial_kernel,
        out_shape=[jax.ShapeDtypeStruct((ROWS, WIDE), BF)] * 4,
        in_specs=[SMEM] + [ANY] * 8,
        out_specs=[ANY] * 4,
        scratch_shapes=[
            pltpu.VMEM((8, 4 * WINDOW, 128), BF),
            pltpu.VMEM((8, 4 * DOWN_ROWS, 128), BF),
            pltpu.VMEM((4, PAIR, PAIR), BF),
            pltpu.VMEM((1024, WIDE), BF),
            pltpu.VMEM((1024, WIDE), BF),
            pltpu.VMEM((4, ROWS, WIDE), BF),
            pltpu.SemaphoreType.DMA,
            pltpu.SemaphoreType.DMA,
            pltpu.SemaphoreType.DMA((4,)),
            pltpu.SemaphoreType.DMA,
        ],
        compiler_params=pltpu.CompilerParams(vmem_limit_bytes=60 << 20),
        cost_estimate=pl.CostEstimate(flops=2 * 4 * ROWS * 1024 * WIDE, bytes_accessed=6 << 20, transcendentals=0),
    )(bounds, *columns, *inner)
    arrived = [send_across(sums[k - 1], k) for k in (1, 2, 3)]

    kept = (first_moment_up, second_moment_up, up_row_seeds, down_row_seeds)
    own, kept = lax.optimization_barrier((own, kept))
    first_moment_up, second_moment_up, up_row_seeds, down_row_seeds = kept
    offset = me * UP_ROWS - window_start(me)
    seeds = jnp.concatenate(
        [
            lax.dynamic_update_slice_in_dim(jnp.full((WINDOW,), -1, jnp.int32), up_row_seeds[0], offset, 0),
            down_row_seeds[0],
        ]
    )
    select = (jnp.arange(BANK, dtype=jnp.int32)[:, None] == seeds[None, :]).astype(BF)
    blocks = pl.pallas_call(
        feature_kernel,
        out_shape=jax.ShapeDtypeStruct((BANK, WIDE), F32),
        in_specs=[VMEM] * 4 + [SMEM] * 2 + [VMEM] * 5,
        out_specs=VMEM,
        scratch_shapes=[pltpu.VMEM((ROWS, RANK), F32), pltpu.VMEM((ROWS, RANK), F32)],
        compiler_params=pltpu.CompilerParams(vmem_limit_bytes=24 << 20),
        cost_estimate=pl.CostEstimate(flops=0, bytes_accessed=3 << 20, transcendentals=0),
    )(
        own, *arrived, bounds, offset.astype(jnp.int32)[None], select,
        first_moment_up[0], first_moment_down[0], second_moment_up[0], second_moment_down[0],
    )

    half = BANK // 2
    kept = lax.dynamic_slice_in_dim(blocks, c * half, half, 0)
    given = lax.dynamic_slice_in_dim(blocks, (1 - c) * half, half, 0)
    total = kept + lax.ppermute(given, "co", [(0, 1), (1, 0)])
    total = spread_sum(total, True)
    total = spread_sum(total, False)
    theirs = lax.ppermute(total, "co", [(0, 1), (1, 0)])
    summed = jnp.concatenate([jnp.where(c == 0, total, theirs), jnp.where(c == 0, theirs, total)], axis=0)
    inverse = 1.0 / math.sqrt((MODEL_WIDTH + HIDDEN_WIDTH) * RANK)
    sketch = jnp.einsum(
        "jer,jrk->ek", summed.reshape(BANK, EXAMPLES, RANK), bank.astype(F32), precision=lax.Precision.HIGHEST
    )
    return sketch * inverse


def solution(mesh):
    rows = ("ex", "py", "co")
    tp = ("t1", "t0")
    split = Mesh(mesh.devices.reshape(4, 2, 2, 4, 2), ("ex", "t1", "t0", "py", "co"))
    return jax.shard_map(
        on_device,
        mesh=split,
        in_specs=(
            P(rows, tp),
            P(rows, tp),
            P(tp, None),
            P(tp, None),
            P(tp, rows, None),
            P(tp, rows, None),
            P(tp, rows, None),
            P(tp, rows, None),
            P(tp, rows),
            P(tp, rows),
            P(),
            P(None, None, ("ex", "t1", "t0", "py", "co")),
        ),
        out_specs=P(None, ("ex", "t1", "t0", "py", "co")),
        check_vma=False,
    )
```

```python
import functools
import math

import jax
import jax.numpy as jnp
from jax import lax
from jax.experimental import pallas as pl
from jax.experimental.pallas import tpu as pltpu
from jax.sharding import Mesh, PartitionSpec as P

MODEL_WIDTH = 8192
HIDDEN_WIDTH = 29568
RANK = 128
BANK = 16
EXAMPLES = 4
UP_ROWS = 231
DOWN_ROWS = 64
WINDOW = 256
ROWS = WINDOW + DOWN_ROWS
FIRST = 3 * ROWS
LOCAL_UP = 7392
PAIR = 2 * RANK
WIDE = EXAMPLES * RANK
BF = jnp.bfloat16
F32 = jnp.float32
VMEM = pl.BlockSpec(memory_space=pltpu.VMEM)
ANY = pl.BlockSpec(memory_space=pl.ANY)
SMEM = pl.BlockSpec(memory_space=pltpu.SMEM)
PLANE = ("ex", "py", "co")


def window_start(owner):
    return jnp.minimum((owner * UP_ROWS) // 16 * 16, LOCAL_UP - WINDOW)


def along(position, shift):
    x, y, c = position
    return (x, (y + shift) % 4, 0) if c == 0 else ((x + shift) % 4, y, 1)


def across(position, shift):
    x, y, c = position
    return ((x + shift) % 4, y, 0) if c == 0 else (x, (y + shift) % 4, 1)


def flat(position):
    return position[0] * 8 + position[1] * 2 + position[2]


def pairs(move):
    everyone = [(x, y, c) for x in range(4) for y in range(4) for c in range(2)]
    return [(flat(p), flat(move(p))) for p in everyone]


def send_same(value, shift):
    return lax.ppermute(value, PLANE, pairs(lambda p: along(p, shift)))


def send_across(value, shift):
    return lax.ppermute(value, PLANE, pairs(lambda p: across(p, shift)))


def position():
    return lax.axis_index("ex"), lax.axis_index("py"), lax.axis_index("co")


def tie(value, arrived):
    return lax.optimization_barrier((value, arrived))


def pack_kernel(grad_hbm, tokens_hbm, down_hbm, up_hbm, give_ref, *rest):
    firsts, seconds, portion_ref = rest[:4], rest[4:8], rest[8]
    grad, tokens, down, up, turned, loads, sent = rest[9:]
    arrivals = [
        pltpu.make_async_copy(source, target, loads.at[i])
        for i, (source, target) in enumerate(((tokens_hbm, tokens), (grad_hbm, grad), (down_hbm, down), (up_hbm, up)))
    ]
    for arrival in arrivals:
        arrival.start()
    x, y, c = position()
    turned_copies, grad_copies = [], []
    for slot in range(8):
        target = 1 - c if slot < 4 else c
        k = slot % 4
        for i in range(4):
            to_x = lax.rem(x + jnp.where(target == 0, i, k), 4)
            to_y = lax.rem(y + jnp.where(target == 0, k, i), 4)
            owner = to_x * 8 + to_y * 2 + target
            start = pl.multiple_of(window_start(owner), 16)
            column = pl.multiple_of(owner * DOWN_ROWS, DOWN_ROWS)
            if i:
                out = give_ref.at[k] if slot < 4 else firsts[k].at[0]
                window_at, down_at = (i - 1) * WINDOW, 3 * WINDOW + (i - 1) * DOWN_ROWS
            else:
                out = give_ref.at[k] if slot < 4 else seconds[k].at[0]
                window_at = FIRST if slot < 4 else 0
                down_at = window_at + WINDOW
            grad_copies.append(
                pltpu.make_async_copy(grad.at[pl.ds(start, WINDOW)], out.at[pl.ds(window_at, WINDOW)], sent)
            )
            turned_copies.append(
                pltpu.make_async_copy(turned.at[pl.ds(column, DOWN_ROWS)], out.at[pl.ds(down_at, DOWN_ROWS)], sent)
            )
    arrivals[0].wait()
    turned[...] = tokens[...].T
    for copy in turned_copies:
        copy.start()
    arrivals[1].wait()
    for copy in grad_copies:
        copy.start()
    arrivals[2].wait()
    portion_ref[:, :RANK] = jnp.dot(tokens[...], down[...], preferred_element_type=F32)
    arrivals[3].wait()
    product = jnp.zeros((128, RANK), F32)
    for begin in range(0, LOCAL_UP, 1024):
        end = min(begin + 1024, LOCAL_UP)
        product += lax.dot_general(
            grad[begin:end, :], up[begin:end, :], (((0,), (0,)), ((), ())), preferred_element_type=F32
        )
    portion_ref[:, RANK:] = product
    for copy in turned_copies + grad_copies:
        copy.wait()


def fill_kernel(taken_ref, *rest):
    firsts, seconds, (held, load, sent) = rest[8:12], rest[12:16], rest[16:]
    order = (1, 3, 2, 0)
    loads = {k: pltpu.make_async_copy(taken_ref.at[k], held.at[k], load.at[k]) for k in order}
    for k in order:
        loads[k].start()
    copies = []
    for k in order:
        loads[k].wait()
        copies.append(pltpu.make_async_copy(held.at[k, pl.ds(0, FIRST)], firsts[k].at[1], sent))
        copies.append(pltpu.make_async_copy(held.at[k, pl.ds(FIRST, ROWS)], seconds[k].at[1], sent))
        copies[-2].start()
        copies[-1].start()
    for copy in copies:
        copy.wait()


def partial_kernel(count, bounds_ref, *rest):
    columns, inner, outs = rest[0:4], rest[4:8], rest[8:8 + count]
    left, side, right_h, right_u, done, inner_sem, columns_sem, sent = rest[8 + count:]
    inner_copies = [pltpu.make_async_copy(inner[k], side.at[k], inner_sem) for k in range(4)]
    column_copies = [pltpu.make_async_copy(columns[k], left.at[k], columns_sem) for k in range(4)]
    for copy in inner_copies + column_copies:
        copy.start()
    x, y, c = position()
    row = lax.broadcasted_iota(jnp.int32, (128, RANK), 0)
    for copy in inner_copies:
        copy.wait()
    for k in range(4):
        chip = jnp.where(c == 0, x * 4 + lax.rem(y - k + 4, 4), lax.rem(x - k + 4, 4) * 4 + y)
        for part in range(2):
            token = row + (chip * PAIR + jnp.where(part == 0, c, 1 - c) * 128)
            rows = pl.ds(k * PAIR + part * 128, 128)
            h = side[k, part * 128:(part + 1) * 128, :RANK]
            u = side[k, part * 128:(part + 1) * 128, RANK:]
            for e in range(EXAMPLES):
                inside = (token >= bounds_ref[e]) & (token < bounds_ref[e + 1])
                picked = jnp.where(inside, 1.0, 0.0).astype(BF)
                right_h[rows, e * RANK:(e + 1) * RANK] = h * picked
                right_u[rows, e * RANK:(e + 1) * RANK] = u * picked
    for copy in column_copies:
        copy.wait()

    def joined(begin, size):
        return jnp.concatenate([left[s // 2, s % 2, begin:begin + size, :] for s in range(8)], axis=1)

    down = jnp.dot(joined(count * WINDOW, count * DOWN_ROWS), right_u[...], preferred_element_type=F32)
    out_copies = []
    for n in range(count):
        up = jnp.dot(joined(n * WINDOW, WINDOW), right_h[...], preferred_element_type=F32)
        done[n, :WINDOW, :] = up.astype(BF)
        done[n, WINDOW:, :] = down[n * DOWN_ROWS:(n + 1) * DOWN_ROWS].astype(BF)
        out_copies.append(pltpu.make_async_copy(done.at[n], outs[n], sent))
        out_copies[-1].start()
    for copy in out_copies:
        copy.wait()


def partial_call(count, bounds, columns, inner):
    return pl.pallas_call(
        functools.partial(partial_kernel, count),
        out_shape=[jax.ShapeDtypeStruct((ROWS, WIDE), BF)] * count,
        in_specs=[SMEM] + [ANY] * 8,
        out_specs=[ANY] * count,
        scratch_shapes=[
            pltpu.VMEM((4, 2, count * ROWS, 128), BF),
            pltpu.VMEM((4, PAIR, PAIR), BF),
            pltpu.VMEM((1024, WIDE), BF),
            pltpu.VMEM((1024, WIDE), BF),
            pltpu.VMEM((count, ROWS, WIDE), BF),
            pltpu.SemaphoreType.DMA,
            pltpu.SemaphoreType.DMA,
            pltpu.SemaphoreType.DMA,
        ],
        compiler_params=pltpu.CompilerParams(vmem_limit_bytes=60 << 20),
        cost_estimate=pl.CostEstimate(flops=2 * count * ROWS * 1024 * WIDE, bytes_accessed=6 << 20, transcendentals=0),
    )(bounds, *columns, *inner)


def feature_kernel(
    own_ref, a_ref, b_ref, c_ref, bounds_ref, offset_ref, select_ref,
    first_up, first_down, second_up, second_down, out_ref, first_ref, second_ref,
):
    for up, down, space in ((first_up, first_down, first_ref), (second_up, second_down, second_ref)):
        space[:WINDOW, :] = jnp.zeros((WINDOW, RANK), F32)
        space[:UP_ROWS, :] = up[...]
        space[:WINDOW, :] = pltpu.roll(space[:WINDOW, :], offset_ref[0], 0)
        space[WINDOW:, :] = down[...]
    first = 0.9 * first_ref[...]
    second = 0.999 * second_ref[...]
    select = select_ref[...]
    for e in range(EXAMPLES):
        at = pl.ds(e * RANK, RANK)
        length = (bounds_ref[e + 1] - bounds_ref[e]).astype(F32)
        total = (own_ref[:, at].astype(F32) + a_ref[:, at].astype(F32)) + (b_ref[:, at].astype(F32) + c_ref[:, at].astype(F32))
        grad = total / length
        feature = (first + 0.1 * grad) / (jnp.sqrt(second + 0.001 * grad * grad) + 1e-08)
        high = feature.astype(BF)
        low = (feature - high.astype(F32)).astype(BF)
        out_ref[:, at] = jnp.dot(select, high, preferred_element_type=F32) + jnp.dot(
            select, low, preferred_element_type=F32
        )


EVERY = ("ex", "t1", "t0", "py", "co")


def groups(along_x):
    found = []
    for fixed in range(4):
        for c in range(2):
            for zs in ((0, 1), (2, 3)) if along_x else ((0, 3), (1, 2)):
                found.append(
                    [
                        (((x * 4 + z) * 4) + y) * 2 + c
                        for w in range(4)
                        for z in zs
                        for x, y in [(w, fixed) if along_x else (fixed, w)]
                    ]
                )
    return found


def spread_sum(value, along_x):
    copies = jnp.broadcast_to(value[None], (8,) + value.shape)
    arrived = lax.all_to_all(
        copies, EVERY, split_axis=0, concat_axis=0, tiled=True, axis_index_groups=groups(along_x)
    )
    return jnp.sum(arrived, axis=0)


def on_device(
    tokens,
    output_gradient,
    adapter_down_factor,
    adapter_up_factor,
    first_moment_down,
    second_moment_down,
    first_moment_up,
    second_moment_up,
    down_row_seeds,
    up_row_seeds,
    segments,
    bank,
):
    x, y, c = position()
    me = x * 8 + y * 2 + c
    bounds = jnp.sum(
        (segments[None, :] < jnp.arange(EXAMPLES + 1, dtype=jnp.int32)[:, None]).astype(jnp.int32), axis=1
    )

    shapes = [jax.ShapeDtypeStruct((2, FIRST, 128), BF)] * 4 + [jax.ShapeDtypeStruct((2, ROWS, 128), BF)] * 4
    give, *packed, portion = pl.pallas_call(
        pack_kernel,
        out_shape=[jax.ShapeDtypeStruct((4, 4 * ROWS, 128), BF)] + shapes + [jax.ShapeDtypeStruct((128, PAIR), F32)],
        in_specs=[ANY] * 4,
        out_specs=[ANY] * 9 + [VMEM],
        scratch_shapes=[
            pltpu.VMEM((LOCAL_UP, 128), BF),
            pltpu.VMEM((128, 2048), BF),
            pltpu.VMEM((2048, 128), BF),
            pltpu.VMEM((LOCAL_UP, 128), BF),
            pltpu.VMEM((2048, 128), BF),
            pltpu.SemaphoreType.DMA((4,)),
            pltpu.SemaphoreType.DMA,
        ],
        compiler_params=pltpu.CompilerParams(vmem_limit_bytes=60 << 20),
        cost_estimate=pl.CostEstimate(flops=2 * 128 * 9440 * 128, bytes_accessed=8 << 20, transcendentals=0),
    )(output_gradient.T, tokens, adapter_down_factor, adapter_up_factor)
    taken = lax.ppermute(give, "co", [(0, 1), (1, 0)])
    filled = pl.pallas_call(
        fill_kernel,
        out_shape=shapes,
        in_specs=[ANY] * 9,
        out_specs=[ANY] * 8,
        scratch_shapes=[
            pltpu.VMEM((4, 4 * ROWS, 128), BF),
            pltpu.SemaphoreType.DMA((4,)),
            pltpu.SemaphoreType.DMA,
        ],
        input_output_aliases={k + 1: k for k in range(8)},
        compiler_params=pltpu.CompilerParams(vmem_limit_bytes=60 << 20),
        cost_estimate=pl.CostEstimate(flops=0, bytes_accessed=2 << 20, transcendentals=0),
    )(taken, *packed)
    first, second = list(filled[:4]), list(filled[4:])
    peers = [lax.ppermute(portion, ("t1", "t0"), [(i, (i + shift) % 4) for i in range(4)]) for shift in (1, 2, 3)]
    first[2], peers[0] = tie(first[2], peers[0])
    first[1:] = [send_same(first[k], k) for k in (1, 2, 3)]
    whole = ((portion + peers[0]) + (peers[1] + peers[2])).astype(BF)
    sibling = lax.ppermute(whole, "co", [(0, 1), (1, 0)])
    chip_inner = jnp.concatenate([whole, sibling], axis=0)
    inner = [chip_inner, send_same(chip_inner, 1), None, send_same(chip_inner, 3)]
    late, first[1] = tie(chip_inner, first[1])
    inner[2] = send_same(late, 2)
    second[1], first[3] = tie(second[1], first[3])
    second[1] = send_same(second[1], 1)
    second[3], first[2] = tie(second[3], first[2])
    second[3] = send_same(second[3], 3)
    second[2], inner[1] = tie(second[2], inner[1])
    second[2] = send_same(second[2], 2)

    sums = partial_call(3, bounds, first, inner)
    arrived = [send_across(sums[k - 1], k) for k in (1, 2, 3)]
    bounds_late, sums = tie(bounds, sums)
    (own,) = partial_call(1, bounds_late, second, inner)

    kept = (first_moment_up, second_moment_up, up_row_seeds, down_row_seeds)
    own, kept = lax.optimization_barrier((own, kept))
    first_moment_up, second_moment_up, up_row_seeds, down_row_seeds = kept
    offset = me * UP_ROWS - window_start(me)
    seeds = jnp.concatenate(
        [
            lax.dynamic_update_slice_in_dim(jnp.full((WINDOW,), -1, jnp.int32), up_row_seeds[0], offset, 0),
            down_row_seeds[0],
        ]
    )
    select = (jnp.arange(BANK, dtype=jnp.int32)[:, None] == seeds[None, :]).astype(BF)
    blocks = pl.pallas_call(
        feature_kernel,
        out_shape=jax.ShapeDtypeStruct((BANK, WIDE), F32),
        in_specs=[VMEM] * 4 + [SMEM] * 2 + [VMEM] * 5,
        out_specs=VMEM,
        scratch_shapes=[pltpu.VMEM((ROWS, RANK), F32), pltpu.VMEM((ROWS, RANK), F32)],
        compiler_params=pltpu.CompilerParams(vmem_limit_bytes=24 << 20),
        cost_estimate=pl.CostEstimate(flops=0, bytes_accessed=3 << 20, transcendentals=0),
    )(
        own, *arrived, bounds, offset.astype(jnp.int32)[None], select,
        first_moment_up[0], first_moment_down[0], second_moment_up[0], second_moment_down[0],
    )

    half = BANK // 2
    kept = lax.dynamic_slice_in_dim(blocks, c * half, half, 0)
    given = lax.dynamic_slice_in_dim(blocks, (1 - c) * half, half, 0)
    total = kept + lax.ppermute(given, "co", [(0, 1), (1, 0)])
    total = spread_sum(total, True)
    total = spread_sum(total, False)
    theirs = lax.ppermute(total, "co", [(0, 1), (1, 0)])
    summed = jnp.concatenate([jnp.where(c == 0, total, theirs), jnp.where(c == 0, theirs, total)], axis=0)
    inverse = 1.0 / math.sqrt((MODEL_WIDTH + HIDDEN_WIDTH) * RANK)
    sketch = jnp.einsum(
        "jer,jrk->ek", summed.reshape(BANK, EXAMPLES, RANK), bank.astype(F32), precision=lax.Precision.HIGHEST
    )
    return sketch * inverse


def solution(mesh):
    rows = ("ex", "py", "co")
    tp = ("t1", "t0")
    split = Mesh(mesh.devices.reshape(4, 2, 2, 4, 2), ("ex", "t1", "t0", "py", "co"))
    return jax.shard_map(
        on_device,
        mesh=split,
        in_specs=(
            P(rows, tp),
            P(rows, tp),
            P(tp, None),
            P(tp, None),
            P(tp, rows, None),
            P(tp, rows, None),
            P(tp, rows, None),
            P(tp, rows, None),
            P(tp, rows),
            P(tp, rows),
            P(),
            P(None, None, ("ex", "t1", "t0", "py", "co")),
        ),
        out_specs=P(None, ("ex", "t1", "t0", "py", "co")),
        check_vma=False,
    )
```

```python
import functools
import math

import jax
import jax.numpy as jnp
from jax import lax
from jax.experimental import pallas as pl
from jax.experimental.pallas import tpu as pltpu
from jax.sharding import Mesh, PartitionSpec as P

MODEL_WIDTH = 8192
HIDDEN_WIDTH = 29568
RANK = 128
BANK = 16
EXAMPLES = 4
UP_ROWS = 231
DOWN_ROWS = 64
WINDOW = 256
ROWS = WINDOW + DOWN_ROWS
FIRST = 3 * ROWS
PARTED = (1, 3)
LOCAL_UP = 7392
PAIR = 2 * RANK
WIDE = EXAMPLES * RANK
BF = jnp.bfloat16
F32 = jnp.float32
VMEM = pl.BlockSpec(memory_space=pltpu.VMEM)
ANY = pl.BlockSpec(memory_space=pl.ANY)
SMEM = pl.BlockSpec(memory_space=pltpu.SMEM)
PLANE = ("ex", "py", "co")


def window_start(owner):
    return jnp.minimum((owner * UP_ROWS) // 16 * 16, LOCAL_UP - WINDOW)


def along(position, shift):
    x, y, c = position
    return (x, (y + shift) % 4, 0) if c == 0 else ((x + shift) % 4, y, 1)


def across(position, shift):
    x, y, c = position
    return ((x + shift) % 4, y, 0) if c == 0 else (x, (y + shift) % 4, 1)


def flat(position):
    return position[0] * 8 + position[1] * 2 + position[2]


def pairs(move):
    everyone = [(x, y, c) for x in range(4) for y in range(4) for c in range(2)]
    return [(flat(p), flat(move(p))) for p in everyone]


def send_same(value, shift):
    return lax.ppermute(value, PLANE, pairs(lambda p: along(p, shift)))


def send_across(value, shift):
    return lax.ppermute(value, PLANE, pairs(lambda p: across(p, shift)))


def position():
    return lax.axis_index("ex"), lax.axis_index("py"), lax.axis_index("co")


def tie(value, arrived):
    return lax.optimization_barrier((value, arrived))


def pack_kernel(grad_hbm, tokens_hbm, down_hbm, up_hbm, give_ref, *rest):
    buffers, portion_ref = rest[:6], rest[6]
    grad, tokens, down, up, turned, loads, sent = rest[7:]
    arrivals = [
        pltpu.make_async_copy(source, target, loads.at[i])
        for i, (source, target) in enumerate(((tokens_hbm, tokens), (grad_hbm, grad), (down_hbm, down), (up_hbm, up)))
    ]
    for arrival in arrivals:
        arrival.start()
    x, y, c = position()
    turned_copies, grad_copies = [], []
    for slot in range(8):
        target = 1 - c if slot < 4 else c
        k = slot % 4
        for i in range(4):
            to_x = lax.rem(x + jnp.where(target == 0, i, k), 4)
            to_y = lax.rem(y + jnp.where(target == 0, k, i), 4)
            owner = to_x * 8 + to_y * 2 + target
            start = pl.multiple_of(window_start(owner), 16)
            column = pl.multiple_of(owner * DOWN_ROWS, DOWN_ROWS)
            out = give_ref.at[k] if slot < 4 else buffers[k].at[0]
            window_at, down_at = ((i - 1) * WINDOW, 3 * WINDOW + (i - 1) * DOWN_ROWS) if i else (FIRST, FIRST + WINDOW)
            if slot >= 4 and i == 0 and k in PARTED:
                out, window_at, down_at = buffers[4 + PARTED.index(k)].at[0], 0, WINDOW
            grad_copies.append(
                pltpu.make_async_copy(grad.at[pl.ds(start, WINDOW)], out.at[pl.ds(window_at, WINDOW)], sent)
            )
            turned_copies.append(
                pltpu.make_async_copy(turned.at[pl.ds(column, DOWN_ROWS)], out.at[pl.ds(down_at, DOWN_ROWS)], sent)
            )
    arrivals[0].wait()
    turned[...] = tokens[...].T
    for copy in turned_copies:
        copy.start()
    arrivals[1].wait()
    for copy in grad_copies:
        copy.start()
    arrivals[2].wait()
    portion_ref[:, :RANK] = jnp.dot(tokens[...], down[...], preferred_element_type=F32)
    arrivals[3].wait()
    product = jnp.zeros((128, RANK), F32)
    for begin in range(0, LOCAL_UP, 1024):
        end = min(begin + 1024, LOCAL_UP)
        product += lax.dot_general(
            grad[begin:end, :], up[begin:end, :], (((0,), (0,)), ((), ())), preferred_element_type=F32
        )
    portion_ref[:, RANK:] = product
    for copy in turned_copies + grad_copies:
        copy.wait()


def fill_kernel(taken_ref, *rest):
    buffers, (held, load, sent) = rest[6:12], rest[12:]
    order = (2, 1, 3, 0)
    loads = {k: pltpu.make_async_copy(taken_ref.at[k], held.at[k], load.at[k]) for k in order}
    for k in order:
        loads[k].start()
    copies = []
    for k in order:
        loads[k].wait()
        if k in PARTED:
            copies.append(pltpu.make_async_copy(held.at[k, pl.ds(0, FIRST)], buffers[k].at[1], sent))
            copies[-1].start()
            second = buffers[4 + PARTED.index(k)]
            copies.append(pltpu.make_async_copy(held.at[k, pl.ds(FIRST, ROWS)], second.at[1], sent))
        else:
            copies.append(pltpu.make_async_copy(held.at[k], buffers[k].at[1], sent))
        copies[-1].start()
    for copy in copies:
        copy.wait()


def partial_kernel(count, segments_hbm, *rest):
    columns, inner, outs = rest[0:4], rest[4:8], rest[8:8 + count]
    left, side, segments, right_h, right_u, total, done, segments_sem, inner_sem, columns_sem, sent = rest[8 + count:]
    segments_copy = pltpu.make_async_copy(segments_hbm, segments, segments_sem)
    segments_copy.start()
    inner_copies = [pltpu.make_async_copy(inner[k], side.at[k], inner_sem) for k in range(4)]
    column_copies = []
    for k in range(4):
        begin = FIRST if count == 1 and k not in PARTED else 0
        for part in range(2):
            source = columns[k].at[part, pl.ds(begin, count * ROWS)]
            column_copies.append(pltpu.make_async_copy(source, left.at[k, part], columns_sem.at[k]))
    for copy in inner_copies + column_copies:
        copy.start()
    x, y, c = position()
    segments_copy.wait()
    masks = []
    for k in range(4):
        chip = jnp.where(c == 0, x * 4 + lax.rem(y - k + 4, 4), lax.rem(x - k + 4, 4) * 4 + y)
        for part in range(2):
            labels = segments[pl.ds(2 * chip + jnp.where(part == 0, c, 1 - c), 1), :]
            labels = jnp.broadcast_to(labels.astype(F32), (128, RANK)).T
            masks.append([jnp.where(labels == e, 1.0, 0.0).astype(BF) for e in range(EXAMPLES)])
    for copy in inner_copies:
        copy.wait()
    for s in range(8):
        rows = pl.ds(s * 128, 128)
        h = side[s // 2, s % 2 * 128:(s % 2 + 1) * 128, :RANK]
        u = side[s // 2, s % 2 * 128:(s % 2 + 1) * 128, RANK:]
        for e in range(EXAMPLES):
            right_h[rows, e * RANK:(e + 1) * RANK] = h * masks[s][e]
            right_u[rows, e * RANK:(e + 1) * RANK] = u * masks[s][e]
    split = count * WINDOW
    for k in range(4):
        for copy in column_copies[2 * k:2 * k + 2]:
            copy.wait()
        both = pl.ds(k * PAIR, PAIR)
        for n in range(count + 1):
            rows = slice(n * WINDOW, (n + 1) * WINDOW) if n < count else slice(split, count * ROWS)
            joined = jnp.concatenate([left[k, 0, rows, :], left[k, 1, rows, :]], axis=1)
            right = (right_h if n < count else right_u)[both, :]
            product = jnp.dot(joined, right, preferred_element_type=F32)
            total[rows, :] = product if k == 0 else total[rows, :] + product
    out_copies = []
    for n in range(count):
        done[n, :WINDOW, :] = total[n * WINDOW:(n + 1) * WINDOW, :].astype(BF)
        done[n, WINDOW:, :] = total[split + n * DOWN_ROWS:split + (n + 1) * DOWN_ROWS, :].astype(BF)
        out_copies.append(pltpu.make_async_copy(done.at[n], outs[n], sent))
        out_copies[-1].start()
    for copy in out_copies:
        copy.wait()


def partial_call(count, labels, columns, inner):
    return pl.pallas_call(
        functools.partial(partial_kernel, count),
        out_shape=[jax.ShapeDtypeStruct((ROWS, WIDE), BF)] * count,
        in_specs=[ANY] * 9,
        out_specs=[ANY] * count,
        scratch_shapes=[
            pltpu.VMEM((4, 2, count * ROWS, 128), BF),
            pltpu.VMEM((4, PAIR, PAIR), BF),
            pltpu.VMEM((32, 128), jnp.int32),
            pltpu.VMEM((1024, WIDE), BF),
            pltpu.VMEM((1024, WIDE), BF),
            pltpu.VMEM((count * ROWS, WIDE), F32),
            pltpu.VMEM((count, ROWS, WIDE), BF),
            pltpu.SemaphoreType.DMA,
            pltpu.SemaphoreType.DMA,
            pltpu.SemaphoreType.DMA((4,)),
            pltpu.SemaphoreType.DMA,
        ],
        compiler_params=pltpu.CompilerParams(vmem_limit_bytes=60 << 20),
        cost_estimate=pl.CostEstimate(flops=2 * count * ROWS * 1024 * WIDE, bytes_accessed=6 << 20, transcendentals=0),
    )(labels, *columns, *inner)


def feature_kernel(
    own_ref, a_ref, b_ref, c_ref, bounds_ref, offset_ref, select_ref,
    first_up, first_down, second_up, second_down, out_ref, first_ref, second_ref,
):
    for up, down, space in ((first_up, first_down, first_ref), (second_up, second_down, second_ref)):
        space[:WINDOW, :] = jnp.zeros((WINDOW, RANK), F32)
        space[:UP_ROWS, :] = up[...]
        space[:WINDOW, :] = pltpu.roll(space[:WINDOW, :], offset_ref[0], 0)
        space[WINDOW:, :] = down[...]
    first = 0.9 * first_ref[...]
    second = 0.999 * second_ref[...]
    select = select_ref[...]
    for e in range(EXAMPLES):
        at = pl.ds(e * RANK, RANK)
        length = (bounds_ref[e + 1] - bounds_ref[e]).astype(F32)
        total = (own_ref[:, at].astype(F32) + a_ref[:, at].astype(F32)) + (b_ref[:, at].astype(F32) + c_ref[:, at].astype(F32))
        grad = total / length
        feature = (first + 0.1 * grad) / (jnp.sqrt(second + 0.001 * grad * grad) + 1e-08)
        high = feature.astype(BF)
        low = (feature - high.astype(F32)).astype(BF)
        out_ref[:, at] = jnp.dot(select, high, preferred_element_type=F32) + jnp.dot(
            select, low, preferred_element_type=F32
        )


EVERY = ("ex", "t1", "t0", "py", "co")


def groups(along_x):
    found = []
    for fixed in range(4):
        for c in range(2):
            for zs in ((0, 1), (2, 3)) if along_x else ((0, 3), (1, 2)):
                found.append(
                    [
                        (((x * 4 + z) * 4) + y) * 2 + c
                        for w in range(4)
                        for z in zs
                        for x, y in [(w, fixed) if along_x else (fixed, w)]
                    ]
                )
    return found


def spread_sum(value, along_x):
    copies = jnp.broadcast_to(value[None], (8,) + value.shape)
    arrived = lax.all_to_all(
        copies, EVERY, split_axis=0, concat_axis=0, tiled=True, axis_index_groups=groups(along_x)
    )
    return jnp.sum(arrived, axis=0)


def on_device(
    tokens,
    output_gradient,
    adapter_down_factor,
    adapter_up_factor,
    first_moment_down,
    second_moment_down,
    first_moment_up,
    second_moment_up,
    down_row_seeds,
    up_row_seeds,
    segments,
    bank,
):
    x, y, c = position()
    me = x * 8 + y * 2 + c
    shapes = [jax.ShapeDtypeStruct((2, rows, 128), BF) for rows in (4 * ROWS, FIRST, 4 * ROWS, FIRST, ROWS, ROWS)]
    give, *packed, portion = pl.pallas_call(
        pack_kernel,
        out_shape=[jax.ShapeDtypeStruct((4, 4 * ROWS, 128), BF)] + shapes + [jax.ShapeDtypeStruct((128, PAIR), F32)],
        in_specs=[ANY] * 4,
        out_specs=[ANY] * 7 + [VMEM],
        scratch_shapes=[
            pltpu.VMEM((LOCAL_UP, 128), BF),
            pltpu.VMEM((128, 2048), BF),
            pltpu.VMEM((2048, 128), BF),
            pltpu.VMEM((LOCAL_UP, 128), BF),
            pltpu.VMEM((2048, 128), BF),
            pltpu.SemaphoreType.DMA((4,)),
            pltpu.SemaphoreType.DMA,
        ],
        compiler_params=pltpu.CompilerParams(vmem_limit_bytes=60 << 20),
        cost_estimate=pl.CostEstimate(flops=2 * 128 * 9440 * 128, bytes_accessed=8 << 20, transcendentals=0),
    )(output_gradient.T, tokens, adapter_down_factor, adapter_up_factor)
    taken = lax.ppermute(give, "co", [(0, 1), (1, 0)])
    filled = pl.pallas_call(
        fill_kernel,
        out_shape=shapes,
        in_specs=[ANY] * 7,
        out_specs=[ANY] * 6,
        scratch_shapes=[
            pltpu.VMEM((4, 4 * ROWS, 128), BF),
            pltpu.SemaphoreType.DMA((4,)),
            pltpu.SemaphoreType.DMA,
        ],
        input_output_aliases={k + 1: k for k in range(6)},
        compiler_params=pltpu.CompilerParams(vmem_limit_bytes=60 << 20),
        cost_estimate=pl.CostEstimate(flops=0, bytes_accessed=2 << 20, transcendentals=0),
    )(taken, *packed)
    first, second = list(filled[:4]), dict(zip(PARTED, filled[4:]))
    pair = portion + lax.ppermute(portion, ("t1", "t0"), [(0, 1), (1, 0), (2, 3), (3, 2)])
    whole = pair + lax.ppermute(pair, ("t1", "t0"), [(0, 3), (3, 0), (1, 2), (2, 1)])
    for k in (2, 1, 3):
        first[k] = send_same(first[k], k)
    whole = whole.astype(BF)
    sibling = lax.ppermute(whole, "co", [(0, 1), (1, 0)])
    chip_inner = jnp.concatenate([whole, sibling], axis=0)
    inner = [chip_inner, None, None, None]
    for k in (2, 1):
        inner[k] = send_same(chip_inner, k)
    late, first[2] = tie(chip_inner, first[2])
    inner[3] = send_same(late, 3)
    second[1], first[1] = tie(second[1], first[1])
    second[3], first[3] = tie(second[3], first[3])
    for k in PARTED:
        second[k] = send_same(second[k], k)

    labels = segments.reshape(32, 128)
    sums = partial_call(3, labels, first, inner)
    arrived = [send_across(sums[k - 1], k) for k in (2, 1, 3)]
    kept = (labels, segments, first_moment_up, second_moment_up, up_row_seeds, down_row_seeds)
    kept, sums = tie(kept, sums)
    labels, segments, first_moment_up, second_moment_up, up_row_seeds, down_row_seeds = kept
    (own,) = partial_call(1, labels, [first[0], second[1], first[2], second[3]], inner)
    own = own.astype(F32)

    bounds = jnp.sum(
        (segments[None, :] < jnp.arange(EXAMPLES + 1, dtype=jnp.int32)[:, None]).astype(jnp.int32), axis=1
    )

    offset = me * UP_ROWS - window_start(me)
    seeds = jnp.concatenate(
        [
            lax.dynamic_update_slice_in_dim(jnp.full((WINDOW,), -1, jnp.int32), up_row_seeds[0], offset, 0),
            down_row_seeds[0],
        ]
    )
    select = (jnp.arange(BANK, dtype=jnp.int32)[:, None] == seeds[None, :]).astype(BF)
    blocks = pl.pallas_call(
        feature_kernel,
        out_shape=jax.ShapeDtypeStruct((BANK, WIDE), F32),
        in_specs=[VMEM] * 4 + [SMEM] * 2 + [VMEM] * 5,
        out_specs=VMEM,
        scratch_shapes=[pltpu.VMEM((ROWS, RANK), F32), pltpu.VMEM((ROWS, RANK), F32)],
        compiler_params=pltpu.CompilerParams(vmem_limit_bytes=24 << 20),
        cost_estimate=pl.CostEstimate(flops=0, bytes_accessed=3 << 20, transcendentals=0),
    )(
        own, *arrived, bounds, offset.astype(jnp.int32)[None], select,
        first_moment_up[0], first_moment_down[0], second_moment_up[0], second_moment_down[0],
    )

    half = BANK // 2
    kept = lax.dynamic_slice_in_dim(blocks, c * half, half, 0)
    given = lax.dynamic_slice_in_dim(blocks, (1 - c) * half, half, 0)
    total = kept + lax.ppermute(given, "co", [(0, 1), (1, 0)])
    total = spread_sum(total, True)
    total = spread_sum(total, False)
    theirs = lax.ppermute(total, "co", [(0, 1), (1, 0)])
    summed = jnp.concatenate([jnp.where(c == 0, total, theirs), jnp.where(c == 0, theirs, total)], axis=0)
    inverse = 1.0 / math.sqrt((MODEL_WIDTH + HIDDEN_WIDTH) * RANK)
    sketch = jnp.einsum(
        "jer,jrk->ek", summed.reshape(BANK, EXAMPLES, RANK), bank.astype(F32), precision=lax.Precision.HIGHEST
    )
    return sketch * inverse


def solution(mesh):
    rows = ("ex", "py", "co")
    tp = ("t1", "t0")
    split = Mesh(mesh.devices.reshape(4, 2, 2, 4, 2), ("ex", "t1", "t0", "py", "co"))
    return jax.shard_map(
        on_device,
        mesh=split,
        in_specs=(
            P(rows, tp),
            P(rows, tp),
            P(tp, None),
            P(tp, None),
            P(tp, rows, None),
            P(tp, rows, None),
            P(tp, rows, None),
            P(tp, rows, None),
            P(tp, rows),
            P(tp, rows),
            P(),
            P(None, None, ("ex", "t1", "t0", "py", "co")),
        ),
        out_specs=P(None, ("ex", "t1", "t0", "py", "co")),
        check_vma=False,
    )
```

```python
import functools
import math

import jax
import jax.numpy as jnp
from jax import lax
from jax.experimental import pallas as pl
from jax.experimental.pallas import tpu as pltpu
from jax.sharding import Mesh, PartitionSpec as P

MODEL_WIDTH = 8192
HIDDEN_WIDTH = 29568
RANK = 128
BANK = 16
EXAMPLES = 4
UP_ROWS = 231
DOWN_ROWS = 64
WINDOW = 256
ROWS = WINDOW + DOWN_ROWS
FIRST = 3 * ROWS
EARLY = {2: (0, 0), 1: (0, 1), 3: (1, 0), 0: (1, 1)}
PARTED = (1, 3)
LOCAL_UP = 7392
PAIR = 2 * RANK
WIDE = EXAMPLES * RANK
BF = jnp.bfloat16
F32 = jnp.float32
VMEM = pl.BlockSpec(memory_space=pltpu.VMEM)
ANY = pl.BlockSpec(memory_space=pl.ANY)
SMEM = pl.BlockSpec(memory_space=pltpu.SMEM)
PLANE = ("ex", "py", "co")


def window_start(owner):
    return jnp.minimum((owner * UP_ROWS) // 16 * 16, LOCAL_UP - WINDOW)


def along(position, shift):
    x, y, c = position
    return (x, (y + shift) % 4, 0) if c == 0 else ((x + shift) % 4, y, 1)


def across(position, shift):
    x, y, c = position
    return ((x + shift) % 4, y, 0) if c == 0 else (x, (y + shift) % 4, 1)


def flat(position):
    return position[0] * 8 + position[1] * 2 + position[2]


def pairs(move):
    everyone = [(x, y, c) for x in range(4) for y in range(4) for c in range(2)]
    return [(flat(p), flat(move(p))) for p in everyone]


def send_same(value, shift):
    return lax.ppermute(value, PLANE, pairs(lambda p: along(p, shift)))


def send_across(value, shift):
    return lax.ppermute(value, PLANE, pairs(lambda p: across(p, shift)))


def position():
    return lax.axis_index("ex"), lax.axis_index("py"), lax.axis_index("co")


def tie(value, arrived):
    return lax.optimization_barrier((value, arrived))


def pack_kernel(grad_hbm, tokens_hbm, down_hbm, up_hbm, *rest):
    gives, rest = rest[:2], rest[2:]
    buffers, portion_ref = rest[:6], rest[6]
    grad, tokens, down, up, turned, loads, sent = rest[7:]
    arrivals = [
        pltpu.make_async_copy(source, target, loads.at[i])
        for i, (source, target) in enumerate(((tokens_hbm, tokens), (grad_hbm, grad), (down_hbm, down), (up_hbm, up)))
    ]
    for arrival in arrivals:
        arrival.start()
    x, y, c = position()
    turned_copies, grad_copies = [], []
    for slot in range(8):
        target = 1 - c if slot < 4 else c
        k = slot % 4
        for i in range(4):
            to_x = lax.rem(x + jnp.where(target == 0, i, k), 4)
            to_y = lax.rem(y + jnp.where(target == 0, k, i), 4)
            owner = to_x * 8 + to_y * 2 + target
            start = pl.multiple_of(window_start(owner), 16)
            column = pl.multiple_of(owner * DOWN_ROWS, DOWN_ROWS)
            out = gives[EARLY[k][0]].at[EARLY[k][1]] if slot < 4 else buffers[k].at[0]
            window_at, down_at = ((i - 1) * WINDOW, 3 * WINDOW + (i - 1) * DOWN_ROWS) if i else (FIRST, FIRST + WINDOW)
            if slot >= 4 and i == 0 and k in PARTED:
                out, window_at, down_at = buffers[4 + PARTED.index(k)].at[0], 0, WINDOW
            grad_copies.append(
                pltpu.make_async_copy(grad.at[pl.ds(start, WINDOW)], out.at[pl.ds(window_at, WINDOW)], sent)
            )
            turned_copies.append(
                pltpu.make_async_copy(turned.at[pl.ds(column, DOWN_ROWS)], out.at[pl.ds(down_at, DOWN_ROWS)], sent)
            )
    arrivals[0].wait()
    turned[...] = tokens[...].T
    for copy in turned_copies:
        copy.start()
    arrivals[1].wait()
    for copy in grad_copies:
        copy.start()
    arrivals[2].wait()
    portion_ref[:, :RANK] = jnp.dot(tokens[...], down[...], preferred_element_type=F32)
    arrivals[3].wait()
    product = jnp.zeros((128, RANK), F32)
    for begin in range(0, LOCAL_UP, 1024):
        end = min(begin + 1024, LOCAL_UP)
        product += lax.dot_general(
            grad[begin:end, :], up[begin:end, :], (((0,), (0,)), ((), ())), preferred_element_type=F32
        )
    portion_ref[:, RANK:] = product
    for copy in turned_copies + grad_copies:
        copy.wait()


def fill_kernel(shifts, taken_ref, *rest):
    count = sum(2 if k in PARTED else 1 for k in shifts)
    buffers, (held, load, sent) = rest[count:2 * count], rest[2 * count:]
    loads = [pltpu.make_async_copy(taken_ref.at[n], held.at[n], load.at[n]) for n in range(len(shifts))]
    for copy in loads:
        copy.start()
    copies, at = [], 0
    for n, k in enumerate(shifts):
        loads[n].wait()
        for begin, size in ((0, FIRST), (FIRST, ROWS)) if k in PARTED else ((0, 4 * ROWS),):
            copies.append(pltpu.make_async_copy(held.at[n, pl.ds(begin, size)], buffers[at].at[1], sent))
            copies[-1].start()
            at += 1
    for copy in copies:
        copy.wait()


def fill_call(shifts, taken, buffers):
    return pl.pallas_call(
        functools.partial(fill_kernel, shifts),
        out_shape=[jax.ShapeDtypeStruct(buffer.shape, BF) for buffer in buffers],
        in_specs=[ANY] * (1 + len(buffers)),
        out_specs=[ANY] * len(buffers),
        scratch_shapes=[
            pltpu.VMEM((len(shifts), 4 * ROWS, 128), BF),
            pltpu.SemaphoreType.DMA((len(shifts),)),
            pltpu.SemaphoreType.DMA,
        ],
        input_output_aliases={k + 1: k for k in range(len(buffers))},
        compiler_params=pltpu.CompilerParams(vmem_limit_bytes=60 << 20),
        cost_estimate=pl.CostEstimate(flops=0, bytes_accessed=1 << 20, transcendentals=0),
    )(taken, *buffers)


def partial_kernel(count, segments_hbm, *rest):
    columns, inner, outs = rest[0:4], rest[4:8], rest[8:8 + count]
    left, side, segments, right_h, right_u, total, done, segments_sem, inner_sem, columns_sem, sent = rest[8 + count:]
    segments_copy = pltpu.make_async_copy(segments_hbm, segments, segments_sem)
    segments_copy.start()
    inner_copies = [pltpu.make_async_copy(inner[k], side.at[k], inner_sem) for k in range(4)]
    column_copies = []
    for k in range(4):
        begin = FIRST if count == 1 and k not in PARTED else 0
        for part in range(2):
            source = columns[k].at[part, pl.ds(begin, count * ROWS)]
            column_copies.append(pltpu.make_async_copy(source, left.at[k, part], columns_sem.at[k]))
    for copy in inner_copies + column_copies:
        copy.start()
    x, y, c = position()
    segments_copy.wait()
    masks = []
    for k in range(4):
        chip = jnp.where(c == 0, x * 4 + lax.rem(y - k + 4, 4), lax.rem(x - k + 4, 4) * 4 + y)
        for part in range(2):
            labels = segments[pl.ds(2 * chip + jnp.where(part == 0, c, 1 - c), 1), :]
            labels = jnp.broadcast_to(labels.astype(F32), (128, RANK)).T
            masks.append([jnp.where(labels == e, 1.0, 0.0).astype(BF) for e in range(EXAMPLES)])
    for copy in inner_copies:
        copy.wait()
    for s in range(8):
        rows = pl.ds(s * 128, 128)
        h = side[s // 2, s % 2 * 128:(s % 2 + 1) * 128, :RANK]
        u = side[s // 2, s % 2 * 128:(s % 2 + 1) * 128, RANK:]
        for e in range(EXAMPLES):
            right_h[rows, e * RANK:(e + 1) * RANK] = h * masks[s][e]
            right_u[rows, e * RANK:(e + 1) * RANK] = u * masks[s][e]
    split = count * WINDOW
    for k in range(4):
        for copy in column_copies[2 * k:2 * k + 2]:
            copy.wait()
        both = pl.ds(k * PAIR, PAIR)
        for n in range(count + 1):
            rows = slice(n * WINDOW, (n + 1) * WINDOW) if n < count else slice(split, count * ROWS)
            joined = jnp.concatenate([left[k, 0, rows, :], left[k, 1, rows, :]], axis=1)
            right = (right_h if n < count else right_u)[both, :]
            product = jnp.dot(joined, right, preferred_element_type=F32)
            total[rows, :] = product if k == 0 else total[rows, :] + product
    out_copies = []
    for n in range(count):
        done[n, :WINDOW, :] = total[n * WINDOW:(n + 1) * WINDOW, :].astype(BF)
        done[n, WINDOW:, :] = total[split + n * DOWN_ROWS:split + (n + 1) * DOWN_ROWS, :].astype(BF)
        out_copies.append(pltpu.make_async_copy(done.at[n], outs[n], sent))
        out_copies[-1].start()
    for copy in out_copies:
        copy.wait()


def partial_call(count, labels, columns, inner):
    return pl.pallas_call(
        functools.partial(partial_kernel, count),
        out_shape=[jax.ShapeDtypeStruct((ROWS, WIDE), BF)] * count,
        in_specs=[ANY] * 9,
        out_specs=[ANY] * count,
        scratch_shapes=[
            pltpu.VMEM((4, 2, count * ROWS, 128), BF),
            pltpu.VMEM((4, PAIR, PAIR), BF),
            pltpu.VMEM((32, 128), jnp.int32),
            pltpu.VMEM((1024, WIDE), BF),
            pltpu.VMEM((1024, WIDE), BF),
            pltpu.VMEM((count * ROWS, WIDE), F32),
            pltpu.VMEM((count, ROWS, WIDE), BF),
            pltpu.SemaphoreType.DMA,
            pltpu.SemaphoreType.DMA,
            pltpu.SemaphoreType.DMA((4,)),
            pltpu.SemaphoreType.DMA,
        ],
        compiler_params=pltpu.CompilerParams(vmem_limit_bytes=60 << 20),
        cost_estimate=pl.CostEstimate(flops=2 * count * ROWS * 1024 * WIDE, bytes_accessed=6 << 20, transcendentals=0),
    )(labels, *columns, *inner)


def feature_kernel(
    own_ref, a_ref, b_ref, c_ref, bounds_ref, offset_ref, select_ref,
    first_up, first_down, second_up, second_down, out_ref, first_ref, second_ref,
):
    for up, down, space in ((first_up, first_down, first_ref), (second_up, second_down, second_ref)):
        space[:WINDOW, :] = jnp.zeros((WINDOW, RANK), F32)
        space[:UP_ROWS, :] = up[...]
        space[:WINDOW, :] = pltpu.roll(space[:WINDOW, :], offset_ref[0], 0)
        space[WINDOW:, :] = down[...]
    first = 0.9 * first_ref[...]
    second = 0.999 * second_ref[...]
    select = select_ref[...]
    for e in range(EXAMPLES):
        at = pl.ds(e * RANK, RANK)
        length = (bounds_ref[e + 1] - bounds_ref[e]).astype(F32)
        total = (own_ref[:, at].astype(F32) + a_ref[:, at].astype(F32)) + (b_ref[:, at].astype(F32) + c_ref[:, at].astype(F32))
        grad = total / length
        feature = (first + 0.1 * grad) / (jnp.sqrt(second + 0.001 * grad * grad) + 1e-08)
        high = feature.astype(BF)
        low = (feature - high.astype(F32)).astype(BF)
        out_ref[:, at] = jnp.dot(select, high, preferred_element_type=F32) + jnp.dot(
            select, low, preferred_element_type=F32
        )


EVERY = ("ex", "t1", "t0", "py", "co")


def groups(along_x):
    found = []
    for fixed in range(4):
        for c in range(2):
            for zs in ((0, 1), (2, 3)) if along_x else ((0, 3), (1, 2)):
                found.append(
                    [
                        (((x * 4 + z) * 4) + y) * 2 + c
                        for w in range(4)
                        for z in zs
                        for x, y in [(w, fixed) if along_x else (fixed, w)]
                    ]
                )
    return found


def spread_sum(value, along_x):
    copies = jnp.broadcast_to(value[None], (8,) + value.shape)
    arrived = lax.all_to_all(
        copies, EVERY, split_axis=0, concat_axis=0, tiled=True, axis_index_groups=groups(along_x)
    )
    return jnp.sum(arrived, axis=0)


def on_device(
    tokens,
    output_gradient,
    adapter_down_factor,
    adapter_up_factor,
    first_moment_down,
    second_moment_down,
    first_moment_up,
    second_moment_up,
    down_row_seeds,
    up_row_seeds,
    segments,
    bank,
):
    x, y, c = position()
    me = x * 8 + y * 2 + c
    shapes = [jax.ShapeDtypeStruct((2, rows, 128), BF) for rows in (4 * ROWS, FIRST, 4 * ROWS, FIRST, ROWS, ROWS)]
    give, give_late, *packed, portion = pl.pallas_call(
        pack_kernel,
        out_shape=[jax.ShapeDtypeStruct((2, 4 * ROWS, 128), BF)] * 2 + shapes + [jax.ShapeDtypeStruct((128, PAIR), F32)],
        in_specs=[ANY] * 4,
        out_specs=[ANY] * 8 + [VMEM],
        scratch_shapes=[
            pltpu.VMEM((LOCAL_UP, 128), BF),
            pltpu.VMEM((128, 2048), BF),
            pltpu.VMEM((2048, 128), BF),
            pltpu.VMEM((LOCAL_UP, 128), BF),
            pltpu.VMEM((2048, 128), BF),
            pltpu.SemaphoreType.DMA((4,)),
            pltpu.SemaphoreType.DMA,
        ],
        compiler_params=pltpu.CompilerParams(vmem_limit_bytes=60 << 20),
        cost_estimate=pl.CostEstimate(flops=2 * 128 * 9440 * 128, bytes_accessed=8 << 20, transcendentals=0),
    )(output_gradient.T, tokens, adapter_down_factor, adapter_up_factor)
    taken = lax.ppermute(give, "co", [(0, 1), (1, 0)])
    give_late, taken = tie(give_late, taken)
    taken_late = lax.ppermute(give_late, "co", [(0, 1), (1, 0)])
    first, second = {}, {}
    first[2], first[1], second[1] = fill_call((2, 1), taken, (packed[2], packed[1], packed[4]))
    taken_late, first[2] = tie(taken_late, first[2])
    first[3], second[3], first[0] = fill_call((3, 0), taken_late, (packed[3], packed[5], packed[0]))
    pair = portion + lax.ppermute(portion, ("t1", "t0"), [(0, 1), (1, 0), (2, 3), (3, 2)])
    whole = pair + lax.ppermute(pair, ("t1", "t0"), [(0, 3), (3, 0), (1, 2), (2, 1)])
    for k in (2, 1, 3):
        first[k] = send_same(first[k], k)
    whole = whole.astype(BF)
    sibling = lax.ppermute(whole, "co", [(0, 1), (1, 0)])
    chip_inner = jnp.concatenate([whole, sibling], axis=0)
    inner = [chip_inner, None, None, None]
    for k in (2, 1):
        inner[k] = send_same(chip_inner, k)
    late, first[2] = tie(chip_inner, first[2])
    inner[3] = send_same(late, 3)
    second[1], first[1] = tie(second[1], first[1])
    second[3], first[3] = tie(second[3], first[3])
    for k in PARTED:
        second[k] = send_same(second[k], k)

    labels = segments.reshape(32, 128)
    sums = partial_call(3, labels, [first[k] for k in range(4)], inner)
    arrived = [send_across(sums[k - 1], k) for k in (2, 1, 3)]
    kept = (labels, segments, first_moment_up, second_moment_up, up_row_seeds, down_row_seeds)
    kept, sums = tie(kept, sums)
    labels, segments, first_moment_up, second_moment_up, up_row_seeds, down_row_seeds = kept
    (own,) = partial_call(1, labels, [first[0], second[1], first[2], second[3]], inner)
    own = own.astype(F32)

    bounds = jnp.sum(
        (segments[None, :] < jnp.arange(EXAMPLES + 1, dtype=jnp.int32)[:, None]).astype(jnp.int32), axis=1
    )

    offset = me * UP_ROWS - window_start(me)
    seeds = jnp.concatenate(
        [
            lax.dynamic_update_slice_in_dim(jnp.full((WINDOW,), -1, jnp.int32), up_row_seeds[0], offset, 0),
            down_row_seeds[0],
        ]
    )
    select = (jnp.arange(BANK, dtype=jnp.int32)[:, None] == seeds[None, :]).astype(BF)
    blocks = pl.pallas_call(
        feature_kernel,
        out_shape=jax.ShapeDtypeStruct((BANK, WIDE), F32),
        in_specs=[VMEM] * 4 + [SMEM] * 2 + [VMEM] * 5,
        out_specs=VMEM,
        scratch_shapes=[pltpu.VMEM((ROWS, RANK), F32), pltpu.VMEM((ROWS, RANK), F32)],
        compiler_params=pltpu.CompilerParams(vmem_limit_bytes=24 << 20),
        cost_estimate=pl.CostEstimate(flops=0, bytes_accessed=3 << 20, transcendentals=0),
    )(
        own, *arrived, bounds, offset.astype(jnp.int32)[None], select,
        first_moment_up[0], first_moment_down[0], second_moment_up[0], second_moment_down[0],
    )

    summed = blocks + lax.ppermute(blocks, "co", [(0, 1), (1, 0)])
    summed = spread_sum(summed, True)
    summed = spread_sum(summed, False)
    inverse = 1.0 / math.sqrt((MODEL_WIDTH + HIDDEN_WIDTH) * RANK)
    sketch = jnp.einsum(
        "jer,jrk->ek", summed.reshape(BANK, EXAMPLES, RANK), bank.astype(F32), precision=lax.Precision.HIGHEST
    )
    return sketch * inverse


def solution(mesh):
    rows = ("ex", "py", "co")
    tp = ("t1", "t0")
    split = Mesh(mesh.devices.reshape(4, 2, 2, 4, 2), ("ex", "t1", "t0", "py", "co"))
    return jax.shard_map(
        on_device,
        mesh=split,
        in_specs=(
            P(rows, tp),
            P(rows, tp),
            P(tp, None),
            P(tp, None),
            P(tp, rows, None),
            P(tp, rows, None),
            P(tp, rows, None),
            P(tp, rows, None),
            P(tp, rows),
            P(tp, rows),
            P(),
            P(None, None, ("ex", "t1", "t0", "py", "co")),
        ),
        out_specs=P(None, ("ex", "t1", "t0", "py", "co")),
        check_vma=False,
    )
```

```python
import functools
import math

import jax
import jax.numpy as jnp
from jax import lax
from jax.experimental import pallas as pl
from jax.experimental.pallas import tpu as pltpu
from jax.sharding import Mesh, PartitionSpec as P

MODEL_WIDTH = 8192
HIDDEN_WIDTH = 29568
RANK = 128
BANK = 16
EXAMPLES = 4
UP_ROWS = 231
DOWN_ROWS = 64
WINDOW = 256
HELD = 240
ROWS = HELD + DOWN_ROWS
FIRST = 3 * ROWS
EARLY = {2: (0, 0), 1: (0, 1), 3: (1, 0), 0: (1, 1)}
PARTED = (1, 3)
LOCAL_UP = 7392
PAIR = 2 * RANK
WIDE = EXAMPLES * RANK
BF = jnp.bfloat16
F32 = jnp.float32
VMEM = pl.BlockSpec(memory_space=pltpu.VMEM)
ANY = pl.BlockSpec(memory_space=pl.ANY)
SMEM = pl.BlockSpec(memory_space=pltpu.SMEM)
PLANE = ("ex", "py", "co")


def window_start(owner):
    return jnp.minimum((owner * UP_ROWS) // 16 * 16, LOCAL_UP - WINDOW)


def along(position, shift):
    x, y, c = position
    return (x, (y + shift) % 4, 0) if c == 0 else ((x + shift) % 4, y, 1)


def across(position, shift):
    x, y, c = position
    return ((x + shift) % 4, y, 0) if c == 0 else (x, (y + shift) % 4, 1)


def flat(position):
    return position[0] * 8 + position[1] * 2 + position[2]


def pairs(move):
    everyone = [(x, y, c) for x in range(4) for y in range(4) for c in range(2)]
    return [(flat(p), flat(move(p))) for p in everyone]


def send_same(value, shift):
    return lax.ppermute(value, PLANE, pairs(lambda p: along(p, shift)))


def send_across(value, shift):
    return lax.ppermute(value, PLANE, pairs(lambda p: across(p, shift)))


def position():
    return lax.axis_index("ex"), lax.axis_index("py"), lax.axis_index("co")


def tie(value, arrived):
    return lax.optimization_barrier((value, arrived))


def pack_kernel(grad_hbm, tokens_hbm, down_hbm, up_hbm, *rest):
    gives, rest = rest[:2], rest[2:]
    buffers, portion_ref = rest[:6], rest[6]
    grad, tokens, down, up, turned, staged, loads, sent = rest[7:]
    arrivals = [
        pltpu.make_async_copy(source, target, loads.at[i])
        for i, (source, target) in enumerate(((tokens_hbm, tokens), (grad_hbm, grad), (down_hbm, down), (up_hbm, up)))
    ]
    for arrival in arrivals:
        arrival.start()
    x, y, c = position()
    arrivals[0].wait()
    turned[...] = tokens[...].T
    arrivals[1].wait()
    copies = []
    for slot in (2, 6, 1, 5, 3, 7, 0, 4):
        target = 1 - c if slot < 4 else c
        k = slot % 4
        for i in range(4):
            to_x = lax.rem(x + jnp.where(target == 0, i, k), 4)
            to_y = lax.rem(y + jnp.where(target == 0, k, i), 4)
            owner = to_x * 8 + to_y * 2 + target
            start = pl.multiple_of(window_start(owner), 16)
            column = pl.multiple_of(owner * DOWN_ROWS, DOWN_ROWS)
            window_at, down_at = ((i - 1) * HELD, 3 * HELD + (i - 1) * DOWN_ROWS) if i else (FIRST, FIRST + HELD)
            window = pltpu.roll(grad[pl.ds(start, WINDOW), :].astype(F32), WINDOW + start - owner * UP_ROWS, 0)
            staged[slot, window_at:window_at + HELD, :] = window[:HELD].astype(BF)
            staged[slot, down_at:down_at + DOWN_ROWS, :] = turned[pl.ds(column, DOWN_ROWS), :]
        if slot < 4:
            parts = [(0, 4 * ROWS, gives[EARLY[k][0]].at[EARLY[k][1]])]
        elif k in PARTED:
            parts = [(0, FIRST, buffers[k].at[0]), (FIRST, ROWS, buffers[4 + PARTED.index(k)].at[0])]
        else:
            parts = [(0, 4 * ROWS, buffers[k].at[0])]
        for begin, size, out in parts:
            copies.append(pltpu.make_async_copy(staged.at[slot, pl.ds(begin, size)], out, sent))
            copies[-1].start()
    arrivals[2].wait()
    portion_ref[:, :RANK] = jnp.dot(tokens[...], down[...], preferred_element_type=F32)
    arrivals[3].wait()
    product = jnp.zeros((128, RANK), F32)
    for begin in range(0, LOCAL_UP, 1024):
        end = min(begin + 1024, LOCAL_UP)
        product += lax.dot_general(
            grad[begin:end, :], up[begin:end, :], (((0,), (0,)), ((), ())), preferred_element_type=F32
        )
    portion_ref[:, RANK:] = product
    for copy in copies:
        copy.wait()


def fill_kernel(shifts, taken_ref, *rest):
    count = sum(2 if k in PARTED else 1 for k in shifts)
    buffers, (held, load, sent) = rest[count:2 * count], rest[2 * count:]
    loads = [pltpu.make_async_copy(taken_ref.at[n], held.at[n], load.at[n]) for n in range(len(shifts))]
    for copy in loads:
        copy.start()
    copies, at = [], 0
    for n, k in enumerate(shifts):
        loads[n].wait()
        for begin, size in ((0, FIRST), (FIRST, ROWS)) if k in PARTED else ((0, 4 * ROWS),):
            copies.append(pltpu.make_async_copy(held.at[n, pl.ds(begin, size)], buffers[at].at[1], sent))
            copies[-1].start()
            at += 1
    for copy in copies:
        copy.wait()


def fill_call(shifts, taken, buffers):
    return pl.pallas_call(
        functools.partial(fill_kernel, shifts),
        out_shape=[jax.ShapeDtypeStruct(buffer.shape, BF) for buffer in buffers],
        in_specs=[ANY] * (1 + len(buffers)),
        out_specs=[ANY] * len(buffers),
        scratch_shapes=[
            pltpu.VMEM((len(shifts), 4 * ROWS, 128), BF),
            pltpu.SemaphoreType.DMA((len(shifts),)),
            pltpu.SemaphoreType.DMA,
        ],
        input_output_aliases={k + 1: k for k in range(len(buffers))},
        compiler_params=pltpu.CompilerParams(vmem_limit_bytes=60 << 20),
        cost_estimate=pl.CostEstimate(flops=0, bytes_accessed=1 << 20, transcendentals=0),
    )(taken, *buffers)


def partial_kernel(count, segments_hbm, *rest):
    columns, inner, outs = rest[0:4], rest[4:8], rest[8:8 + count]
    left, side, segments, right_h, right_u, total, done, segments_sem, inner_sem, columns_sem, sent = rest[8 + count:]
    segments_copy = pltpu.make_async_copy(segments_hbm, segments, segments_sem)
    segments_copy.start()
    inner_copies = [pltpu.make_async_copy(inner[k], side.at[k], inner_sem) for k in range(4)]
    column_copies = []
    for k in range(4):
        begin = FIRST if count == 1 and k not in PARTED else 0
        for part in range(2):
            source = columns[k].at[part, pl.ds(begin, count * ROWS)]
            column_copies.append(pltpu.make_async_copy(source, left.at[k, part], columns_sem.at[k]))
    for copy in inner_copies + column_copies:
        copy.start()
    x, y, c = position()
    segments_copy.wait()
    masks = []
    for k in range(4):
        chip = jnp.where(c == 0, x * 4 + lax.rem(y - k + 4, 4), lax.rem(x - k + 4, 4) * 4 + y)
        for part in range(2):
            labels = segments[pl.ds(2 * chip + jnp.where(part == 0, c, 1 - c), 1), :]
            labels = jnp.broadcast_to(labels.astype(F32), (128, RANK)).T
            masks.append([jnp.where(labels == e, 1.0, 0.0).astype(BF) for e in range(EXAMPLES)])
    for copy in inner_copies:
        copy.wait()
    for s in range(8):
        rows = pl.ds(s * 128, 128)
        h = side[s // 2, s % 2 * 128:(s % 2 + 1) * 128, :RANK]
        u = side[s // 2, s % 2 * 128:(s % 2 + 1) * 128, RANK:]
        for e in range(EXAMPLES):
            right_h[rows, e * RANK:(e + 1) * RANK] = h * masks[s][e]
            right_u[rows, e * RANK:(e + 1) * RANK] = u * masks[s][e]
    split = count * HELD
    for k in range(4):
        for copy in column_copies[2 * k:2 * k + 2]:
            copy.wait()
        both = pl.ds(k * PAIR, PAIR)
        for n in range(count + 1):
            rows = slice(n * HELD, (n + 1) * HELD) if n < count else slice(split, count * ROWS)
            joined = jnp.concatenate([left[k, 0, rows, :], left[k, 1, rows, :]], axis=1)
            right = (right_h if n < count else right_u)[both, :]
            product = jnp.dot(joined, right, preferred_element_type=F32)
            total[rows, :] = product if k == 0 else total[rows, :] + product
    out_copies = []
    for n in range(count):
        done[n, :HELD, :] = total[n * HELD:(n + 1) * HELD, :].astype(BF)
        done[n, HELD:, :] = total[split + n * DOWN_ROWS:split + (n + 1) * DOWN_ROWS, :].astype(BF)
        out_copies.append(pltpu.make_async_copy(done.at[n], outs[n], sent))
        out_copies[-1].start()
    for copy in out_copies:
        copy.wait()


def partial_call(count, labels, columns, inner):
    return pl.pallas_call(
        functools.partial(partial_kernel, count),
        out_shape=[jax.ShapeDtypeStruct((ROWS, WIDE), BF)] * count,
        in_specs=[ANY] * 9,
        out_specs=[ANY] * count,
        scratch_shapes=[
            pltpu.VMEM((4, 2, count * ROWS, 128), BF),
            pltpu.VMEM((4, PAIR, PAIR), BF),
            pltpu.VMEM((32, 128), jnp.int32),
            pltpu.VMEM((1024, WIDE), BF),
            pltpu.VMEM((1024, WIDE), BF),
            pltpu.VMEM((count * ROWS, WIDE), F32),
            pltpu.VMEM((count, ROWS, WIDE), BF),
            pltpu.SemaphoreType.DMA,
            pltpu.SemaphoreType.DMA,
            pltpu.SemaphoreType.DMA((4,)),
            pltpu.SemaphoreType.DMA,
        ],
        compiler_params=pltpu.CompilerParams(vmem_limit_bytes=60 << 20),
        cost_estimate=pl.CostEstimate(flops=2 * count * ROWS * 1024 * WIDE, bytes_accessed=6 << 20, transcendentals=0),
    )(labels, *columns, *inner)


def feature_kernel(
    own_ref, a_ref, b_ref, c_ref, bounds_ref, select_ref,
    first_up, first_down, second_up, second_down, out_ref, first_ref, second_ref,
):
    for up, down, space in ((first_up, first_down, first_ref), (second_up, second_down, second_ref)):
        space[HELD - 16:HELD, :] = jnp.zeros((16, RANK), F32)
        space[:UP_ROWS, :] = up[...]
        space[HELD:, :] = down[...]
    first = 0.9 * first_ref[...]
    second = 0.999 * second_ref[...]
    select = select_ref[...]
    for e in range(EXAMPLES):
        at = pl.ds(e * RANK, RANK)
        length = (bounds_ref[e + 1] - bounds_ref[e]).astype(F32)
        total = (own_ref[:, at].astype(F32) + a_ref[:, at].astype(F32)) + (b_ref[:, at].astype(F32) + c_ref[:, at].astype(F32))
        grad = total / length
        feature = (first + 0.1 * grad) / (jnp.sqrt(second + 0.001 * grad * grad) + 1e-08)
        high = feature.astype(BF)
        low = (feature - high.astype(F32)).astype(BF)
        out_ref[:, at] = jnp.dot(select, high, preferred_element_type=F32) + jnp.dot(
            select, low, preferred_element_type=F32
        )


EVERY = ("ex", "t1", "t0", "py", "co")


def groups(along_x):
    found = []
    for fixed in range(4):
        for c in range(2):
            for zs in ((0, 1), (2, 3)) if along_x else ((0, 3), (1, 2)):
                found.append(
                    [
                        (((x * 4 + z) * 4) + y) * 2 + c
                        for w in range(4)
                        for z in zs
                        for x, y in [(w, fixed) if along_x else (fixed, w)]
                    ]
                )
    return found


def spread_sum(value, along_x):
    copies = jnp.broadcast_to(value[None], (8,) + value.shape)
    arrived = lax.all_to_all(
        copies, EVERY, split_axis=0, concat_axis=0, tiled=True, axis_index_groups=groups(along_x)
    )
    return jnp.sum(arrived, axis=0)


def on_device(
    tokens,
    output_gradient,
    adapter_down_factor,
    adapter_up_factor,
    first_moment_down,
    second_moment_down,
    first_moment_up,
    second_moment_up,
    down_row_seeds,
    up_row_seeds,
    segments,
    bank,
):
    shapes = [jax.ShapeDtypeStruct((2, rows, 128), BF) for rows in (4 * ROWS, FIRST, 4 * ROWS, FIRST, ROWS, ROWS)]
    give, give_late, *packed, portion = pl.pallas_call(
        pack_kernel,
        out_shape=[jax.ShapeDtypeStruct((2, 4 * ROWS, 128), BF)] * 2 + shapes + [jax.ShapeDtypeStruct((128, PAIR), F32)],
        in_specs=[ANY] * 4,
        out_specs=[ANY] * 8 + [VMEM],
        scratch_shapes=[
            pltpu.VMEM((LOCAL_UP, 128), BF),
            pltpu.VMEM((128, 2048), BF),
            pltpu.VMEM((2048, 128), BF),
            pltpu.VMEM((LOCAL_UP, 128), BF),
            pltpu.VMEM((2048, 128), BF),
            pltpu.VMEM((8, 4 * ROWS, 128), BF),
            pltpu.SemaphoreType.DMA((4,)),
            pltpu.SemaphoreType.DMA,
        ],
        compiler_params=pltpu.CompilerParams(vmem_limit_bytes=60 << 20),
        cost_estimate=pl.CostEstimate(flops=2 * 128 * 9440 * 128, bytes_accessed=8 << 20, transcendentals=0),
    )(output_gradient.T, tokens, adapter_down_factor, adapter_up_factor)
    taken = lax.ppermute(give, "co", [(0, 1), (1, 0)])
    give_late, taken = tie(give_late, taken)
    taken_late = lax.ppermute(give_late, "co", [(0, 1), (1, 0)])
    first, second = {}, {}
    first[2], first[1], second[1] = fill_call((2, 1), taken, (packed[2], packed[1], packed[4]))
    taken_late, first[2] = tie(taken_late, first[2])
    first[3], second[3], first[0] = fill_call((3, 0), taken_late, (packed[3], packed[5], packed[0]))
    pair = portion + lax.ppermute(portion, ("t1", "t0"), [(0, 1), (1, 0), (2, 3), (3, 2)])
    whole = pair + lax.ppermute(pair, ("t1", "t0"), [(0, 3), (3, 0), (1, 2), (2, 1)])
    for k in (2, 1, 3):
        first[k] = send_same(first[k], k)
    whole = whole.astype(BF)
    sibling = lax.ppermute(whole, "co", [(0, 1), (1, 0)])
    chip_inner = jnp.concatenate([whole, sibling], axis=0)
    inner = [chip_inner, None, None, None]
    for k in (2, 1):
        inner[k] = send_same(chip_inner, k)
    late, first[2] = tie(chip_inner, first[2])
    inner[3] = send_same(late, 3)
    second[1], first[1] = tie(second[1], first[1])
    second[3], first[3] = tie(second[3], first[3])
    for k in PARTED:
        second[k] = send_same(second[k], k)

    labels = segments.reshape(32, 128)
    sums = partial_call(3, labels, [first[k] for k in range(4)], inner)
    arrived = [send_across(sums[k - 1], k) for k in (2, 1, 3)]
    kept = (labels, segments, first_moment_up, second_moment_up, up_row_seeds, down_row_seeds)
    kept, sums = tie(kept, sums)
    labels, segments, first_moment_up, second_moment_up, up_row_seeds, down_row_seeds = kept
    (own,) = partial_call(1, labels, [first[0], second[1], first[2], second[3]], inner)
    own = own.astype(F32)

    bounds = jnp.sum(
        (segments[None, :] < jnp.arange(EXAMPLES + 1, dtype=jnp.int32)[:, None]).astype(jnp.int32), axis=1
    )

    seeds = jnp.concatenate([up_row_seeds[0], jnp.full((HELD - UP_ROWS,), -1, jnp.int32), down_row_seeds[0]])
    select = (jnp.arange(BANK, dtype=jnp.int32)[:, None] == seeds[None, :]).astype(BF)
    blocks = pl.pallas_call(
        feature_kernel,
        out_shape=jax.ShapeDtypeStruct((BANK, WIDE), F32),
        in_specs=[VMEM] * 4 + [SMEM] + [VMEM] * 5,
        out_specs=VMEM,
        scratch_shapes=[pltpu.VMEM((ROWS, RANK), F32), pltpu.VMEM((ROWS, RANK), F32)],
        compiler_params=pltpu.CompilerParams(vmem_limit_bytes=24 << 20),
        cost_estimate=pl.CostEstimate(flops=0, bytes_accessed=3 << 20, transcendentals=0),
    )(
        own, *arrived, bounds, select,
        first_moment_up[0], first_moment_down[0], second_moment_up[0], second_moment_down[0],
    )

    summed = blocks + lax.ppermute(blocks, "co", [(0, 1), (1, 0)])
    summed = spread_sum(summed, False)
    summed = spread_sum(summed, True)
    inverse = 1.0 / math.sqrt((MODEL_WIDTH + HIDDEN_WIDTH) * RANK)
    sketch = jnp.einsum(
        "jer,jrk->ek", summed.reshape(BANK, EXAMPLES, RANK), bank.astype(F32), precision=lax.Precision.HIGHEST
    )
    return sketch * inverse


def solution(mesh):
    rows = ("ex", "py", "co")
    tp = ("t1", "t0")
    split = Mesh(mesh.devices.reshape(4, 2, 2, 4, 2), ("ex", "t1", "t0", "py", "co"))
    return jax.shard_map(
        on_device,
        mesh=split,
        in_specs=(
            P(rows, tp),
            P(rows, tp),
            P(tp, None),
            P(tp, None),
            P(tp, rows, None),
            P(tp, rows, None),
            P(tp, rows, None),
            P(tp, rows, None),
            P(tp, rows),
            P(tp, rows),
            P(),
            P(None, None, ("ex", "t1", "t0", "py", "co")),
        ),
        out_specs=P(None, ("ex", "t1", "t0", "py", "co")),
        check_vma=False,
    )
```

```python
import functools
import math

import jax
import jax.numpy as jnp
from jax import lax
from jax.experimental import pallas as pl
from jax.experimental.pallas import tpu as pltpu
from jax.sharding import Mesh, PartitionSpec as P

MODEL_WIDTH = 8192
HIDDEN_WIDTH = 29568
RANK = 128
BANK = 16
EXAMPLES = 4
UP_ROWS = 231
DOWN_ROWS = 64
WINDOW = 256
HELD = 240
ROWS = HELD + DOWN_ROWS
FIRST = 3 * ROWS
PARTED = (1, 3)
LOCAL_UP = 7392
PAIR = 2 * RANK
WIDE = EXAMPLES * RANK
BF = jnp.bfloat16
F32 = jnp.float32
VMEM = pl.BlockSpec(memory_space=pltpu.VMEM)
ANY = pl.BlockSpec(memory_space=pl.ANY)
SMEM = pl.BlockSpec(memory_space=pltpu.SMEM)
PLANE = ("ex", "py", "co")


def window_start(owner):
    return jnp.minimum((owner * UP_ROWS) // 16 * 16, LOCAL_UP - WINDOW)


def along(position, shift):
    x, y, c = position
    return (x, (y + shift) % 4, 0) if c == 0 else ((x + shift) % 4, y, 1)


def across(position, shift):
    x, y, c = position
    return ((x + shift) % 4, y, 0) if c == 0 else (x, (y + shift) % 4, 1)


def flat(position):
    return position[0] * 8 + position[1] * 2 + position[2]


def pairs(move):
    everyone = [(x, y, c) for x in range(4) for y in range(4) for c in range(2)]
    return [(flat(p), flat(move(p))) for p in everyone]


def send_same(value, shift):
    return lax.ppermute(value, PLANE, pairs(lambda p: along(p, shift)))


def send_across(value, shift):
    return lax.ppermute(value, PLANE, pairs(lambda p: across(p, shift)))


def position():
    return lax.axis_index("ex"), lax.axis_index("py"), lax.axis_index("co")


def tie(value, arrived):
    return lax.optimization_barrier((value, arrived))


def pack_kernel(grad, tokens, *rest):
    give, mine, turned = rest[0], rest[1:5], rest[5]
    x, y, c = position()
    turned[...] = tokens[...].T
    for slot in (2, 6, 1, 5, 3, 7, 0, 4):
        target = 1 - c if slot < 4 else c
        k = slot % 4
        for i in range(4):
            to_x = lax.rem(x + jnp.where(target == 0, i, k), 4)
            to_y = lax.rem(y + jnp.where(target == 0, k, i), 4)
            owner = to_x * 8 + to_y * 2 + target
            start = pl.multiple_of(window_start(owner), 16)
            column = pl.multiple_of(owner * DOWN_ROWS, DOWN_ROWS)
            window_at, down_at = ((i - 1) * HELD, 3 * HELD + (i - 1) * DOWN_ROWS) if i else (FIRST, FIRST + HELD)
            out = give.at[k] if slot < 4 else mine[k]
            window = pltpu.roll(grad[pl.ds(start, WINDOW), :].astype(F32), WINDOW + start - owner * UP_ROWS, 0)
            out[window_at:window_at + HELD, :] = window[:HELD].astype(BF)
            out[down_at:down_at + DOWN_ROWS, :] = turned[pl.ds(column, DOWN_ROWS), :]


def product_kernel(grad, tokens, down, up, portion_ref):
    portion_ref[:, :RANK] = jnp.dot(tokens[...], down[...], preferred_element_type=F32)
    product = jnp.zeros((128, RANK), F32)
    for begin in range(0, LOCAL_UP, 1024):
        end = min(begin + 1024, LOCAL_UP)
        product += lax.dot_general(
            grad[begin:end, :], up[begin:end, :], (((0,), (0,)), ((), ())), preferred_element_type=F32
        )
    portion_ref[:, RANK:] = product


def fill_kernel(shifts, taken_ref, *rest):
    mine, buffers = rest[:len(shifts)], rest[len(shifts):]
    at = 0
    for n, k in enumerate(shifts):
        for begin, size in ((0, FIRST), (FIRST, ROWS)) if k in PARTED else ((0, 4 * ROWS),):
            buffers[at][0] = mine[n][begin:begin + size, :]
            buffers[at][1] = taken_ref[k, begin:begin + size, :]
            at += 1


def fill_call(shifts, taken, mine):
    sizes = [size for k in shifts for size in ((FIRST, ROWS) if k in PARTED else (4 * ROWS,))]
    return pl.pallas_call(
        functools.partial(fill_kernel, shifts),
        out_shape=[jax.ShapeDtypeStruct((2, size, 128), BF) for size in sizes],
        in_specs=[VMEM] * (1 + len(shifts)),
        out_specs=[VMEM] * len(sizes),
        compiler_params=pltpu.CompilerParams(vmem_limit_bytes=16 << 20),
        cost_estimate=pl.CostEstimate(flops=0, bytes_accessed=1 << 20, transcendentals=0),
    )(taken, *mine)


def partial_kernel(count, segments, *rest):
    columns, inner, outs = rest[0:4], rest[4:8], rest[8:8 + count]
    right_h, right_u, total = rest[8 + count:]
    x, y, c = position()
    split = count * HELD
    for k in range(4):
        chip = jnp.where(c == 0, x * 4 + lax.rem(y - k + 4, 4), lax.rem(x - k + 4, 4) * 4 + y)
        for part in range(2):
            labels = segments[pl.ds(2 * chip + jnp.where(part == 0, c, 1 - c), 1), :]
            labels = jnp.broadcast_to(labels.astype(F32), (128, RANK)).T
            rows = pl.ds(k * PAIR + part * 128, 128)
            h = inner[k][part * 128:(part + 1) * 128, :RANK]
            u = inner[k][part * 128:(part + 1) * 128, RANK:]
            for e in range(EXAMPLES):
                mask = jnp.where(labels == e, 1.0, 0.0).astype(BF)
                right_h[rows, e * RANK:(e + 1) * RANK] = h * mask
                right_u[rows, e * RANK:(e + 1) * RANK] = u * mask
        begin = FIRST if count == 1 and k not in PARTED else 0
        both = pl.ds(k * PAIR, PAIR)
        for n in range(count + 1):
            at, size = (n * HELD, HELD) if n < count else (split, count * DOWN_ROWS)
            pieces = [columns[k][part, begin + at:begin + at + size, :] for part in range(2)]
            right = (right_h if n < count else right_u)[both, :]
            product = jnp.dot(jnp.concatenate(pieces, axis=1), right, preferred_element_type=F32)
            total[at:at + size, :] = product if k == 0 else total[at:at + size, :] + product
    for n in range(count):
        outs[n][:HELD, :] = total[n * HELD:(n + 1) * HELD, :].astype(BF)
        outs[n][HELD:, :] = total[split + n * DOWN_ROWS:split + (n + 1) * DOWN_ROWS, :].astype(BF)


def partial_call(count, labels, columns, inner):
    return pl.pallas_call(
        functools.partial(partial_kernel, count),
        out_shape=[jax.ShapeDtypeStruct((ROWS, WIDE), BF)] * count,
        in_specs=[VMEM] * 9,
        out_specs=[VMEM] * count,
        scratch_shapes=[
            pltpu.VMEM((1024, WIDE), BF),
            pltpu.VMEM((1024, WIDE), BF),
            pltpu.VMEM((count * ROWS, WIDE), F32),
        ],
        compiler_params=pltpu.CompilerParams(vmem_limit_bytes=24 << 20),
        cost_estimate=pl.CostEstimate(flops=2 * count * ROWS * 1024 * WIDE, bytes_accessed=6 << 20, transcendentals=0),
    )(labels, *columns, *inner)


def feature_kernel(
    own_ref, a_ref, b_ref, c_ref, bounds_ref, select_ref,
    first_up, first_down, second_up, second_down, out_ref, first_ref, second_ref,
):
    for up, down, space in ((first_up, first_down, first_ref), (second_up, second_down, second_ref)):
        space[HELD - 16:HELD, :] = jnp.zeros((16, RANK), F32)
        space[:UP_ROWS, :] = up[...]
        space[HELD:, :] = down[...]
    first = 0.9 * first_ref[...]
    second = 0.999 * second_ref[...]
    select = select_ref[...]
    for e in range(EXAMPLES):
        at = pl.ds(e * RANK, RANK)
        length = (bounds_ref[e + 1] - bounds_ref[e]).astype(F32)
        total = (own_ref[:, at].astype(F32) + a_ref[:, at].astype(F32)) + (b_ref[:, at].astype(F32) + c_ref[:, at].astype(F32))
        grad = total / length
        feature = (first + 0.1 * grad) / (jnp.sqrt(second + 0.001 * grad * grad) + 1e-08)
        high = feature.astype(BF)
        low = (feature - high.astype(F32)).astype(BF)
        out_ref[:, at] = jnp.dot(select, high, preferred_element_type=F32) + jnp.dot(
            select, low, preferred_element_type=F32
        )


EVERY = ("ex", "t1", "t0", "py", "co")


def groups(along_x):
    found = []
    for fixed in range(4):
        for c in range(2):
            for zs in ((0, 1), (2, 3)) if along_x else ((0, 3), (1, 2)):
                found.append(
                    [
                        (((x * 4 + z) * 4) + y) * 2 + c
                        for w in range(4)
                        for z in zs
                        for x, y in [(w, fixed) if along_x else (fixed, w)]
                    ]
                )
    return found


def spread_sum(value, along_x):
    copies = jnp.broadcast_to(value[None], (8,) + value.shape)
    arrived = lax.all_to_all(
        copies, EVERY, split_axis=0, concat_axis=0, tiled=True, axis_index_groups=groups(along_x)
    )
    return jnp.sum(arrived, axis=0)


def on_device(
    tokens,
    output_gradient,
    adapter_down_factor,
    adapter_up_factor,
    first_moment_down,
    second_moment_down,
    first_moment_up,
    second_moment_up,
    down_row_seeds,
    up_row_seeds,
    segments,
    bank,
):
    turned_grad = output_gradient.T
    give, *mine = pl.pallas_call(
        pack_kernel,
        out_shape=[jax.ShapeDtypeStruct((4, 4 * ROWS, 128), BF)] + [jax.ShapeDtypeStruct((4 * ROWS, 128), BF)] * 4,
        in_specs=[VMEM] * 2,
        out_specs=[VMEM] * 5,
        scratch_shapes=[pltpu.VMEM((2048, 128), BF)],
        compiler_params=pltpu.CompilerParams(vmem_limit_bytes=24 << 20),
        cost_estimate=pl.CostEstimate(flops=0, bytes_accessed=5 << 20, transcendentals=0),
    )(turned_grad, tokens)
    portion = pl.pallas_call(
        product_kernel,
        out_shape=jax.ShapeDtypeStruct((128, PAIR), F32),
        in_specs=[VMEM] * 4,
        out_specs=VMEM,
        compiler_params=pltpu.CompilerParams(vmem_limit_bytes=24 << 20),
        cost_estimate=pl.CostEstimate(flops=2 * 128 * 9440 * 128, bytes_accessed=5 << 20, transcendentals=0),
    )(turned_grad, tokens, adapter_down_factor, adapter_up_factor)
    taken = lax.ppermute(give, "co", [(0, 1), (1, 0)])
    taken, portion = tie(taken, portion)
    first, second = {}, {}
    (first[2],) = fill_call((2,), taken, (mine[2],))
    first[1], second[1], first[3], second[3], first[0] = fill_call((1, 3, 0), taken, (mine[1], mine[3], mine[0]))
    peers = [lax.ppermute(portion, ("t1", "t0"), [(i, (i + shift) % 4) for i in range(4)]) for shift in (2, 1, 3)]
    for k in (2, 1, 3):
        first[k] = send_same(first[k], k)
    whole = ((portion + peers[0]) + (peers[1] + peers[2])).astype(BF)
    sibling = lax.ppermute(whole, "co", [(0, 1), (1, 0)])
    chip_inner = jnp.concatenate([whole, sibling], axis=0)
    inner = [chip_inner, None, None, None]
    for k in (2, 1):
        inner[k] = send_same(chip_inner, k)
    late, first[2] = tie(chip_inner, first[2])
    inner[3] = send_same(late, 3)
    second[1], first[1] = tie(second[1], first[1])
    second[3], first[3] = tie(second[3], first[3])
    for k in PARTED:
        second[k] = send_same(second[k], k)

    labels = segments.reshape(32, 128)
    sums = partial_call(3, labels, [first[k] for k in range(4)], inner)
    arrived = [send_across(sums[k - 1], k) for k in (2, 1, 3)]
    kept = (labels, segments, first_moment_up, second_moment_up, up_row_seeds, down_row_seeds)
    kept, sums = tie(kept, sums)
    labels, segments, first_moment_up, second_moment_up, up_row_seeds, down_row_seeds = kept
    (own,) = partial_call(1, labels, [first[0], second[1], first[2], second[3]], inner)
    own = own.astype(F32)

    bounds = jnp.sum(
        (segments[None, :] < jnp.arange(EXAMPLES + 1, dtype=jnp.int32)[:, None]).astype(jnp.int32), axis=1
    )

    seeds = jnp.concatenate([up_row_seeds[0], jnp.full((HELD - UP_ROWS,), -1, jnp.int32), down_row_seeds[0]])
    select = (jnp.arange(BANK, dtype=jnp.int32)[:, None] == seeds[None, :]).astype(BF)
    blocks = pl.pallas_call(
        feature_kernel,
        out_shape=jax.ShapeDtypeStruct((BANK, WIDE), F32),
        in_specs=[VMEM] * 4 + [SMEM] + [VMEM] * 5,
        out_specs=VMEM,
        scratch_shapes=[pltpu.VMEM((ROWS, RANK), F32), pltpu.VMEM((ROWS, RANK), F32)],
        compiler_params=pltpu.CompilerParams(vmem_limit_bytes=24 << 20),
        cost_estimate=pl.CostEstimate(flops=0, bytes_accessed=3 << 20, transcendentals=0),
    )(
        own, *arrived, bounds, select,
        first_moment_up[0], first_moment_down[0], second_moment_up[0], second_moment_down[0],
    )

    summed = blocks + lax.ppermute(blocks, "co", [(0, 1), (1, 0)])
    summed = spread_sum(summed, False)
    summed = spread_sum(summed, True)
    inverse = 1.0 / math.sqrt((MODEL_WIDTH + HIDDEN_WIDTH) * RANK)
    sketch = jnp.einsum(
        "jer,jrk->ek", summed.reshape(BANK, EXAMPLES, RANK), bank.astype(F32), precision=lax.Precision.HIGHEST
    )
    return sketch * inverse


def solution(mesh):
    rows = ("ex", "py", "co")
    tp = ("t1", "t0")
    split = Mesh(mesh.devices.reshape(4, 2, 2, 4, 2), ("ex", "t1", "t0", "py", "co"))
    return jax.shard_map(
        on_device,
        mesh=split,
        in_specs=(
            P(rows, tp),
            P(rows, tp),
            P(tp, None),
            P(tp, None),
            P(tp, rows, None),
            P(tp, rows, None),
            P(tp, rows, None),
            P(tp, rows, None),
            P(tp, rows),
            P(tp, rows),
            P(),
            P(None, None, ("ex", "t1", "t0", "py", "co")),
        ),
        out_specs=P(None, ("ex", "t1", "t0", "py", "co")),
        check_vma=False,
    )
```

```python
import functools
import math

import jax
import jax.numpy as jnp
from jax import lax
from jax.experimental import pallas as pl
from jax.experimental.pallas import tpu as pltpu
from jax.sharding import Mesh, PartitionSpec as P

MODEL_WIDTH = 8192
HIDDEN_WIDTH = 29568
RANK = 128
BANK = 16
EXAMPLES = 4
UP_ROWS = 231
DOWN_ROWS = 64
WINDOW = 256
HELD = 240
ROWS = HELD + DOWN_ROWS
FIRST = 3 * ROWS
PARTED = (1, 3)
LOCAL_UP = 7392
PAIR = 2 * RANK
WIDE = EXAMPLES * RANK
BF = jnp.bfloat16
F32 = jnp.float32
VMEM = pl.BlockSpec(memory_space=pltpu.VMEM)
ANY = pl.BlockSpec(memory_space=pl.ANY)
SMEM = pl.BlockSpec(memory_space=pltpu.SMEM)
PLANE = ("ex", "py", "co")


def window_start(owner):
    return jnp.minimum((owner * UP_ROWS) // 16 * 16, LOCAL_UP - WINDOW)


def along(position, shift):
    x, y, c = position
    return (x, (y + shift) % 4, 0) if c == 0 else ((x + shift) % 4, y, 1)


def across(position, shift):
    x, y, c = position
    return ((x + shift) % 4, y, 0) if c == 0 else (x, (y + shift) % 4, 1)


def flat(position):
    return position[0] * 8 + position[1] * 2 + position[2]


def pairs(move):
    everyone = [(x, y, c) for x in range(4) for y in range(4) for c in range(2)]
    return [(flat(p), flat(move(p))) for p in everyone]


def send_same(value, shift):
    return lax.ppermute(value, PLANE, pairs(lambda p: along(p, shift)))


def send_across(value, shift):
    return lax.ppermute(value, PLANE, pairs(lambda p: across(p, shift)))


def position():
    return lax.axis_index("ex"), lax.axis_index("py"), lax.axis_index("co")


def tie(value, arrived):
    return lax.optimization_barrier((value, arrived))


def pack_kernel(grad, tokens, *rest):
    give, mine, turned = rest[0], rest[1:5], rest[5]
    x, y, c = position()
    turned[...] = tokens[...].T
    for slot in (2, 6, 1, 5, 3, 7, 0, 4):
        target = 1 - c if slot < 4 else c
        k = slot % 4
        for i in range(4):
            to_x = lax.rem(x + jnp.where(target == 0, i, k), 4)
            to_y = lax.rem(y + jnp.where(target == 0, k, i), 4)
            owner = to_x * 8 + to_y * 2 + target
            start = pl.multiple_of(window_start(owner), 16)
            column = pl.multiple_of(owner * DOWN_ROWS, DOWN_ROWS)
            window_at, down_at = ((i - 1) * HELD, 3 * HELD + (i - 1) * DOWN_ROWS) if i else (FIRST, FIRST + HELD)
            out = give.at[k] if slot < 4 else mine[k]
            window = pltpu.roll(grad[pl.ds(start, WINDOW), :].astype(F32), WINDOW + start - owner * UP_ROWS, 0)
            out[window_at:window_at + HELD, :] = window[:HELD].astype(BF)
            out[down_at:down_at + DOWN_ROWS, :] = turned[pl.ds(column, DOWN_ROWS), :]


def product_kernel(grad, tokens, down, up, portion_ref):
    portion_ref[:, :RANK] = jnp.dot(tokens[...], down[...], preferred_element_type=F32)
    product = jnp.zeros((128, RANK), F32)
    for begin in range(0, LOCAL_UP, 1024):
        end = min(begin + 1024, LOCAL_UP)
        product += lax.dot_general(
            grad[begin:end, :], up[begin:end, :], (((0,), (0,)), ((), ())), preferred_element_type=F32
        )
    portion_ref[:, RANK:] = product


def fill_kernel(shifts, taken_ref, *rest):
    mine, buffers = rest[:len(shifts)], rest[len(shifts):]
    at = 0
    for n, k in enumerate(shifts):
        for begin, size in ((0, FIRST), (FIRST, ROWS)) if k in PARTED else ((0, 4 * ROWS),):
            buffers[at][0] = mine[n][begin:begin + size, :]
            buffers[at][1] = taken_ref[k, begin:begin + size, :]
            at += 1


def fill_call(shifts, taken, mine):
    sizes = [size for k in shifts for size in ((FIRST, ROWS) if k in PARTED else (4 * ROWS,))]
    return pl.pallas_call(
        functools.partial(fill_kernel, shifts),
        out_shape=[jax.ShapeDtypeStruct((2, size, 128), BF) for size in sizes],
        in_specs=[VMEM] * (1 + len(shifts)),
        out_specs=[VMEM] * len(sizes),
        compiler_params=pltpu.CompilerParams(vmem_limit_bytes=16 << 20),
        cost_estimate=pl.CostEstimate(flops=0, bytes_accessed=1 << 20, transcendentals=0),
    )(taken, *mine)


def partial_kernel(count, segments, *rest):
    columns, inner, outs = rest[0:4], rest[4:8], rest[8:8 + count]
    right_h, right_u, total = rest[8 + count:]
    x, y, c = position()
    split = count * HELD
    for k in range(4):
        chip = jnp.where(c == 0, x * 4 + lax.rem(y - k + 4, 4), lax.rem(x - k + 4, 4) * 4 + y)
        for part in range(2):
            labels = segments[pl.ds(2 * chip + jnp.where(part == 0, c, 1 - c), 1), :]
            labels = jnp.broadcast_to(labels.astype(F32), (128, RANK)).T
            rows = pl.ds(k * PAIR + part * 128, 128)
            h = inner[k][part * 128:(part + 1) * 128, :RANK]
            u = inner[k][part * 128:(part + 1) * 128, RANK:]
            for e in range(EXAMPLES):
                mask = jnp.where(labels == e, 1.0, 0.0).astype(BF)
                right_h[rows, e * RANK:(e + 1) * RANK] = h * mask
                right_u[rows, e * RANK:(e + 1) * RANK] = u * mask
        begin = FIRST if count == 1 and k not in PARTED else 0
        both = pl.ds(k * PAIR, PAIR)
        for n in range(count + 1):
            at, size = (n * HELD, HELD) if n < count else (split, count * DOWN_ROWS)
            pieces = [columns[k][part, begin + at:begin + at + size, :] for part in range(2)]
            right = (right_h if n < count else right_u)[both, :]
            product = jnp.dot(jnp.concatenate(pieces, axis=1), right, preferred_element_type=F32)
            total[at:at + size, :] = product if k == 0 else total[at:at + size, :] + product
    for n in range(count):
        outs[n][:HELD, :] = total[n * HELD:(n + 1) * HELD, :].astype(BF)
        outs[n][HELD:, :] = total[split + n * DOWN_ROWS:split + (n + 1) * DOWN_ROWS, :].astype(BF)


def partial_call(count, labels, columns, inner):
    return pl.pallas_call(
        functools.partial(partial_kernel, count),
        out_shape=[jax.ShapeDtypeStruct((ROWS, WIDE), BF)] * count,
        in_specs=[VMEM] * 9,
        out_specs=[VMEM] * count,
        scratch_shapes=[
            pltpu.VMEM((1024, WIDE), BF),
            pltpu.VMEM((1024, WIDE), BF),
            pltpu.VMEM((count * ROWS, WIDE), F32),
        ],
        compiler_params=pltpu.CompilerParams(vmem_limit_bytes=24 << 20),
        cost_estimate=pl.CostEstimate(flops=2 * count * ROWS * 1024 * WIDE, bytes_accessed=6 << 20, transcendentals=0),
    )(labels, *columns, *inner)


def feature_kernel(
    own_ref, a_ref, b_ref, c_ref, bounds_ref, select_ref,
    first_up, first_down, second_up, second_down, out_ref, first_ref, second_ref,
):
    for up, down, space in ((first_up, first_down, first_ref), (second_up, second_down, second_ref)):
        space[HELD - 16:HELD, :] = jnp.zeros((16, RANK), F32)
        space[:UP_ROWS, :] = up[...]
        space[HELD:, :] = down[...]
    first = 0.9 * first_ref[...]
    second = 0.999 * second_ref[...]
    select = select_ref[...]
    for e in range(EXAMPLES):
        at = pl.ds(e * RANK, RANK)
        length = (bounds_ref[e + 1] - bounds_ref[e]).astype(F32)
        total = (own_ref[:, at].astype(F32) + a_ref[:, at].astype(F32)) + (b_ref[:, at].astype(F32) + c_ref[:, at].astype(F32))
        grad = total / length
        feature = (first + 0.1 * grad) / (jnp.sqrt(second + 0.001 * grad * grad) + 1e-08)
        high = feature.astype(BF)
        low = (feature - high.astype(F32)).astype(BF)
        out_ref[:, at] = jnp.dot(select, high, preferred_element_type=F32) + jnp.dot(
            select, low, preferred_element_type=F32
        )


EVERY = ("ex", "t1", "t0", "py", "co")


def groups(along_x):
    found = []
    for fixed in range(4):
        for c in range(2):
            for zs in ((0, 1), (2, 3)) if along_x else ((0, 3), (1, 2)):
                found.append(
                    [
                        (((x * 4 + z) * 4) + y) * 2 + c
                        for w in range(4)
                        for z in zs
                        for x, y in [(w, fixed) if along_x else (fixed, w)]
                    ]
                )
    return found


def spread_sum(value, along_x):
    copies = jnp.broadcast_to(value.astype(BF)[None], (8,) + value.shape)
    arrived = lax.all_to_all(
        copies, EVERY, split_axis=0, concat_axis=0, tiled=True, axis_index_groups=groups(along_x)
    )
    return jnp.sum(arrived.astype(F32), axis=0)


def on_device(
    tokens,
    output_gradient,
    adapter_down_factor,
    adapter_up_factor,
    first_moment_down,
    second_moment_down,
    first_moment_up,
    second_moment_up,
    down_row_seeds,
    up_row_seeds,
    segments,
    bank,
):
    turned_grad = output_gradient.T
    give, *mine = pl.pallas_call(
        pack_kernel,
        out_shape=[jax.ShapeDtypeStruct((4, 4 * ROWS, 128), BF)] + [jax.ShapeDtypeStruct((4 * ROWS, 128), BF)] * 4,
        in_specs=[VMEM] * 2,
        out_specs=[VMEM] * 5,
        scratch_shapes=[pltpu.VMEM((2048, 128), BF)],
        compiler_params=pltpu.CompilerParams(vmem_limit_bytes=24 << 20),
        cost_estimate=pl.CostEstimate(flops=0, bytes_accessed=5 << 20, transcendentals=0),
    )(turned_grad, tokens)
    portion = pl.pallas_call(
        product_kernel,
        out_shape=jax.ShapeDtypeStruct((128, PAIR), F32),
        in_specs=[VMEM] * 4,
        out_specs=VMEM,
        compiler_params=pltpu.CompilerParams(vmem_limit_bytes=24 << 20),
        cost_estimate=pl.CostEstimate(flops=2 * 128 * 9440 * 128, bytes_accessed=5 << 20, transcendentals=0),
    )(turned_grad, tokens, adapter_down_factor, adapter_up_factor)
    taken = lax.ppermute(give, "co", [(0, 1), (1, 0)])
    taken, portion = tie(taken, portion)
    first, second = {}, {}
    (first[2],) = fill_call((2,), taken, (mine[2],))
    first[1], second[1], first[3], second[3], first[0] = fill_call((1, 3, 0), taken, (mine[1], mine[3], mine[0]))
    peers = [lax.ppermute(portion, ("t1", "t0"), [(i, (i + shift) % 4) for i in range(4)]) for shift in (2, 1, 3)]
    for k in (2, 1, 3):
        first[k] = send_same(first[k], k)
    whole = ((portion + peers[0]) + (peers[1] + peers[2])).astype(BF)
    sibling = lax.ppermute(whole, "co", [(0, 1), (1, 0)])
    chip_inner = jnp.concatenate([whole, sibling], axis=0)
    inner = [chip_inner, None, None, None]
    for k in (2, 1):
        inner[k] = send_same(chip_inner, k)
    late, first[2] = tie(chip_inner, first[2])
    inner[3] = send_same(late, 3)
    second[1], first[1] = tie(second[1], first[1])
    second[3], first[3] = tie(second[3], first[3])
    for k in PARTED:
        second[k] = send_same(second[k], k)

    labels = segments.reshape(32, 128)
    sums = partial_call(3, labels, [first[k] for k in range(4)], inner)
    arrived = [send_across(sums[k - 1], k) for k in (2, 1, 3)]
    kept = (labels, segments, first_moment_up, second_moment_up, up_row_seeds, down_row_seeds)
    kept, sums = tie(kept, sums)
    labels, segments, first_moment_up, second_moment_up, up_row_seeds, down_row_seeds = kept
    (own,) = partial_call(1, labels, [first[0], second[1], first[2], second[3]], inner)
    own = own.astype(F32)

    bounds = jnp.sum(
        (segments[None, :] < jnp.arange(EXAMPLES + 1, dtype=jnp.int32)[:, None]).astype(jnp.int32), axis=1
    )

    seeds = jnp.concatenate([up_row_seeds[0], jnp.full((HELD - UP_ROWS,), -1, jnp.int32), down_row_seeds[0]])
    select = (jnp.arange(BANK, dtype=jnp.int32)[:, None] == seeds[None, :]).astype(BF)
    blocks = pl.pallas_call(
        feature_kernel,
        out_shape=jax.ShapeDtypeStruct((BANK, WIDE), F32),
        in_specs=[VMEM] * 4 + [SMEM] + [VMEM] * 5,
        out_specs=VMEM,
        scratch_shapes=[pltpu.VMEM((ROWS, RANK), F32), pltpu.VMEM((ROWS, RANK), F32)],
        compiler_params=pltpu.CompilerParams(vmem_limit_bytes=24 << 20),
        cost_estimate=pl.CostEstimate(flops=0, bytes_accessed=3 << 20, transcendentals=0),
    )(
        own, *arrived, bounds, select,
        first_moment_up[0], first_moment_down[0], second_moment_up[0], second_moment_down[0],
    )

    summed = blocks + lax.ppermute(blocks, "co", [(0, 1), (1, 0)])
    summed = spread_sum(summed, False)
    summed = spread_sum(summed, True)
    inverse = 1.0 / math.sqrt((MODEL_WIDTH + HIDDEN_WIDTH) * RANK)
    sketch = jnp.einsum(
        "jer,jrk->ek", summed.reshape(BANK, EXAMPLES, RANK), bank.astype(F32), precision=lax.Precision.HIGHEST
    )
    return sketch * inverse


def solution(mesh):
    rows = ("ex", "py", "co")
    tp = ("t1", "t0")
    split = Mesh(mesh.devices.reshape(4, 2, 2, 4, 2), ("ex", "t1", "t0", "py", "co"))
    return jax.shard_map(
        on_device,
        mesh=split,
        in_specs=(
            P(rows, tp),
            P(rows, tp),
            P(tp, None),
            P(tp, None),
            P(tp, rows, None),
            P(tp, rows, None),
            P(tp, rows, None),
            P(tp, rows, None),
            P(tp, rows),
            P(tp, rows),
            P(),
            P(None, None, ("ex", "t1", "t0", "py", "co")),
        ),
        out_specs=P(None, ("ex", "t1", "t0", "py", "co")),
        check_vma=False,
    )
```

```python
import functools
import math

import jax
import jax.numpy as jnp
from jax import lax
from jax.experimental import pallas as pl
from jax.experimental.pallas import tpu as pltpu
from jax.sharding import Mesh, PartitionSpec as P

MODEL_WIDTH = 8192
HIDDEN_WIDTH = 29568
RANK = 128
BANK = 16
EXAMPLES = 4
UP_ROWS = 231
DOWN_ROWS = 64
WINDOW = 256
HELD = 240
ROWS = HELD + DOWN_ROWS
FIRST = 3 * ROWS
PARTED = (1, 3)
LOCAL_UP = 7392
PAIR = 2 * RANK
WIDE = EXAMPLES * RANK
BF = jnp.bfloat16
F32 = jnp.float32
VMEM = pl.BlockSpec(memory_space=pltpu.VMEM)
ANY = pl.BlockSpec(memory_space=pl.ANY)
SMEM = pl.BlockSpec(memory_space=pltpu.SMEM)
PLANE = ("ex", "py", "co")


def window_start(owner):
    return jnp.minimum((owner * UP_ROWS) // 16 * 16, LOCAL_UP - WINDOW)


def along(position, shift):
    x, y, c = position
    return (x, (y + shift) % 4, 0) if c == 0 else ((x + shift) % 4, y, 1)


def across(position, shift):
    x, y, c = position
    return ((x + shift) % 4, y, 0) if c == 0 else (x, (y + shift) % 4, 1)


def flat(position):
    return position[0] * 8 + position[1] * 2 + position[2]


def pairs(move):
    everyone = [(x, y, c) for x in range(4) for y in range(4) for c in range(2)]
    return [(flat(p), flat(move(p))) for p in everyone]


def send_same(value, shift):
    return lax.ppermute(value, PLANE, pairs(lambda p: along(p, shift)))


def send_across(value, shift):
    return lax.ppermute(value, PLANE, pairs(lambda p: across(p, shift)))


def position():
    return lax.axis_index("ex"), lax.axis_index("py"), lax.axis_index("co")


def tie(value, arrived):
    return lax.optimization_barrier((value, arrived))


def pack_kernel(grad, tokens, *rest):
    give, mine, turned = rest[0], rest[1:5], rest[5]
    x, y, c = position()
    turned[...] = tokens[...].T
    for slot in (2, 6, 1, 5, 3, 7, 0, 4):
        target = 1 - c if slot < 4 else c
        k = slot % 4
        for i in range(4):
            to_x = lax.rem(x + jnp.where(target == 0, i, k), 4)
            to_y = lax.rem(y + jnp.where(target == 0, k, i), 4)
            owner = to_x * 8 + to_y * 2 + target
            start = pl.multiple_of(window_start(owner), 16)
            column = pl.multiple_of(owner * DOWN_ROWS, DOWN_ROWS)
            window_at, down_at = ((i - 1) * HELD, 3 * HELD + (i - 1) * DOWN_ROWS) if i else (FIRST, FIRST + HELD)
            out = give.at[k] if slot < 4 else mine[k]
            window = pltpu.roll(grad[pl.ds(start, WINDOW), :].astype(F32), WINDOW + start - owner * UP_ROWS, 0)
            out[window_at:window_at + HELD, :] = window[:HELD].astype(BF)
            out[down_at:down_at + DOWN_ROWS, :] = turned[pl.ds(column, DOWN_ROWS), :]


def product_kernel(grad, tokens, down, up, portion_ref):
    portion_ref[:, :RANK] = jnp.dot(tokens[...], down[...], preferred_element_type=F32)
    product = jnp.zeros((128, RANK), F32)
    for begin in range(0, LOCAL_UP, 1024):
        end = min(begin + 1024, LOCAL_UP)
        product += lax.dot_general(
            grad[begin:end, :], up[begin:end, :], (((0,), (0,)), ((), ())), preferred_element_type=F32
        )
    portion_ref[:, RANK:] = product


def fill_kernel(shifts, taken_ref, *rest):
    mine, buffers = rest[:len(shifts)], rest[len(shifts):]
    at = 0
    for n, k in enumerate(shifts):
        for begin, size in ((0, FIRST), (FIRST, ROWS)) if k in PARTED else ((0, 4 * ROWS),):
            buffers[at][0] = mine[n][begin:begin + size, :]
            buffers[at][1] = taken_ref[k, begin:begin + size, :]
            at += 1


def fill_call(shifts, taken, mine):
    sizes = [size for k in shifts for size in ((FIRST, ROWS) if k in PARTED else (4 * ROWS,))]
    return pl.pallas_call(
        functools.partial(fill_kernel, shifts),
        out_shape=[jax.ShapeDtypeStruct((2, size, 128), BF) for size in sizes],
        in_specs=[VMEM] * (1 + len(shifts)),
        out_specs=[VMEM] * len(sizes),
        compiler_params=pltpu.CompilerParams(vmem_limit_bytes=16 << 20),
        cost_estimate=pl.CostEstimate(flops=0, bytes_accessed=1 << 20, transcendentals=0),
    )(taken, *mine)


def partial_kernel(count, segments, *rest):
    columns, inner, outs = rest[0:4], rest[4:8], rest[8:8 + count]
    right_h, right_u, total = rest[8 + count:]
    x, y, c = position()
    split = count * HELD
    for k in range(4):
        chip = jnp.where(c == 0, x * 4 + lax.rem(y - k + 4, 4), lax.rem(x - k + 4, 4) * 4 + y)
        for part in range(2):
            labels = segments[pl.ds(2 * chip + jnp.where(part == 0, c, 1 - c), 1), :]
            labels = jnp.broadcast_to(labels.astype(F32), (128, RANK)).T
            rows = pl.ds(k * PAIR + part * 128, 128)
            h = inner[k][part * 128:(part + 1) * 128, :RANK]
            u = inner[k][part * 128:(part + 1) * 128, RANK:]
            for e in range(EXAMPLES):
                mask = jnp.where(labels == e, 1.0, 0.0).astype(BF)
                right_h[rows, e * RANK:(e + 1) * RANK] = h * mask
                right_u[rows, e * RANK:(e + 1) * RANK] = u * mask
        begin = FIRST if count == 1 and k not in PARTED else 0
        both = pl.ds(k * PAIR, PAIR)
        for n in range(count + 1):
            at, size = (n * HELD, HELD) if n < count else (split, count * DOWN_ROWS)
            pieces = [columns[k][part, begin + at:begin + at + size, :] for part in range(2)]
            right = (right_h if n < count else right_u)[both, :]
            product = jnp.dot(jnp.concatenate(pieces, axis=1), right, preferred_element_type=F32)
            total[at:at + size, :] = product if k == 0 else total[at:at + size, :] + product
    for n in range(count):
        outs[n][:HELD, :] = total[n * HELD:(n + 1) * HELD, :].astype(BF)
        outs[n][HELD:, :] = total[split + n * DOWN_ROWS:split + (n + 1) * DOWN_ROWS, :].astype(BF)


def partial_call(count, labels, columns, inner):
    return pl.pallas_call(
        functools.partial(partial_kernel, count),
        out_shape=[jax.ShapeDtypeStruct((ROWS, WIDE), BF)] * count,
        in_specs=[VMEM] * 9,
        out_specs=[VMEM] * count,
        scratch_shapes=[
            pltpu.VMEM((1024, WIDE), BF),
            pltpu.VMEM((1024, WIDE), BF),
            pltpu.VMEM((count * ROWS, WIDE), F32),
        ],
        compiler_params=pltpu.CompilerParams(vmem_limit_bytes=24 << 20),
        cost_estimate=pl.CostEstimate(flops=2 * count * ROWS * 1024 * WIDE, bytes_accessed=6 << 20, transcendentals=0),
    )(labels, *columns, *inner)


def feature_kernel(
    own_ref, a_ref, b_ref, c_ref, bounds_ref, select_ref,
    first_up, first_down, second_up, second_down, out_ref, first_ref, second_ref,
):
    for up, down, space in ((first_up, first_down, first_ref), (second_up, second_down, second_ref)):
        space[HELD - 16:HELD, :] = jnp.zeros((16, RANK), F32)
        space[:UP_ROWS, :] = up[...]
        space[HELD:, :] = down[...]
    first = 0.9 * first_ref[...]
    second = 0.999 * second_ref[...]
    select = select_ref[...]
    for e in range(EXAMPLES):
        at = pl.ds(e * RANK, RANK)
        length = (bounds_ref[e + 1] - bounds_ref[e]).astype(F32)
        total = (own_ref[:, at].astype(F32) + a_ref[:, at].astype(F32)) + (b_ref[:, at].astype(F32) + c_ref[:, at].astype(F32))
        grad = total / length
        feature = (first + 0.1 * grad) / (jnp.sqrt(second + 0.001 * grad * grad) + 1e-08)
        high = feature.astype(BF)
        low = (feature - high.astype(F32)).astype(BF)
        out_ref[:, at] = jnp.dot(select, high, preferred_element_type=F32) + jnp.dot(
            select, low, preferred_element_type=F32
        )


EVERY = ("ex", "t1", "t0", "py", "co")


def groups(along_x):
    found = []
    for fixed in range(4):
        for c in range(2):
            for zs in ((0, 1), (2, 3)) if along_x else ((0, 3), (1, 2)):
                found.append(
                    [
                        (((x * 4 + z) * 4) + y) * 2 + c
                        for w in range(4)
                        for z in zs
                        for x, y in [(w, fixed) if along_x else (fixed, w)]
                    ]
                )
    return found


def spread(value, along_x):
    copies = jnp.broadcast_to(value[None], (8,) + value.shape)
    return lax.all_to_all(
        copies, EVERY, split_axis=0, concat_axis=0, tiled=True, axis_index_groups=groups(along_x)
    )


def sketch_kernel(arrived_ref, bank_ref, out_ref):
    summed = arrived_ref[0].astype(F32)
    for i in range(1, 8):
        summed = summed + arrived_ref[i].astype(F32)
    total = jnp.zeros((2 * EXAMPLES, bank_ref.shape[1]), F32)
    for j in range(BANK):
        rows = jnp.concatenate([summed[j:j + 1, e * RANK:(e + 1) * RANK] for e in range(EXAMPLES)], axis=0)
        high = rows.astype(BF).astype(F32)
        left = jnp.concatenate([high, rows - high], axis=0).astype(BF)
        total += lax.dot_general(left, bank_ref[j], (((1,), (1,)), ((), ())), preferred_element_type=F32)
    inverse = 1.0 / math.sqrt((MODEL_WIDTH + HIDDEN_WIDTH) * RANK)
    out_ref[...] = (total[:EXAMPLES] + total[EXAMPLES:]) * inverse


def on_device(
    tokens,
    output_gradient,
    adapter_down_factor,
    adapter_up_factor,
    first_moment_down,
    second_moment_down,
    first_moment_up,
    second_moment_up,
    down_row_seeds,
    up_row_seeds,
    segments,
    bank,
):
    turned_grad = output_gradient.T
    give, *mine = pl.pallas_call(
        pack_kernel,
        out_shape=[jax.ShapeDtypeStruct((4, 4 * ROWS, 128), BF)] + [jax.ShapeDtypeStruct((4 * ROWS, 128), BF)] * 4,
        in_specs=[VMEM] * 2,
        out_specs=[VMEM] * 5,
        scratch_shapes=[pltpu.VMEM((2048, 128), BF)],
        compiler_params=pltpu.CompilerParams(vmem_limit_bytes=24 << 20),
        cost_estimate=pl.CostEstimate(flops=0, bytes_accessed=5 << 20, transcendentals=0),
    )(turned_grad, tokens)
    portion = pl.pallas_call(
        product_kernel,
        out_shape=jax.ShapeDtypeStruct((128, PAIR), F32),
        in_specs=[VMEM] * 4,
        out_specs=VMEM,
        compiler_params=pltpu.CompilerParams(vmem_limit_bytes=24 << 20),
        cost_estimate=pl.CostEstimate(flops=2 * 128 * 9440 * 128, bytes_accessed=5 << 20, transcendentals=0),
    )(turned_grad, tokens, adapter_down_factor, adapter_up_factor)
    taken = lax.ppermute(give, "co", [(0, 1), (1, 0)])
    taken, portion = tie(taken, portion)
    first, second = {}, {}
    (first[2],) = fill_call((2,), taken, (mine[2],))
    first[1], second[1], first[3], second[3], first[0] = fill_call((1, 3, 0), taken, (mine[1], mine[3], mine[0]))
    peers = [lax.ppermute(portion, ("t1", "t0"), [(i, (i + shift) % 4) for i in range(4)]) for shift in (2, 1, 3)]
    for k in (2, 1, 3):
        first[k] = send_same(first[k], k)
    whole = ((portion + peers[0]) + (peers[1] + peers[2])).astype(BF)
    sibling = lax.ppermute(whole, "co", [(0, 1), (1, 0)])
    chip_inner = jnp.concatenate([whole, sibling], axis=0)
    inner = [chip_inner, None, None, None]
    for k in (2, 1):
        inner[k] = send_same(chip_inner, k)
    late, first[2] = tie(chip_inner, first[2])
    inner[3] = send_same(late, 3)
    second[1], first[1] = tie(second[1], first[1])
    second[3], first[3] = tie(second[3], first[3])
    for k in PARTED:
        second[k] = send_same(second[k], k)

    labels = segments.reshape(32, 128)
    sums = partial_call(3, labels, [first[k] for k in range(4)], inner)
    arrived = [send_across(sums[k - 1], k) for k in (2, 1, 3)]
    kept = (labels, segments, first_moment_up, second_moment_up, up_row_seeds, down_row_seeds)
    kept, sums = tie(kept, sums)
    labels, segments, first_moment_up, second_moment_up, up_row_seeds, down_row_seeds = kept
    (own,) = partial_call(1, labels, [first[0], second[1], first[2], second[3]], inner)
    own = own.astype(F32)

    bounds = jnp.sum(
        (segments[None, :] < jnp.arange(EXAMPLES + 1, dtype=jnp.int32)[:, None]).astype(jnp.int32), axis=1
    )

    seeds = jnp.concatenate([up_row_seeds[0], jnp.full((HELD - UP_ROWS,), -1, jnp.int32), down_row_seeds[0]])
    select = (jnp.arange(BANK, dtype=jnp.int32)[:, None] == seeds[None, :]).astype(BF)
    blocks = pl.pallas_call(
        feature_kernel,
        out_shape=jax.ShapeDtypeStruct((BANK, WIDE), F32),
        in_specs=[VMEM] * 4 + [SMEM] + [VMEM] * 5,
        out_specs=VMEM,
        scratch_shapes=[pltpu.VMEM((ROWS, RANK), F32), pltpu.VMEM((ROWS, RANK), F32)],
        compiler_params=pltpu.CompilerParams(vmem_limit_bytes=24 << 20),
        cost_estimate=pl.CostEstimate(flops=0, bytes_accessed=3 << 20, transcendentals=0),
    )(
        own, *arrived, bounds, select,
        first_moment_up[0], first_moment_down[0], second_moment_up[0], second_moment_down[0],
    )

    summed = blocks + lax.ppermute(blocks, "co", [(0, 1), (1, 0)])
    summed = jnp.sum(spread(summed, False), axis=0)
    arrived = spread(summed.astype(F32), True)
    return pl.pallas_call(
        sketch_kernel,
        out_shape=jax.ShapeDtypeStruct((EXAMPLES, bank.shape[2]), F32),
        in_specs=[VMEM] * 2,
        out_specs=VMEM,
        compiler_params=pltpu.CompilerParams(vmem_limit_bytes=24 << 20),
        cost_estimate=pl.CostEstimate(flops=1 << 22, bytes_accessed=1 << 20, transcendentals=0),
    )(arrived, jnp.transpose(bank, (0, 2, 1)))


def solution(mesh):
    rows = ("ex", "py", "co")
    tp = ("t1", "t0")
    split = Mesh(mesh.devices.reshape(4, 2, 2, 4, 2), ("ex", "t1", "t0", "py", "co"))
    return jax.shard_map(
        on_device,
        mesh=split,
        in_specs=(
            P(rows, tp),
            P(rows, tp),
            P(tp, None),
            P(tp, None),
            P(tp, rows, None),
            P(tp, rows, None),
            P(tp, rows, None),
            P(tp, rows, None),
            P(tp, rows),
            P(tp, rows),
            P(),
            P(None, None, ("ex", "t1", "t0", "py", "co")),
        ),
        out_specs=P(None, ("ex", "t1", "t0", "py", "co")),
        check_vma=False,
    )
```

```python
import functools
import math

import jax
import jax.numpy as jnp
from jax import lax
from jax.experimental import pallas as pl
from jax.experimental.pallas import tpu as pltpu
from jax.sharding import Mesh, PartitionSpec as P

MODEL_WIDTH = 8192
HIDDEN_WIDTH = 29568
RANK = 128
BANK = 16
EXAMPLES = 4
UP_ROWS = 231
DOWN_ROWS = 64
WINDOW = 256
HELD = 240
ROWS = HELD + DOWN_ROWS
FIRST = 3 * ROWS
PARTED = (1, 3)
LOCAL_UP = 7392
PAIR = 2 * RANK
WIDE = EXAMPLES * RANK
BF = jnp.bfloat16
F32 = jnp.float32
VMEM = pl.BlockSpec(memory_space=pltpu.VMEM)
ANY = pl.BlockSpec(memory_space=pl.ANY)
SMEM = pl.BlockSpec(memory_space=pltpu.SMEM)
PLANE = ("ex", "py", "co")


def window_start(owner):
    return jnp.minimum((owner * UP_ROWS) // 16 * 16, LOCAL_UP - WINDOW)


def along(position, shift):
    x, y, c = position
    return (x, (y + shift) % 4, 0) if c == 0 else ((x + shift) % 4, y, 1)


def across(position, shift):
    x, y, c = position
    return ((x + shift) % 4, y, 0) if c == 0 else (x, (y + shift) % 4, 1)


def flat(position):
    return position[0] * 8 + position[1] * 2 + position[2]


def pairs(move):
    everyone = [(x, y, c) for x in range(4) for y in range(4) for c in range(2)]
    return [(flat(p), flat(move(p))) for p in everyone]


def send_same(value, shift):
    return lax.ppermute(value, PLANE, pairs(lambda p: along(p, shift)))


def send_across(value, shift):
    return lax.ppermute(value, PLANE, pairs(lambda p: across(p, shift)))


def position():
    return lax.axis_index("ex"), lax.axis_index("py"), lax.axis_index("co")


def tie(value, arrived):
    return lax.optimization_barrier((value, arrived))


def pack_kernel(grad, turned, *rest):
    give, mine = rest[0], rest[1:5]
    x, y, c = position()
    for slot in (2, 6, 1, 5, 3, 7, 0, 4):
        target = 1 - c if slot < 4 else c
        k = slot % 4
        for i in range(4):
            to_x = lax.rem(x + jnp.where(target == 0, i, k), 4)
            to_y = lax.rem(y + jnp.where(target == 0, k, i), 4)
            owner = to_x * 8 + to_y * 2 + target
            start = pl.multiple_of(window_start(owner), 16)
            column = pl.multiple_of(owner * DOWN_ROWS, DOWN_ROWS)
            window_at, down_at = ((i - 1) * HELD, 3 * HELD + (i - 1) * DOWN_ROWS) if i else (FIRST, FIRST + HELD)
            out = give.at[k] if slot < 4 else mine[k]
            window = pltpu.roll(grad[pl.ds(start, WINDOW), :].astype(F32), WINDOW + start - owner * UP_ROWS, 0)
            out[window_at:window_at + HELD, :] = window[:HELD].astype(BF)
            out[down_at:down_at + DOWN_ROWS, :] = turned[pl.ds(column, DOWN_ROWS), :]


def product_kernel(grad, tokens, down, up, portion_ref):
    portion_ref[:, :RANK] = jnp.dot(tokens[...], down[...], preferred_element_type=F32)
    product = jnp.zeros((128, RANK), F32)
    for begin in range(0, LOCAL_UP, 1024):
        end = min(begin + 1024, LOCAL_UP)
        product += lax.dot_general(
            grad[begin:end, :], up[begin:end, :], (((0,), (0,)), ((), ())), preferred_element_type=F32
        )
    portion_ref[:, RANK:] = product


def fill_kernel(shifts, taken_ref, *rest):
    mine, buffers = rest[:len(shifts)], rest[len(shifts):]
    at = 0
    for n, k in enumerate(shifts):
        for begin, size in ((0, FIRST), (FIRST, ROWS)) if k in PARTED else ((0, 4 * ROWS),):
            buffers[at][0] = mine[n][begin:begin + size, :]
            buffers[at][1] = taken_ref[k, begin:begin + size, :]
            at += 1


def fill_call(shifts, taken, mine):
    sizes = [size for k in shifts for size in ((FIRST, ROWS) if k in PARTED else (4 * ROWS,))]
    return pl.pallas_call(
        functools.partial(fill_kernel, shifts),
        out_shape=[jax.ShapeDtypeStruct((2, size, 128), BF) for size in sizes],
        in_specs=[VMEM] * (1 + len(shifts)),
        out_specs=[VMEM] * len(sizes),
        compiler_params=pltpu.CompilerParams(vmem_limit_bytes=16 << 20),
        cost_estimate=pl.CostEstimate(flops=0, bytes_accessed=1 << 20, transcendentals=0),
    )(taken, *mine)


def partial_kernel(count, segments, *rest):
    columns, inner, outs = rest[0:4], rest[4:8], rest[8:8 + count]
    right_h, right_u, total = rest[8 + count:]
    x, y, c = position()
    split = count * HELD
    for k in range(4):
        chip = jnp.where(c == 0, x * 4 + lax.rem(y - k + 4, 4), lax.rem(x - k + 4, 4) * 4 + y)
        for part in range(2):
            labels = segments[pl.ds(2 * chip + jnp.where(part == 0, c, 1 - c), 1), :]
            labels = jnp.broadcast_to(labels.astype(F32), (128, RANK)).T
            rows = pl.ds(k * PAIR + part * 128, 128)
            h = inner[k][part * 128:(part + 1) * 128, :RANK]
            u = inner[k][part * 128:(part + 1) * 128, RANK:]
            for e in range(EXAMPLES):
                mask = jnp.where(labels == e, 1.0, 0.0).astype(BF)
                right_h[rows, e * RANK:(e + 1) * RANK] = h * mask
                right_u[rows, e * RANK:(e + 1) * RANK] = u * mask
        begin = FIRST if count == 1 and k not in PARTED else 0
        both = pl.ds(k * PAIR, PAIR)
        for n in range(count + 1):
            at, size = (n * HELD, HELD) if n < count else (split, count * DOWN_ROWS)
            pieces = [columns[k][part, begin + at:begin + at + size, :] for part in range(2)]
            right = (right_h if n < count else right_u)[both, :]
            product = jnp.dot(jnp.concatenate(pieces, axis=1), right, preferred_element_type=F32)
            total[at:at + size, :] = product if k == 0 else total[at:at + size, :] + product
    for n in range(count):
        outs[n][:HELD, :] = total[n * HELD:(n + 1) * HELD, :].astype(BF)
        outs[n][HELD:, :] = total[split + n * DOWN_ROWS:split + (n + 1) * DOWN_ROWS, :].astype(BF)


def partial_call(count, labels, columns, inner):
    return pl.pallas_call(
        functools.partial(partial_kernel, count),
        out_shape=[jax.ShapeDtypeStruct((ROWS, WIDE), BF)] * count,
        in_specs=[VMEM] * 9,
        out_specs=[VMEM] * count,
        scratch_shapes=[
            pltpu.VMEM((1024, WIDE), BF),
            pltpu.VMEM((1024, WIDE), BF),
            pltpu.VMEM((count * ROWS, WIDE), F32),
        ],
        compiler_params=pltpu.CompilerParams(vmem_limit_bytes=24 << 20),
        cost_estimate=pl.CostEstimate(flops=2 * count * ROWS * 1024 * WIDE, bytes_accessed=6 << 20, transcendentals=0),
    )(labels, *columns, *inner)


def feature_kernel(
    own_ref, a_ref, b_ref, c_ref, bounds_ref, select_ref,
    first_up, first_down, second_up, second_down, out_ref, first_ref, second_ref,
):
    for up, down, space in ((first_up, first_down, first_ref), (second_up, second_down, second_ref)):
        space[HELD - 16:HELD, :] = jnp.zeros((16, RANK), F32)
        space[:UP_ROWS, :] = up[...]
        space[HELD:, :] = down[...]
    first = 0.9 * first_ref[...]
    second = 0.999 * second_ref[...]
    select = select_ref[...]
    for e in range(EXAMPLES):
        at = pl.ds(e * RANK, RANK)
        length = (bounds_ref[e + 1] - bounds_ref[e]).astype(F32)
        total = (own_ref[:, at].astype(F32) + a_ref[:, at].astype(F32)) + (b_ref[:, at].astype(F32) + c_ref[:, at].astype(F32))
        grad = total / length
        feature = (first + 0.1 * grad) / (jnp.sqrt(second + 0.001 * grad * grad) + 1e-08)
        high = feature.astype(BF)
        low = (feature - high.astype(F32)).astype(BF)
        out_ref[:, at] = jnp.dot(select, high, preferred_element_type=F32) + jnp.dot(
            select, low, preferred_element_type=F32
        )


EVERY = ("ex", "t1", "t0", "py", "co")


def groups(along_x):
    found = []
    for fixed in range(4):
        for c in range(2):
            for zs in ((0, 1), (2, 3)) if along_x else ((0, 3), (1, 2)):
                found.append(
                    [
                        (((x * 4 + z) * 4) + y) * 2 + c
                        for w in range(4)
                        for z in zs
                        for x, y in [(w, fixed) if along_x else (fixed, w)]
                    ]
                )
    return found


def spread(value, along_x):
    copies = jnp.broadcast_to(value[None], (8,) + value.shape)
    return lax.all_to_all(
        copies, EVERY, split_axis=0, concat_axis=0, tiled=True, axis_index_groups=groups(along_x)
    )


def sketch_kernel(arrived_ref, bank_ref, out_ref):
    summed = arrived_ref[0].astype(F32)
    for i in range(1, 8):
        summed = summed + arrived_ref[i].astype(F32)
    total = jnp.zeros((2 * EXAMPLES, bank_ref.shape[1]), F32)
    for j in range(BANK):
        rows = jnp.concatenate([summed[j:j + 1, e * RANK:(e + 1) * RANK] for e in range(EXAMPLES)], axis=0)
        high = rows.astype(BF).astype(F32)
        left = jnp.concatenate([high, rows - high], axis=0).astype(BF)
        total += lax.dot_general(left, bank_ref[j], (((1,), (1,)), ((), ())), preferred_element_type=F32)
    inverse = 1.0 / math.sqrt((MODEL_WIDTH + HIDDEN_WIDTH) * RANK)
    out_ref[...] = (total[:EXAMPLES] + total[EXAMPLES:]) * inverse


def on_device(
    tokens,
    output_gradient,
    adapter_down_factor,
    adapter_up_factor,
    first_moment_down,
    second_moment_down,
    first_moment_up,
    second_moment_up,
    down_row_seeds,
    up_row_seeds,
    segments,
    bank,
):
    turned_grad = output_gradient.T
    give, *mine = pl.pallas_call(
        pack_kernel,
        out_shape=[jax.ShapeDtypeStruct((4, 4 * ROWS, 128), BF)] + [jax.ShapeDtypeStruct((4 * ROWS, 128), BF)] * 4,
        in_specs=[VMEM] * 2,
        out_specs=[VMEM] * 5,
        compiler_params=pltpu.CompilerParams(vmem_limit_bytes=24 << 20),
        cost_estimate=pl.CostEstimate(flops=0, bytes_accessed=5 << 20, transcendentals=0),
    )(turned_grad, tokens.T)
    portion = pl.pallas_call(
        product_kernel,
        out_shape=jax.ShapeDtypeStruct((128, PAIR), F32),
        in_specs=[VMEM] * 4,
        out_specs=VMEM,
        compiler_params=pltpu.CompilerParams(vmem_limit_bytes=24 << 20),
        cost_estimate=pl.CostEstimate(flops=2 * 128 * 9440 * 128, bytes_accessed=5 << 20, transcendentals=0),
    )(turned_grad, tokens, adapter_down_factor, adapter_up_factor)
    taken = lax.ppermute(give, "co", [(0, 1), (1, 0)])
    taken, portion = tie(taken, portion)
    first, second = {}, {}
    (first[2],) = fill_call((2,), taken, (mine[2],))
    first[1], second[1], first[3], second[3], first[0] = fill_call((1, 3, 0), taken, (mine[1], mine[3], mine[0]))
    peers = [lax.ppermute(portion, ("t1", "t0"), [(i, (i + shift) % 4) for i in range(4)]) for shift in (2, 1, 3)]
    for k in (2, 1, 3):
        first[k] = send_same(first[k], k)
    whole = ((portion + peers[0]) + (peers[1] + peers[2])).astype(BF)
    sibling = lax.ppermute(whole, "co", [(0, 1), (1, 0)])
    chip_inner = jnp.concatenate([whole, sibling], axis=0)
    inner = [chip_inner, None, None, None]
    for k in (2, 1):
        inner[k] = send_same(chip_inner, k)
    late, first[2] = tie(chip_inner, first[2])
    inner[3] = send_same(late, 3)
    second[1], first[1] = tie(second[1], first[1])
    second[3], first[3] = tie(second[3], first[3])
    for k in PARTED:
        second[k] = send_same(second[k], k)

    labels = segments.reshape(32, 128)
    sums = partial_call(3, labels, [first[k] for k in range(4)], inner)
    arrived = [send_across(sums[k - 1], k) for k in (2, 1, 3)]
    kept = (labels, segments, first_moment_up, second_moment_up, up_row_seeds, down_row_seeds)
    kept, sums = tie(kept, sums)
    labels, segments, first_moment_up, second_moment_up, up_row_seeds, down_row_seeds = kept
    (own,) = partial_call(1, labels, [first[0], second[1], first[2], second[3]], inner)
    own = own.astype(F32)

    bounds = jnp.sum(
        (segments[None, :] < jnp.arange(EXAMPLES + 1, dtype=jnp.int32)[:, None]).astype(jnp.int32), axis=1
    )

    seeds = jnp.concatenate([up_row_seeds[0], jnp.full((HELD - UP_ROWS,), -1, jnp.int32), down_row_seeds[0]])
    select = (jnp.arange(BANK, dtype=jnp.int32)[:, None] == seeds[None, :]).astype(BF)
    blocks = pl.pallas_call(
        feature_kernel,
        out_shape=jax.ShapeDtypeStruct((BANK, WIDE), F32),
        in_specs=[VMEM] * 4 + [SMEM] + [VMEM] * 5,
        out_specs=VMEM,
        scratch_shapes=[pltpu.VMEM((ROWS, RANK), F32), pltpu.VMEM((ROWS, RANK), F32)],
        compiler_params=pltpu.CompilerParams(vmem_limit_bytes=24 << 20),
        cost_estimate=pl.CostEstimate(flops=0, bytes_accessed=3 << 20, transcendentals=0),
    )(
        own, *arrived, bounds, select,
        first_moment_up[0], first_moment_down[0], second_moment_up[0], second_moment_down[0],
    )

    summed = blocks + lax.ppermute(blocks, "co", [(0, 1), (1, 0)])
    summed = jnp.sum(spread(summed, False), axis=0)
    arrived = spread(summed.astype(F32), True)
    return pl.pallas_call(
        sketch_kernel,
        out_shape=jax.ShapeDtypeStruct((EXAMPLES, bank.shape[2]), F32),
        in_specs=[VMEM] * 2,
        out_specs=VMEM,
        compiler_params=pltpu.CompilerParams(vmem_limit_bytes=24 << 20),
        cost_estimate=pl.CostEstimate(flops=1 << 22, bytes_accessed=1 << 20, transcendentals=0),
    )(arrived, jnp.transpose(bank, (0, 2, 1)))


def solution(mesh):
    rows = ("ex", "py", "co")
    tp = ("t1", "t0")
    split = Mesh(mesh.devices.reshape(4, 2, 2, 4, 2), ("ex", "t1", "t0", "py", "co"))
    return jax.shard_map(
        on_device,
        mesh=split,
        in_specs=(
            P(rows, tp),
            P(rows, tp),
            P(tp, None),
            P(tp, None),
            P(tp, rows, None),
            P(tp, rows, None),
            P(tp, rows, None),
            P(tp, rows, None),
            P(tp, rows),
            P(tp, rows),
            P(),
            P(None, None, ("ex", "t1", "t0", "py", "co")),
        ),
        out_specs=P(None, ("ex", "t1", "t0", "py", "co")),
        check_vma=False,
    )
```

```python
import functools
import math

import jax
import jax.numpy as jnp
from jax import lax
from jax.experimental import pallas as pl
from jax.experimental.pallas import tpu as pltpu
from jax.sharding import Mesh, PartitionSpec as P

MODEL_WIDTH = 8192
HIDDEN_WIDTH = 29568
RANK = 128
BANK = 16
EXAMPLES = 4
UP_ROWS = 231
DOWN_ROWS = 64
WINDOW = 256
HELD = 240
ROWS = HELD + DOWN_ROWS
FIRST = 3 * ROWS
PARTED = (1, 3)
LOCAL_UP = 7392
PAIR = 2 * RANK
WIDE = EXAMPLES * RANK
BF = jnp.bfloat16
F32 = jnp.float32
VMEM = pl.BlockSpec(memory_space=pltpu.VMEM)
ANY = pl.BlockSpec(memory_space=pl.ANY)
SMEM = pl.BlockSpec(memory_space=pltpu.SMEM)
PLANE = ("ex", "py", "co")


def window_start(owner):
    return jnp.minimum((owner * UP_ROWS) // 16 * 16, LOCAL_UP - WINDOW)


def along(position, shift):
    x, y, c = position
    return (x, (y + shift) % 4, 0) if c == 0 else ((x + shift) % 4, y, 1)


def across(position, shift):
    x, y, c = position
    return ((x + shift) % 4, y, 0) if c == 0 else (x, (y + shift) % 4, 1)


def flat(position):
    return position[0] * 8 + position[1] * 2 + position[2]


def pairs(move):
    everyone = [(x, y, c) for x in range(4) for y in range(4) for c in range(2)]
    return [(flat(p), flat(move(p))) for p in everyone]


def send_same(value, shift):
    return lax.ppermute(value, PLANE, pairs(lambda p: along(p, shift)))


def send_across(value, shift):
    return lax.ppermute(value, PLANE, pairs(lambda p: across(p, shift)))


def position():
    return lax.axis_index("ex"), lax.axis_index("py"), lax.axis_index("co")


def tie(value, arrived):
    return lax.optimization_barrier((value, arrived))


def pack_kernel(grad, turned, *rest):
    give, mine = rest[0], rest[1:5]
    x, y, c = position()
    for slot in (2, 6, 1, 5, 3, 7, 0, 4):
        target = 1 - c if slot < 4 else c
        k = slot % 4
        for i in range(4):
            to_x = lax.rem(x + jnp.where(target == 0, i, k), 4)
            to_y = lax.rem(y + jnp.where(target == 0, k, i), 4)
            owner = to_x * 8 + to_y * 2 + target
            start = pl.multiple_of(window_start(owner), 16)
            column = pl.multiple_of(owner * DOWN_ROWS, DOWN_ROWS)
            window_at, down_at = ((i - 1) * HELD, 3 * HELD + (i - 1) * DOWN_ROWS) if i else (FIRST, FIRST + HELD)
            out = give.at[k] if slot < 4 else mine[k]
            window = pltpu.roll(grad[pl.ds(start, WINDOW), :].astype(F32), WINDOW + start - owner * UP_ROWS, 0)
            out[window_at:window_at + HELD, :] = window[:HELD].astype(BF)
            out[down_at:down_at + DOWN_ROWS, :] = turned[pl.ds(column, DOWN_ROWS), :]


def product_kernel(grad, tokens, down, up, portion_ref):
    portion_ref[:, :RANK] = jnp.dot(tokens[...], down[...], preferred_element_type=F32)
    product = jnp.zeros((128, RANK), F32)
    for begin in range(0, LOCAL_UP, 1024):
        end = min(begin + 1024, LOCAL_UP)
        product += lax.dot_general(
            grad[begin:end, :], up[begin:end, :], (((0,), (0,)), ((), ())), preferred_element_type=F32
        )
    portion_ref[:, RANK:] = product


def fill_kernel(shifts, taken_ref, *rest):
    mine, buffers = rest[:len(shifts)], rest[len(shifts):]
    at = 0
    for n, k in enumerate(shifts):
        for begin, size in ((0, FIRST), (FIRST, ROWS)) if k in PARTED else ((0, 4 * ROWS),):
            buffers[at][0] = mine[n][begin:begin + size, :]
            buffers[at][1] = taken_ref[k, begin:begin + size, :]
            at += 1


def fill_call(shifts, taken, mine):
    sizes = [size for k in shifts for size in ((FIRST, ROWS) if k in PARTED else (4 * ROWS,))]
    return pl.pallas_call(
        functools.partial(fill_kernel, shifts),
        out_shape=[jax.ShapeDtypeStruct((2, size, 128), BF) for size in sizes],
        in_specs=[VMEM] * (1 + len(shifts)),
        out_specs=[VMEM] * len(sizes),
        compiler_params=pltpu.CompilerParams(vmem_limit_bytes=16 << 20),
        cost_estimate=pl.CostEstimate(flops=0, bytes_accessed=1 << 20, transcendentals=0),
    )(taken, *mine)


def partial_kernel(count, segments, *rest):
    columns, inner, outs = rest[0:4], rest[4:8], rest[8:8 + count]
    right_h, right_u, total = rest[8 + count:]
    x, y, c = position()
    split = count * HELD
    for k in range(4):
        chip = jnp.where(c == 0, x * 4 + lax.rem(y - k + 4, 4), lax.rem(x - k + 4, 4) * 4 + y)
        for part in range(2):
            labels = segments[pl.ds(2 * chip + jnp.where(part == 0, c, 1 - c), 1), :]
            labels = jnp.broadcast_to(labels.astype(F32), (128, RANK)).T
            rows = pl.ds(k * PAIR + part * 128, 128)
            h = inner[k][part * 128:(part + 1) * 128, :RANK]
            u = inner[k][part * 128:(part + 1) * 128, RANK:]
            for e in range(EXAMPLES):
                mask = jnp.where(labels == e, 1.0, 0.0).astype(BF)
                right_h[rows, e * RANK:(e + 1) * RANK] = h * mask
                right_u[rows, e * RANK:(e + 1) * RANK] = u * mask
        begin = FIRST if count == 1 and k not in PARTED else 0
        both = pl.ds(k * PAIR, PAIR)
        for n in range(count + 1):
            at, size = (n * HELD, HELD) if n < count else (split, count * DOWN_ROWS)
            pieces = [columns[k][part, begin + at:begin + at + size, :] for part in range(2)]
            right = (right_h if n < count else right_u)[both, :]
            product = jnp.dot(jnp.concatenate(pieces, axis=1), right, preferred_element_type=F32)
            total[at:at + size, :] = product if k == 0 else total[at:at + size, :] + product
    for n in range(count):
        outs[n][:HELD, :] = total[n * HELD:(n + 1) * HELD, :].astype(BF)
        outs[n][HELD:, :] = total[split + n * DOWN_ROWS:split + (n + 1) * DOWN_ROWS, :].astype(BF)


def partial_call(count, labels, columns, inner):
    return pl.pallas_call(
        functools.partial(partial_kernel, count),
        out_shape=[jax.ShapeDtypeStruct((ROWS, WIDE), BF)] * count,
        in_specs=[VMEM] * 9,
        out_specs=[VMEM] * count,
        scratch_shapes=[
            pltpu.VMEM((1024, WIDE), BF),
            pltpu.VMEM((1024, WIDE), BF),
            pltpu.VMEM((count * ROWS, WIDE), F32),
        ],
        compiler_params=pltpu.CompilerParams(vmem_limit_bytes=24 << 20),
        cost_estimate=pl.CostEstimate(flops=2 * count * ROWS * 1024 * WIDE, bytes_accessed=6 << 20, transcendentals=0),
    )(labels, *columns, *inner)


def feature_kernel(
    own_ref, a_ref, b_ref, c_ref, bounds_ref, select_ref,
    first_up, first_down, second_up, second_down, out_ref, first_ref, second_ref,
):
    for up, down, space in ((first_up, first_down, first_ref), (second_up, second_down, second_ref)):
        space[HELD - 16:HELD, :] = jnp.zeros((16, RANK), F32)
        space[:UP_ROWS, :] = up[...]
        space[HELD:, :] = down[...]
    first = 0.9 * first_ref[...]
    second = 0.999 * second_ref[...]
    select = select_ref[...]
    for e in range(EXAMPLES):
        at = pl.ds(e * RANK, RANK)
        length = (bounds_ref[e + 1] - bounds_ref[e]).astype(F32)
        total = (own_ref[:, at].astype(F32) + a_ref[:, at].astype(F32)) + (b_ref[:, at].astype(F32) + c_ref[:, at].astype(F32))
        grad = total / length
        feature = (first + 0.1 * grad) / (jnp.sqrt(second + 0.001 * grad * grad) + 1e-08)
        high = feature.astype(BF)
        low = (feature - high.astype(F32)).astype(BF)
        out_ref[:, at] = jnp.dot(select, high, preferred_element_type=F32) + jnp.dot(
            select, low, preferred_element_type=F32
        )


EVERY = ("ex", "t1", "t0", "py", "co")


def groups(along_x):
    found = []
    for fixed in range(4):
        for c in range(2):
            for zs in ((0, 1), (2, 3)) if along_x else ((0, 3), (1, 2)):
                found.append(
                    [
                        (((x * 4 + z) * 4) + y) * 2 + c
                        for w in range(4)
                        for z in zs
                        for x, y in [(w, fixed) if along_x else (fixed, w)]
                    ]
                )
    return found


def spread(value, along_x):
    copies = jnp.broadcast_to(value[None], (8,) + value.shape)
    return lax.all_to_all(
        copies, EVERY, split_axis=0, concat_axis=0, tiled=True, axis_index_groups=groups(along_x)
    )


def sketch_kernel(arrived_ref, bank_ref, out_ref):
    summed = arrived_ref[0].astype(F32)
    for i in range(1, 8):
        summed = summed + arrived_ref[i].astype(F32)
    total = jnp.zeros((2 * EXAMPLES, bank_ref.shape[1]), F32)
    for j in range(BANK):
        rows = jnp.concatenate([summed[j:j + 1, e * RANK:(e + 1) * RANK] for e in range(EXAMPLES)], axis=0)
        high = rows.astype(BF).astype(F32)
        left = jnp.concatenate([high, rows - high], axis=0).astype(BF)
        total += lax.dot_general(left, bank_ref[j], (((1,), (1,)), ((), ())), preferred_element_type=F32)
    inverse = 1.0 / math.sqrt((MODEL_WIDTH + HIDDEN_WIDTH) * RANK)
    out_ref[...] = (total[:EXAMPLES] + total[EXAMPLES:]) * inverse


def on_device(
    tokens,
    output_gradient,
    adapter_down_factor,
    adapter_up_factor,
    first_moment_down,
    second_moment_down,
    first_moment_up,
    second_moment_up,
    down_row_seeds,
    up_row_seeds,
    segments,
    bank,
):
    turned_grad = output_gradient.T
    give, *mine = pl.pallas_call(
        pack_kernel,
        out_shape=[jax.ShapeDtypeStruct((4, 4 * ROWS, 128), BF)] + [jax.ShapeDtypeStruct((4 * ROWS, 128), BF)] * 4,
        in_specs=[VMEM] * 2,
        out_specs=[VMEM] * 5,
        compiler_params=pltpu.CompilerParams(vmem_limit_bytes=24 << 20),
        cost_estimate=pl.CostEstimate(flops=0, bytes_accessed=5 << 20, transcendentals=0),
    )(turned_grad, tokens.T)
    portion = pl.pallas_call(
        product_kernel,
        out_shape=jax.ShapeDtypeStruct((128, PAIR), F32),
        in_specs=[VMEM] * 4,
        out_specs=VMEM,
        compiler_params=pltpu.CompilerParams(vmem_limit_bytes=24 << 20),
        cost_estimate=pl.CostEstimate(flops=2 * 128 * 9440 * 128, bytes_accessed=5 << 20, transcendentals=0),
    )(turned_grad, tokens, adapter_down_factor, adapter_up_factor)
    taken = lax.ppermute(give, "co", [(0, 1), (1, 0)])
    taken, portion = tie(taken, portion)
    first, second = {}, {}
    (first[2],) = fill_call((2,), taken, (mine[2],))
    first[1], second[1], first[3], second[3], first[0] = fill_call((1, 3, 0), taken, (mine[1], mine[3], mine[0]))
    peers = [lax.ppermute(portion, ("t1", "t0"), [(i, (i + shift) % 4) for i in range(4)]) for shift in (2, 1, 3)]
    for k in (2, 1, 3):
        first[k] = send_same(first[k], k)
    whole = ((portion + peers[0]) + (peers[1] + peers[2])).astype(BF)
    sibling = lax.ppermute(whole, "co", [(0, 1), (1, 0)])
    chip_inner = jnp.concatenate([whole, sibling], axis=0)
    inner = [chip_inner, None, None, None]
    for k in (2, 1):
        inner[k] = send_same(chip_inner, k)
    late, first[2] = tie(chip_inner, first[2])
    inner[3] = send_same(late, 3)
    second[1], first[1] = tie(second[1], first[1])
    second[3], first[3] = tie(second[3], first[3])
    for k in PARTED:
        second[k] = send_same(second[k], k)

    labels = segments.reshape(32, 128)
    sums = partial_call(3, labels, [first[k] for k in range(4)], inner)
    arrived = [send_across(sums[k - 1], k) for k in (2, 1, 3)]
    kept = (labels, segments, first_moment_up, second_moment_up, up_row_seeds, down_row_seeds)
    kept, sums = tie(kept, sums)
    labels, segments, first_moment_up, second_moment_up, up_row_seeds, down_row_seeds = kept
    (own,) = partial_call(1, labels, [first[0], second[1], first[2], second[3]], inner)
    own = own.astype(F32)

    bounds = jnp.sum(
        (segments[None, :] < jnp.arange(EXAMPLES + 1, dtype=jnp.int32)[:, None]).astype(jnp.int32), axis=1
    )

    seeds = jnp.concatenate([up_row_seeds[0], jnp.full((HELD - UP_ROWS,), -1, jnp.int32), down_row_seeds[0]])
    select = (jnp.arange(BANK, dtype=jnp.int32)[:, None] == seeds[None, :]).astype(BF)
    blocks = pl.pallas_call(
        feature_kernel,
        out_shape=jax.ShapeDtypeStruct((BANK, WIDE), F32),
        in_specs=[VMEM] * 4 + [SMEM] + [VMEM] * 5,
        out_specs=VMEM,
        scratch_shapes=[pltpu.VMEM((ROWS, RANK), F32), pltpu.VMEM((ROWS, RANK), F32)],
        compiler_params=pltpu.CompilerParams(vmem_limit_bytes=24 << 20),
        cost_estimate=pl.CostEstimate(flops=0, bytes_accessed=3 << 20, transcendentals=0),
    )(
        own, *arrived, bounds, select,
        first_moment_up[0], first_moment_down[0], second_moment_up[0], second_moment_down[0],
    )

    summed = blocks + lax.ppermute(blocks, "co", [(0, 1), (1, 0)])
    summed = jnp.sum(spread(summed, False), axis=0)
    arrived = spread(summed.astype(BF), True)
    return pl.pallas_call(
        sketch_kernel,
        out_shape=jax.ShapeDtypeStruct((EXAMPLES, bank.shape[2]), F32),
        in_specs=[VMEM] * 2,
        out_specs=VMEM,
        compiler_params=pltpu.CompilerParams(vmem_limit_bytes=24 << 20),
        cost_estimate=pl.CostEstimate(flops=1 << 22, bytes_accessed=1 << 20, transcendentals=0),
    )(arrived, jnp.transpose(bank, (0, 2, 1)))


def solution(mesh):
    rows = ("ex", "py", "co")
    tp = ("t1", "t0")
    split = Mesh(mesh.devices.reshape(4, 2, 2, 4, 2), ("ex", "t1", "t0", "py", "co"))
    return jax.shard_map(
        on_device,
        mesh=split,
        in_specs=(
            P(rows, tp),
            P(rows, tp),
            P(tp, None),
            P(tp, None),
            P(tp, rows, None),
            P(tp, rows, None),
            P(tp, rows, None),
            P(tp, rows, None),
            P(tp, rows),
            P(tp, rows),
            P(),
            P(None, None, ("ex", "t1", "t0", "py", "co")),
        ),
        out_specs=P(None, ("ex", "t1", "t0", "py", "co")),
        check_vma=False,
    )
```
